128 devices in a mesh: path: 64 (over x, y_lo, z, core), dp: 2 (over y_hi).
Axes of the slice: x: 4, y: 4 (y_hi: 2, y_lo: 2; y = y_hi * 2 + y_lo), z: 4, core: 2. Of those that a mesh axis runs over, the one named last changes fastest.
Arguments:
- activations: bfloat16 [64, 768, 1024], P('path', 'dp'), may hold values from -6 to 6
- cotangent: bfloat16 [64, 768, 1024], P('path', 'dp'), may hold values from -6 to 6
- token_ids: int32 [64, 768], P('path', 'dp'), may hold values from 0 to 31999, as said below
- path_table: int32 [64, 2], replicated, may hold values from 0 to 7
- up_master: float32 [8, 1024, 4096], P(None, 'path', 'dp'), may hold values from -6 to 6
- down_master: float32 [8, 4096, 1024], P(None, 'path', 'dp'), may hold values from -6 to 6
- up_momentum: float32 [8, 1024, 4096], P(None, 'path', 'dp'), may hold values from -3 to 3
- down_momentum: float32 [8, 4096, 1024], P(None, 'path', 'dp'), may hold values from -3 to 3
- up_first: bfloat16 [64, 1024, 4096], P('path', None, 'dp'), may hold values from -0.001953125 to 0.001953125
- up_second: bfloat16 [64, 1024, 4096], P('path', None, 'dp'), may hold values from 3.237801e-10 to 1.169974e-08
- down_first: bfloat16 [64, 4096, 1024], P('path', None, 'dp'), may hold values from -0.001953125 to 0.001953125
- down_second: bfloat16 [64, 4096, 1024], P('path', None, 'dp'), may hold values from 3.237801e-10 to 1.169974e-08
Outputs:
- new_up_master: float32 [8, 1024, 4096], P(None, 'path', 'dp')
- new_down_master: float32 [8, 4096, 1024], P(None, 'path', 'dp')
- new_up_momentum: float32 [8, 1024, 4096], P(None, 'path', 'dp')
- new_down_momentum: float32 [8, 4096, 1024], P(None, 'path', 'dp')
The draws below stay inside these ranges and needn't reach their ends.
Inputs may be any that keep to these rules, and one draw needn't show every extreme that they name: `token_ids`: in each path's row the ids are nonzero up to a length of at least 192 tokens and 0 (padding) after it. path_table[p, l] is the module of level l that path p uses; a module may be used by no path.
All inputs are finite; a program needn't handle non-finite values.
Results may differ from the reference program's by a relative error of at most 0.0075.
Values may be sent and summed in bfloat16 or wider, within the bound.
A program may use at most 192 MiB of HBM per device.

```python
import math
import jax
import jax.numpy as jnp
import numpy as np
from jax import lax

D = 1024
F = 4096
C = 8
VOCAB = 32000
TOK_DEV = 384
TOKENS = 768
PATHS = 64
N_DP = 2


def draw_token_ids(key, part):
    key = jax.random.fold_in(key, 11)
    length_key, value_key = jax.random.split(key)
    lengths = jax.random.randint(length_key, (PATHS, 1), TOKENS // 4, TOKENS + 1)
    lengths = lengths.at[0, 0].set(TOKENS // 4)
    values = jax.random.randint(value_key, (PATHS, TOKENS), 1, VOCAB)
    values = values.at[0, 0].set(VOCAB - 1)
    positions = jnp.arange(TOKENS)[None, :]
    return jnp.where(positions < lengths, values, 0).astype(jnp.int32)


def plant(array, rng, smallest, high):
    dims = array.shape
    spot = [jax.random.randint(jax.random.fold_in(rng, axis), (), 0, dims[axis]) for axis in range(len(dims))]
    array = array.at[tuple(spot)].set(smallest)
    longest = dims.index(max(dims))
    spot[longest] = (spot[longest] + 1) % dims[longest]
    return array.at[tuple(spot)].set(high)


def block_levels(own_key, shape, cuts, low, top_value):
    gain = 1.0
    for dim, blocks in cuts:
        draws = jax.random.uniform(jax.random.fold_in(jax.random.fold_in(own_key, 6), dim), (blocks,), jnp.float32, low / len(cuts), top_value / len(cuts))
        gain = gain * jnp.repeat(jnp.exp(draws), shape[dim] // blocks).reshape((-1,) + (1,) * (len(shape) - 1 - dim))
    return gain


def rank_table(number_of, skew):
    portions = [(1 << 20) // math.isqrt(rank ** skew) + 1 for rank in range(1, number_of + 1)]
    spread = 1 + sum(portions) // (1 << 30)
    return np.cumsum(np.array([max(1, weight // spread) for weight in portions]))


def ranked(key, extent, number_of, slope):
    listing = rank_table(number_of, slope)
    lot = jax.random.randint(jax.random.fold_in(key, 1), extent, 0, int(listing[number_of - 1]))
    standing = jnp.searchsorted(jnp.asarray(listing, jnp.int32), lot, side="right")
    return jax.random.permutation(jax.random.fold_in(key, 2), number_of)[standing].astype(jnp.int32)


def noise(key, extent, width, bound, cuts=(), kind=jnp.bfloat16):
    level = block_levels(key, extent, cuts, -0.22, 0.18) if cuts else 1.0
    values = jax.random.normal(key, extent, jnp.float32) * width * level
    return jnp.minimum(jnp.maximum(values, -bound), bound).astype(kind)


def setup_inputs(seed: int = 0) -> dict:
    arg_keys = jax.random.split(jax.random.key(seed), 13)
    activations = noise(arg_keys[0], (PATHS, TOKENS, D), 1.0, 6.0, ((0, 64), (1, 2)))
    cotangent = noise(arg_keys[1], (PATHS, TOKENS, D), 1.0, 6.0, ((0, 64), (1, 2)))
    token_ids = draw_token_ids(jax.random.fold_in(arg_keys[12], 71), 0)
    path_table = plant(ranked(arg_keys[3], (PATHS, 2), C, 2), jax.random.fold_in(arg_keys[3], 3), 0, C - 1).astype(jnp.int32)
    up_master = noise(arg_keys[4], (C, D, F), 1.0, 6.0, ((1, 64), (2, 2)), jnp.float32)
    down_master = noise(arg_keys[5], (C, F, D), 1.0, 6.0, ((1, 64), (2, 2)), jnp.float32)
    up_momentum = noise(arg_keys[6], (C, D, F), 0.2, 3.0, ((1, 64), (2, 2)), jnp.float32)
    down_momentum = noise(arg_keys[7], (C, F, D), 0.2, 3.0, ((1, 64), (2, 2)), jnp.float32)
    up_first = noise(arg_keys[8], (PATHS, D, F), (TOKENS * 10000) ** -0.5, 0.001953125, ((0, 64), (2, 2)))
    up_second = jnp.clip(jnp.exp(math.log(1.1699739843606949e-08) - 3.58725726 * jax.random.uniform(arg_keys[9], (PATHS, D, F), jnp.float32) ** block_levels(arg_keys[9], (PATHS, D, F), ((0, 64), (2, 2)), -0.2, 0.2)), 3.2378011383116245e-10, 1.1699739843606949e-08).astype(jnp.bfloat16)
    down_first = noise(arg_keys[10], (PATHS, F, D), (TOKENS * 10000) ** -0.5, 0.001953125, ((0, 64), (2, 2)))
    down_second = jnp.clip(jnp.exp(math.log(1.1699739843606949e-08) - 3.58725726 * jax.random.uniform(arg_keys[11], (PATHS, F, D), jnp.float32) ** block_levels(arg_keys[11], (PATHS, F, D), ((0, 64), (2, 2)), -0.2, 0.2)), 3.2378011383116245e-10, 1.1699739843606949e-08).astype(jnp.bfloat16)
    return {"activations": activations, "cotangent": cotangent, "token_ids": token_ids, "path_table": path_table, "up_master": up_master, "down_master": down_master, "up_momentum": up_momentum, "down_momentum": down_momentum, "up_first": up_first, "up_second": up_second, "down_first": down_first, "down_second": down_second}


def inner_update(weights, gradient, first_moment, second_moment):
    first_new = 0.9 * first_moment.astype(jnp.float32) + 0.1 * gradient
    second_new = 0.95 * second_moment.astype(jnp.float32) + 0.05 * gradient * gradient
    direction = first_new / (jnp.sqrt(second_new) + 1e-08) + 0.1 * weights.astype(jnp.float32)
    return (0.1 * direction).astype(jnp.bfloat16)

def rounded_sum(terms):
    rounded = lax.optimization_barrier(terms.astype(jnp.bfloat16))
    return lax.optimization_barrier(jnp.sum(rounded.astype(jnp.float32), axis=0))

def reference(activations, cotangent, token_ids, path_table, up_master, down_master, up_momentum, down_momentum, up_first, up_second, down_first, down_second):
    up_scale = D ** (-0.5)
    down_scale = F ** (-0.5)

    def path_work(totals, inputs):
        up_total, down_total = totals
        tokens, upstream, token_row, choice_row, up_moment, up_square, down_moment, down_square = inputs
        up_weights = up_master[choice_row[0]].astype(jnp.bfloat16)
        down_weights = down_master[choice_row[1]].astype(jnp.bfloat16)
        live_mask = (token_row != 0).astype(jnp.float32)
        live_count = jnp.sum(live_mask)
        tokens_wide = tokens.astype(jnp.float32)
        mean_square = lax.optimization_barrier(jnp.mean(tokens_wide * tokens_wide, axis=-1, keepdims=True))
        normed = (tokens_wide * lax.rsqrt(mean_square + 1e-06)).astype(jnp.bfloat16)
        pre_act = jnp.dot(normed, up_weights, preferred_element_type=jnp.float32) * up_scale
        gate_sig = jax.nn.sigmoid(pre_act)
        act_out = (pre_act * gate_sig).astype(jnp.bfloat16)
        out_grad = (upstream.astype(jnp.float32) * live_mask[:, None] / live_count).astype(jnp.bfloat16)
        act_grad = jnp.dot(out_grad, down_weights.T, preferred_element_type=jnp.float32) * down_scale
        pre_grad = (act_grad * gate_sig * (1.0 + pre_act * (1.0 - gate_sig))).astype(jnp.bfloat16)
        normed_blocks = normed.reshape(N_DP, TOK_DEV, D).astype(jnp.float32)
        pre_blocks = pre_grad.reshape(N_DP, TOK_DEV, F).astype(jnp.float32)
        act_blocks = act_out.reshape(N_DP, TOK_DEV, F).astype(jnp.float32)
        out_blocks = out_grad.reshape(N_DP, TOK_DEV, D).astype(jnp.float32)
        up_grad = rounded_sum(up_scale * jnp.einsum('ntd,ntf->ndf', normed_blocks, pre_blocks))
        down_grad = rounded_sum(down_scale * jnp.einsum('ntf,ntd->nfd', act_blocks, out_blocks))
        up_delta = inner_update(up_weights, up_grad, up_moment, up_square)
        down_delta = inner_update(down_weights, down_grad, down_moment, down_square)
        up_total = up_total.at[choice_row[0]].add(up_delta.astype(jnp.float32))
        down_total = down_total.at[choice_row[1]].add(down_delta.astype(jnp.float32))
        return ((up_total, down_total), None)
    start = (jnp.zeros((C, D, F), jnp.float32), jnp.zeros((C, F, D), jnp.float32))
    (up_total, down_total), _ = lax.scan(path_work, start, (activations, cotangent, token_ids, path_table, up_first, up_second, down_first, down_second))
    levels = jnp.arange(C, dtype=jnp.int32)
    up_used = lax.optimization_barrier(jnp.sum((path_table[:, 0][None, :] == levels[:, None]).astype(jnp.float32), axis=1))
    down_used = lax.optimization_barrier(jnp.sum((path_table[:, 1][None, :] == levels[:, None]).astype(jnp.float32), axis=1))
    up_mean = up_total / jnp.maximum(up_used, 1.0)[:, None, None]
    down_mean = down_total / jnp.maximum(down_used, 1.0)[:, None, None]
    new_up_momentum = 0.9 * up_momentum + up_mean
    new_down_momentum = 0.9 * down_momentum + down_mean
    new_up_master = up_master - 0.7 * (up_mean + 0.9 * new_up_momentum)
    new_down_master = down_master - 0.7 * (down_mean + 0.9 * new_down_momentum)
    return (new_up_master, new_down_master, new_up_momentum, new_down_momentum)
```

```python
import jax
import jax.numpy as jnp
from jax import lax
from jax.experimental import pallas as pl
from jax.experimental.pallas import tpu as pltpu
from jax.sharding import PartitionSpec as P

D = 1024
F = 4096
C = 8
TOK = 384
HALF_F = F // 2
HALF_D = D // 2
GROUP = 32
MESH = pl.DeviceIdType.MESH
BF16 = jnp.bfloat16
F32 = jnp.float32
NT = (((1,), (1,)), ((), ()))
TN = (((0,), (0,)), ((), ()))
UP_SCALE = D ** (-0.5)
DOWN_SCALE = F ** (-0.5)


def step_direction(gradient, first_moment, second_moment):
    first_new = 0.9 * first_moment.astype(F32) + 0.1 * gradient
    second_new = 0.95 * second_moment.astype(F32) + 0.05 * gradient * gradient
    return (0.1 * first_new / (jnp.sqrt(second_new) + 1e-08)).astype(BF16)


def kernel(
    table, coef, choice, live, act_in, cot_in, um_in, dm_in, umom_in, dmom_in, up_first, up_second,
    down_first, down_second, um_out, dm_out, umom_out, dmom_out,
    um, dm, umom, dmom, act, cot, upb, upf, dnb, blk, buf_a, buf_b, wup, wdn, rdn, rup,
    gsend, gmine, grecv, nrm, og, count, gp, mom, pdn_send, pdn_recv, pup_send, pup_recv, pick_up, pick_dn,
    in_sem, mom_sem, out_sem, y_send, y_recv, dn_send, blk_recv, wu_send, wu_recv, wd_send, wd_recv,
    g_send, g_recv, dd_send, dd_recv, du_send, du_recv,
):
    path = lax.axis_index("path")
    here = lax.axis_index("dp")
    x = lax.div(path, 16)
    yl = lax.rem(lax.div(path, 8), 2)
    zc = lax.rem(path, 8)
    z = lax.div(zc, 2)
    core = lax.rem(zc, 2)
    group = x * 8 + zc
    other_yl = 1 - yl
    there = 1 - here

    def place(x_, yl_, zc_):
        return x_ * 16 + yl_ * 8 + zc_

    def zc_at(k):
        return lax.rem(z + lax.rem(lax.div(k, 2), 4), 4) * 2 + lax.rem(core + k, 2)

    def peer(k):
        return lax.rem(x + lax.div(k, 8), 4), zc_at(k)

    def remote(src, dst, send, recv, to_path, to_dp):
        return pltpu.make_async_remote_copy(
            src_ref=src, dst_ref=dst, send_sem=send, recv_sem=recv,
            device_id=(to_path, to_dp), device_id_type=MESH,
        )

    def settle(ref, sem):
        pltpu.make_async_copy(ref, ref, sem).wait()

    loads = [
        pltpu.make_async_copy(src, dst, in_sem.at[i])
        for i, (src, dst) in enumerate(
            [(um_in, um), (act_in, act), (dm_in, dm), (cot_in, cot), (umom_in, umom), (dmom_in, dmom)]
        )
    ]
    for load in loads:
        load.start()

    cross = lax.rem(lax.div(x, 2) + here, 2)
    barrier = pltpu.get_barrier_semaphore()

    def greet(k, _):
        x_, zc_ = peer(k)
        pl.semaphore_signal(barrier, inc=1, device_id=(place(x_, yl, zc_), here), device_id_type=MESH)
        return 0

    lax.fori_loop(1, GROUP, greet, 0)
    for to_path, to_dp in (
        (place(x, other_yl, zc), here),
        (path, there),
        (place(3 - x, yl, zc), there),
        (place(3 - x, other_yl, zc), there),
    ):
        pl.semaphore_signal(barrier, inc=1, device_id=(to_path, to_dp), device_id_type=MESH)

    def pick_up_rows(side, source):
        def one(k, _):
            module = table[2 * (lax.div(k, 8) * 16 + yl * 8 + lax.rem(k, 8))]
            buf_a[side * GROUP + k] = source[module]
            return 0

        lax.fori_loop(0, GROUP, one, 0)

    loads[0].wait()
    upb[...] = um[...].astype(BF16)
    pick_up_rows(yl, upb)
    pl.semaphore_wait(barrier, GROUP + 3)

    up_swap = remote(upb, upf, y_send.at[0], y_recv.at[0], place(x, other_yl, zc), here)
    up_swap.start()

    def send_up_rows(side):
        row = place(x, side, zc)
        pltpu.make_async_copy(buf_a.at[side * GROUP + group], wup.at[row], wu_recv).start()

        def one(k, _):
            x_, zc_ = peer(lax.rem(k * 11, GROUP))
            remote(
                buf_a.at[side * GROUP + x_ * 8 + zc_], wup.at[row], wu_send, wu_recv, place(x_, yl, zc_), here
            ).start()
            return 0

        lax.fori_loop(1, GROUP, one, 0)

    send_up_rows(yl)

    own_rows = pl.ds(pl.multiple_of(here * TOK, TOK), TOK)
    loads[1].wait()
    for part in range(3):
        rows = pl.ds(part * 128, 128)
        wide = act[rows, :].astype(F32)
        mean_square = jnp.mean(wide * wide, axis=-1, keepdims=True)
        to_rows = pl.ds(pl.multiple_of(here * TOK + part * 128, 128), 128)
        nrm[to_rows, :] = (wide * lax.rsqrt(mean_square + 1e-06)).astype(BF16)
    nrm_swap = remote(nrm.at[own_rows], nrm.at[own_rows], y_send.at[1], y_recv.at[1], path, there)
    nrm_swap.start()

    loads[2].wait()
    dnb[...] = dm[...].astype(BF16)
    x_to = x + cross * (3 - 2 * x)
    dp_to = here + cross * (1 - 2 * here)
    dn_far = remote(dnb, blk.at[yl], dn_send.at[0], blk_recv, place(x_to, other_yl, zc), dp_to)
    dn_far.start()
    dn_near = remote(dnb, blk.at[yl], dn_send.at[1], blk_recv, place(3 - x, yl, zc), there)

    @pl.when(cross == 1)
    def _():
        dn_near.start()

    @pl.when(cross == 0)
    def _():
        pltpu.make_async_copy(dnb, blk.at[yl], blk_recv).start()

    loads[3].wait()
    for part in range(3):
        rows = pl.ds(part * 128, 128)
        to_rows = pl.ds(pl.multiple_of(here * TOK + part * 128, 128), 128)
        og[to_rows, :] = (cot[rows, :].astype(F32) * live[rows, :]).astype(BF16)
    count[0] = jnp.broadcast_to(jnp.sum(live[...]), (8, 128))
    og_swap = remote(og.at[own_rows], og.at[own_rows], y_send.at[2], y_recv.at[2], path, there)
    og_swap.start()
    count_swap = remote(count.at[0], count.at[1], y_send.at[3], y_recv.at[3], path, there)
    count_swap.start()

    up_swap.wait()
    pick_up_rows(other_yl, upf)
    send_up_rows(other_yl)

    settle(blk, blk_recv)

    def pick_down_rows(k, _):
        module = table[2 * (lax.div(k, 8) * 16 + yl * 8 + lax.rem(k, 8)) + 1]
        buf_b[k] = blk[0, module]
        buf_b[GROUP + k] = blk[1, module]
        return 0

    lax.fori_loop(0, GROUP, pick_down_rows, 0)

    nrm_swap.wait()
    og_swap.wait()
    count_swap.wait()
    per_count = 1.0 / (count[0] + count[1])
    per_count = per_count[0:1, 0:1]

    def scale_rows(i, _):
        rows = pl.ds(pl.multiple_of(i * 64, 64), 64)
        og[rows, :] = (og[rows, :].astype(F32) * per_count).astype(BF16)
        return 0

    lax.fori_loop(0, 12, scale_rows, 0)

    settle(buf_a.at[pl.ds(0, 2 * GROUP - 2)], wu_send)
    from_x = x_to - 2 * here
    for side in range(2):
        row = from_x * 16 + side * 8 + zc
        pltpu.make_async_copy(buf_b.at[side * GROUP + group], wdn.at[dp_to, row], wd_recv).start()

        def one(k, _, side=side, row=row):
            x_, zc_ = peer(lax.rem(k * 11, GROUP))
            remote(
                buf_b.at[side * GROUP + x_ * 8 + zc_], wdn.at[dp_to, row], wd_send, wd_recv,
                place(x_, yl, zc_), here,
            ).start()
            return 0

        lax.fori_loop(1, GROUP, one, 0)

    down_x = [here * 2 + lax.rem(x + i, 2) for i in range(2)] + [there * 2 + lax.rem(x + i, 2) for i in range(2)]
    up_x = [lax.rem(x + i, 4) for i in (2, 1, 3, 0)]

    def fetch(step):
        slot = step % 2
        for kind, (down_source, up_source) in enumerate(((down_first, up_first), (down_second, up_second))):
            if step < 4:
                rows = pl.ds(pl.multiple_of(down_x[step] * 1024, 1024), 1024)
                pltpu.make_async_copy(
                    down_source.at[rows], mom.at[slot, kind], mom_sem.at[slot, kind]
                ).start()
            else:
                rows = pl.ds(pl.multiple_of(up_x[step - 4] * 256, 256), 256)
                for b in range(4):
                    pltpu.make_async_copy(
                        up_source.at[rows, pl.ds(b * 512, 512)],
                        mom.at[slot, kind, pl.ds(b * 256, 256)],
                        mom_sem.at[slot, kind],
                    ).start()

    def await_moments(step):
        slot = step % 2
        for kind in range(2):
            settle(mom.at[slot, kind], mom_sem.at[slot, kind])

    fetch(0)
    fetch(1)

    settle(wup, wu_recv)
    mine_cols = pl.ds(pl.multiple_of(here * HALF_D, HALF_D), HALF_D)
    their_cols = pl.ds(pl.multiple_of(there * HALF_D, HALF_D), HALF_D)

    def g_copy(chunk):
        rows = pl.ds(pl.multiple_of(chunk * 512, 512), 512)
        return remote(gsend.at[rows], grecv.at[rows], g_send.at[chunk], g_recv.at[chunk], path, there)

    def hidden(i, _):
        cols = pl.ds(pl.multiple_of(i * 256, 256), 256)
        weights = wup[:, :, cols].reshape(D, 256)
        pre = jnp.dot(nrm[...], weights, preferred_element_type=F32) * UP_SCALE
        sig = 0.5 * jnp.tanh(0.5 * pre) + 0.5
        out = (pre * sig).astype(BF16)
        gp[:, cols] = (sig * (1.0 + pre * (1.0 - sig))).astype(BF16)
        theirs = lax.dot_general(out, og[:, their_cols], TN, preferred_element_type=F32)
        gsend[cols, :] = (theirs * DOWN_SCALE).astype(BF16)

        @pl.when(lax.rem(i, 2) == 1)
        def _():
            g_copy(lax.div(i, 2)).start()

        mine = lax.dot_general(out, og[:, mine_cols], TN, preferred_element_type=F32)
        gmine[cols, :] = (mine * DOWN_SCALE).astype(BF16)
        return 0

    lax.fori_loop(0, 8, hidden, 0)

    def down_step(step):
        x_ = down_x[step]
        source = gmine if step < 2 else grecv
        first_row = lax.rem(x_, 2) * 1024
        if step >= 2:
            for half in range(2):
                g_copy(lax.rem(x_, 2) * 2 + half).wait_recv()
        await_moments(step)
        slot = step % 2

        def one(q, _):
            rows = pl.ds(pl.multiple_of(q * 64, 64), 64)
            grad = source[pl.ds(pl.multiple_of(first_row + q * 64, 64), 64), :].astype(F32)
            delta = step_direction(grad, mom[slot, 0, rows, :], mom[slot, 1, rows, :])
            for b in range(4):
                buf_a[x_ * 16 + q, :, pl.ds(b * 512, 512)] = delta[b * 16 : b * 16 + 16, :]
            return 0

        lax.fori_loop(0, 16, one, 0)
        fetch(step + 2)

        def send(k, _):
            zc_ = zc_at(lax.rem(k, 8))
            side = lax.rem(other_yl + lax.div(k, 8), 2)
            row = x_ * 16 + side * 8 + zc_
            away = (x_ * 8 + zc_) != group

            @pl.when(away)
            def _():
                remote(
                    buf_a.at[row], rdn.at[side, group], dd_send, dd_recv.at[side], place(x_, yl, zc_), here
                ).start()

            @pl.when(jnp.logical_not(away))
            def _():
                pltpu.make_async_copy(buf_a.at[row], rdn.at[side, group], dd_recv.at[side]).start()

            return 0

        lax.fori_loop(0, 16, send, 0)

    down_step(0)
    down_step(1)

    settle(wdn, wd_recv)

    def hidden_grad(i, _):
        cols = pl.ds(pl.multiple_of(i * 256, 256), 256)
        low = wdn[0, pl.ds(i * 4, 4)].reshape(256, HALF_D)
        high = wdn[1, pl.ds(i * 4, 4)].reshape(256, HALF_D)
        grad = lax.dot_general(og[:, pl.ds(0, HALF_D)], low, NT, preferred_element_type=F32)
        grad += lax.dot_general(og[:, pl.ds(HALF_D, HALF_D)], high, NT, preferred_element_type=F32)
        gp[:, cols] = (grad * DOWN_SCALE * gp[:, cols].astype(F32)).astype(BF16)
        return 0

    lax.fori_loop(0, 8, hidden_grad, 0)
    settle(buf_b.at[pl.ds(0, 2 * GROUP - 2)], wd_send)
    down_step(2)
    down_step(3)

    def send_up_delta(x_, zc_, side):
        row = x_ * 16 + side * 8 + zc_
        away = (x_ * 8 + zc_) != group

        @pl.when(away)
        def _():
            remote(
                buf_b.at[row], rup.at[side, group], du_send, du_recv.at[side], place(x_, yl, zc_), here
            ).start()

        @pl.when(jnp.logical_not(away))
        def _():
            pltpu.make_async_copy(buf_b.at[row], rup.at[side, group], du_recv.at[side]).start()

    def up_step(step):
        x_ = up_x[step - 4]
        await_moments(step)
        slot = step % 2
        lhs = nrm[:, pl.ds(pl.multiple_of(x_ * 256, 256), 256)]

        def one(b, _):
            cols = pl.ds(pl.multiple_of(b * 512, 512), 512)
            rows = pl.ds(pl.multiple_of(b * 256, 256), 256)
            grad = lax.dot_general(lhs, gp[:, cols], TN, preferred_element_type=F32) * UP_SCALE
            delta = step_direction(grad, mom[slot, 0, rows, :], mom[slot, 1, rows, :])
            buf_b[pl.ds(x_ * 16, 16), pl.ds(pl.multiple_of(b * 16, 16), 16), :] = delta.reshape(16, 16, 512)
            return 0

        lax.fori_loop(0, 4, one, 0)
        if step + 2 < 8:
            fetch(step + 2)

        def send(k, _):
            send_up_delta(x_, zc_at(k), other_yl)
            return 0

        lax.fori_loop(0, 8, send, 0)

    for step in range(4, 8):
        up_step(step)

    def send_rest(k, _):
        x_, zc_ = peer(lax.rem(k * 11, GROUP))
        send_up_delta(x_, zc_, yl)
        return 0

    lax.fori_loop(0, GROUP, send_rest, 0)

    module_row = lax.broadcasted_iota(jnp.int32, (C * 16, GROUP * 16), 0)
    path_row = lax.broadcasted_iota(jnp.int32, (C * 16, GROUP * 16), 1)
    same_row = (module_row & 15) == (path_row & 15)
    module = module_row >> 4
    pick_up[...] = jnp.where(same_row & (module == choice[0:1, :]), 1.0, 0.0).astype(BF16)
    pick_dn[...] = jnp.where(same_row & (module == choice[1:2, :]), 1.0, 0.0).astype(BF16)

    def down_sum(side, b):
        block = rdn[side, :, :, pl.ds(b * 512, 512)].reshape(GROUP * 16, 512)
        return jnp.dot(pick_dn[...], block, preferred_element_type=F32).reshape(C, 16, 512)

    def up_sum(side, b):
        block = rup[side, :, pl.ds(b * 16, 16), :].reshape(GROUP * 16, 512)
        return jnp.dot(pick_up[...], block, preferred_element_type=F32).reshape(C, 16, 512)

    def finish(total, master, momentum, level, rows, cols):
        for m in range(C):
            weights = master[m, rows, cols]
            mean = total[m] * coef[level * 16 + m] + coef[level * 16 + 8 + m] * weights.astype(BF16).astype(F32)
            speed = 0.9 * momentum[m, rows, cols] + mean
            momentum[m, rows, cols] = speed
            master[m, rows, cols] = weights - 0.7 * (mean + 0.9 * speed)

    mate = place(x, other_yl, zc)
    settle(rdn.at[other_yl], dd_recv.at[other_yl])
    for b in range(4):
        pdn_send[:, :, pl.ds(b * 512, 512)] = down_sum(other_yl, b).astype(BF16)
    dn_part = remote(pdn_send, pdn_recv, y_send.at[4], y_recv.at[4], mate, here)
    dn_part.start()
    settle(rdn.at[yl], dd_recv.at[yl])
    for load in loads[4:]:
        load.wait()
    dn_part.wait()
    for b in range(4):
        cols = pl.ds(b * 512, 512)
        total = down_sum(yl, b) + pdn_recv[:, :, cols].astype(F32)
        finish(total, dm, dmom, 1, pl.ds(b * 16, 16), pl.ds(0, 512))
    stores = [
        pltpu.make_async_copy(src, dst, out_sem.at[i])
        for i, (src, dst) in enumerate([(dm, dm_out), (dmom, dmom_out), (um, um_out), (umom, umom_out)])
    ]
    stores[0].start()
    stores[1].start()

    settle(rup.at[other_yl], du_recv.at[other_yl])
    for b in range(4):
        pup_send[:, pl.ds(b * 16, 16), :] = up_sum(other_yl, b).astype(BF16)
    up_part = remote(pup_send, pup_recv, y_send.at[5], y_recv.at[5], mate, here)
    up_part.start()
    settle(rup.at[yl], du_recv.at[yl])
    up_part.wait()
    for b in range(4):
        rows = pl.ds(b * 16, 16)
        total = up_sum(yl, b) + pup_recv[:, rows, :].astype(F32)
        finish(total, um, umom, 0, pl.ds(0, 16), pl.ds(b * 512, 512))
    stores[2].start()
    stores[3].start()

    dn_far.wait_send()

    @pl.when(cross == 1)
    def _():
        dn_near.wait_send()

    for chunk in range(4):
        g_copy(chunk).wait_send()
    settle(buf_a.at[pl.ds(0, 2 * GROUP - 2)], dd_send)
    settle(buf_b.at[pl.ds(0, 2 * GROUP - 2)], du_send)
    for store in stores:
        store.wait()


def shards(
    activations,
    cotangent,
    token_ids,
    path_table,
    up_master,
    down_master,
    up_momentum,
    down_momentum,
    up_first,
    up_second,
    down_first,
    down_second,
):
    yl = (lax.axis_index("path") // 8) % 2
    live = (token_ids[0] != 0).astype(F32)[:, None]
    plane = lax.dynamic_index_in_dim(path_table.reshape(4, 2, 8, 2), yl, 1, keepdims=False)
    choice = jnp.repeat(plane.reshape(GROUP, 2).T, 16, axis=1)
    used = jnp.sum((path_table.T[:, None, :] == jnp.arange(C, dtype=jnp.int32)[None, :, None]).astype(F32), axis=2)
    coef = jnp.stack([1.0 / jnp.maximum(used, 1.0), 0.01 * jnp.minimum(used, 1.0)], axis=1).reshape(4 * C)
    anywhere = pl.BlockSpec(memory_space=pl.ANY)
    smem = pl.BlockSpec(memory_space=pltpu.SMEM)
    vmem = pl.BlockSpec(memory_space=pltpu.VMEM)
    dma = pltpu.SemaphoreType.DMA
    result = [jax.ShapeDtypeStruct(array.shape, F32) for array in (up_master, down_master, up_momentum, down_momentum)]
    return tuple(pl.pallas_call(
        kernel,
        out_shape=result,
        in_specs=[smem, smem, vmem, vmem] + [anywhere] * 10,
        out_specs=[anywhere] * 4,
        scratch_shapes=[
            pltpu.VMEM((C, 16, HALF_F), F32),
            pltpu.VMEM((C, 64, HALF_D), F32),
            pltpu.VMEM((C, 16, HALF_F), F32),
            pltpu.VMEM((C, 64, HALF_D), F32),
            pltpu.VMEM((TOK, D), BF16),
            pltpu.VMEM((TOK, D), BF16),
            pltpu.VMEM((C, 16, HALF_F), BF16),
            pltpu.VMEM((C, 16, HALF_F), BF16),
            pltpu.VMEM((C, 64, HALF_D), BF16),
            pltpu.VMEM((2, C, 64, HALF_D), BF16),
            pltpu.VMEM((2 * GROUP, 16, HALF_F), BF16),
            pltpu.VMEM((2 * GROUP, 64, HALF_D), BF16),
            pltpu.VMEM((2 * GROUP, 16, HALF_F), BF16),
            pltpu.VMEM((2, GROUP, 64, HALF_D), BF16),
            pltpu.VMEM((2, GROUP, 16, HALF_F), BF16),
            pltpu.VMEM((2, GROUP, 64, HALF_D), BF16),
            pltpu.VMEM((HALF_F, HALF_D), BF16),
            pltpu.VMEM((HALF_F, HALF_D), BF16),
            pltpu.VMEM((HALF_F, HALF_D), BF16),
            pltpu.VMEM((2 * TOK, D), BF16),
            pltpu.VMEM((2 * TOK, D), BF16),
            pltpu.VMEM((2, 8, 128), F32),
            pltpu.VMEM((2 * TOK, HALF_F), BF16),
            pltpu.VMEM((2, 2, 1024, 512), BF16),
            pltpu.VMEM((C, 16, HALF_F), BF16),
            pltpu.VMEM((C, 16, HALF_F), BF16),
            pltpu.VMEM((C, 64, HALF_D), BF16),
            pltpu.VMEM((C, 64, HALF_D), BF16),
            pltpu.VMEM((C * 16, GROUP * 16), BF16),
            pltpu.VMEM((C * 16, GROUP * 16), BF16),
            dma((6,)),
            dma((2, 2)),
            dma((4,)),
            dma((6,)),
            dma((6,)),
            dma((2,)),
            dma,
            dma,
            dma,
            dma,
            dma,
            dma((4,)),
            dma((4,)),
            dma,
            dma((2,)),
            dma,
            dma((2,)),
        ],
        compiler_params=pltpu.CompilerParams(
            collective_id=0, has_side_effects=True, vmem_limit_bytes=62 * 1024 * 1024
        ),
        cost_estimate=pl.CostEstimate(flops=12_884_901_888, bytes_accessed=30_000_000, transcendentals=1_572_864),
    )(
        path_table.reshape(-1),
        coef,
        choice,
        live,
        activations[0],
        cotangent[0],
        up_master,
        down_master,
        up_momentum,
        down_momentum,
        up_first[0],
        up_second[0],
        down_first[0],
        down_second[0],
    ))


def solution(mesh):
    placed = (
        P("path", "dp", None),
        P("path", "dp", None),
        P("path", "dp"),
        P(),
        P(None, "path", "dp"),
        P(None, "path", "dp"),
        P(None, "path", "dp"),
        P(None, "path", "dp"),
        P("path", None, "dp"),
        P("path", None, "dp"),
        P("path", None, "dp"),
        P("path", None, "dp"),
    )
    return jax.shard_map(
        shards,
        mesh=mesh,
        in_specs=placed,
        out_specs=(
            P(None, "path", "dp"),
            P(None, "path", "dp"),
            P(None, "path", "dp"),
            P(None, "path", "dp"),
        ),
        check_vma=False,
    )
```

```python
import jax
import jax.numpy as jnp
from jax import lax
from jax.experimental import pallas as pl
from jax.experimental.pallas import tpu as pltpu
from jax.sharding import PartitionSpec as P

D = 1024
F = 4096
C = 8
TOK = 384
HALF_F = F // 2
HALF_D = D // 2
GROUP = 32
MESH = pl.DeviceIdType.MESH
BF16 = jnp.bfloat16
F32 = jnp.float32
NT = (((1,), (1,)), ((), ()))
TN = (((0,), (0,)), ((), ()))
UP_SCALE = D ** (-0.5)
DOWN_SCALE = F ** (-0.5)


def step_direction(gradient, first_moment, second_moment):
    first_new = 0.9 * first_moment.astype(F32) + 0.1 * gradient
    second_new = 0.95 * second_moment.astype(F32) + 0.05 * gradient * gradient
    below = second_new * lax.rsqrt(second_new) + 1e-08
    over = pl.reciprocal(below, approx=True)
    over = over * (2.0 - below * over)
    return (0.1 * first_new * over).astype(BF16)


def kernel(
    table, ids, act_in, cot_in, um_in, dm_in, up_first, up_second, down_first, down_second, um_out, dm_out,
    um, dm, act, cot, upb, upf, dnb, blk, buf_a, buf_b, wup, wdn, rdn, rup,
    gsend, gmine, grecv, nrm, nrm_t, og, og_pass, count, used, gp, wide_a, act_a, wide_b, mom,
    pdn_send, pdn_recv, pup_send, pup_recv, pick_t, pick_up, pick_dn,
    in_sem, mom_sem, out_sem, y_send, y_recv, dn_send, blk_recv, wu_send, wu_recv, wd_send, wd_recv,
    g_send, g_recv, dd_send, dd_recv, du_send, du_recv,
):
    path = lax.axis_index("path")
    here = lax.axis_index("dp")
    x = lax.div(path, 16)
    yl = lax.rem(lax.div(path, 8), 2)
    zc = lax.rem(path, 8)
    z = lax.div(zc, 2)
    core = lax.rem(zc, 2)
    group = x * 8 + zc
    other_yl = 1 - yl
    there = 1 - here

    def place(x_, yl_, zc_):
        return x_ * 16 + yl_ * 8 + zc_

    def zc_at(k):
        return lax.rem(z + lax.rem(lax.div(k, 2), 4), 4) * 2 + lax.rem(core + k, 2)

    def peer(k):
        return lax.rem(x + lax.div(k, 8), 4), zc_at(k)

    def remote(src, dst, send, recv, to_path, to_dp):
        return pltpu.make_async_remote_copy(
            src_ref=src, dst_ref=dst, send_sem=send, recv_sem=recv,
            device_id=(to_path, to_dp), device_id_type=MESH,
        )

    def settle(ref, sem):
        pltpu.make_async_copy(ref, ref, sem).wait()

    loads = [
        pltpu.make_async_copy(src, dst, in_sem.at[i])
        for i, (src, dst) in enumerate(
            [(um_in, um), (act_in, act), (dm_in, dm), (cot_in, cot)]
        )
    ]
    for load in loads:
        load.start()

    cross = lax.rem(lax.div(x, 2) + here, 2)
    barrier = pltpu.get_barrier_semaphore()

    def greet(k, _):
        x_, zc_ = peer(k)
        pl.semaphore_signal(barrier, inc=1, device_id=(place(x_, yl, zc_), here), device_id_type=MESH)
        return 0

    lax.fori_loop(1, GROUP, greet, 0)
    for to_path, to_dp in (
        (place(x, other_yl, zc), here),
        (place(x, other_yl, zc), there),
        (path, there),
        (place(3 - x, yl, zc), there),
        (place(3 - x, other_yl, zc), there),
    ):
        pl.semaphore_signal(barrier, inc=1, device_id=(to_path, to_dp), device_id_type=MESH)

    def pick_up_rows(side, source):
        def one(k, _):
            module = table[lax.div(k, 8) * 16 + yl * 8 + lax.rem(k, 8), 0]
            buf_a[side * GROUP + k] = source[module]
            return 0

        lax.fori_loop(0, GROUP, one, 0)

    loads[0].wait()
    upb[...] = um[...].astype(BF16)
    pick_up_rows(yl, upb)
    pl.semaphore_wait(barrier, GROUP + 4)

    up_swap = remote(upb, upf, y_send.at[0], y_recv.at[0], place(x, other_yl, zc), here)
    up_swap.start()

    def send_up_rows(side):
        row = place(x, side, zc)
        pltpu.make_async_copy(buf_a.at[side * GROUP + group], wup.at[row], wu_recv).start()

        def one(k, _):
            x_, zc_ = peer(lax.rem(k * 11, GROUP))
            remote(
                buf_a.at[side * GROUP + x_ * 8 + zc_], wup.at[row], wu_send, wu_recv, place(x_, yl, zc_), here
            ).start()
            return 0

        lax.fori_loop(1, GROUP, one, 0)

    send_up_rows(yl)

    own_rows = pl.ds(pl.multiple_of(here * TOK, TOK), TOK)
    loads[1].wait()
    for part in range(3):
        rows = pl.ds(part * 128, 128)
        wide = act[rows, :].astype(F32)
        mean_square = jnp.mean(wide * wide, axis=-1, keepdims=True)
        to_rows = pl.ds(pl.multiple_of(here * TOK + part * 128, 128), 128)
        nrm[to_rows, :] = (wide * lax.rsqrt(mean_square + 1e-06)).astype(BF16)
    nrm_swap = remote(nrm.at[own_rows], nrm.at[own_rows], y_send.at[1], y_recv.at[1], path, there)
    nrm_swap.start()

    loads[2].wait()
    dnb[...] = dm[...].astype(BF16)
    x_to = x + cross * (3 - 2 * x)
    dp_to = here + cross * (1 - 2 * here)
    dn_far = remote(dnb, blk.at[yl], dn_send.at[0], blk_recv, place(x_to, other_yl, zc), dp_to)
    dn_far.start()
    dn_near = remote(dnb, blk.at[yl], dn_send.at[1], blk_recv, place(3 - x, yl, zc), there)

    @pl.when(cross == 1)
    def _():
        dn_near.start()

    @pl.when(cross == 0)
    def _():
        pltpu.make_async_copy(dnb, blk.at[yl], blk_recv).start()

    loads[3].wait()
    live = jnp.sum((ids[...] != 0).astype(F32))
    for part in range(3):
        rows = pl.ds(part * 128, 128)
        to_rows = pl.ds(pl.multiple_of(here * TOK + part * 128, 128), 128)
        position = (lax.broadcasted_iota(jnp.int32, (128, D), 0) + part * 128).astype(F32)
        og[to_rows, :] = jnp.where(position < live, cot[rows, :].astype(F32), 0.0).astype(BF16)
    count[0] = jnp.broadcast_to(live, (8, 128))
    count_swap = remote(count.at[0], count.at[1], y_send.at[3], y_recv.at[3], path, there)
    count_swap.start()
    dp_below = lax.rem(here + other_yl, 2)
    below = place(x, other_yl, zc)
    og_first = remote(og.at[own_rows], og_pass, y_send.at[2], y_recv.at[2], below, dp_below)
    og_first.start()

    up_swap.wait()
    pick_up_rows(other_yl, upf)
    send_up_rows(other_yl)

    og_first.wait()
    pass_rows = pl.ds(pl.multiple_of((1 - dp_below) * TOK, TOK), TOK)
    og_second = remote(og_pass, og.at[pass_rows], y_send.at[6], y_recv.at[6], below, dp_below)
    og_second.start()

    settle(blk, blk_recv)

    def pick_down_rows(k, _):
        module = table[lax.div(k, 8) * 16 + yl * 8 + lax.rem(k, 8), 1]
        buf_b[k] = blk[0, module]
        buf_b[GROUP + k] = blk[1, module]
        return 0

    lax.fori_loop(0, GROUP, pick_down_rows, 0)

    settle(buf_a.at[pl.ds(0, 2 * GROUP - 2)], wu_send)
    from_x = x_to - 2 * here
    for side in range(2):
        row = from_x * 16 + side * 8 + zc
        pltpu.make_async_copy(buf_b.at[side * GROUP + group], wdn.at[dp_to, row], wd_recv).start()

        def one(k, _, side=side, row=row):
            x_, zc_ = peer(lax.rem(k * 11, GROUP))
            remote(
                buf_b.at[side * GROUP + x_ * 8 + zc_], wdn.at[dp_to, row], wd_send, wd_recv,
                place(x_, yl, zc_), here,
            ).start()
            return 0

        lax.fori_loop(1, GROUP, one, 0)

    nrm_swap.wait()

    def turn(i, _):
        cols = pl.ds(pl.multiple_of(i * 256, 256), 256)
        nrm_t[cols, :] = nrm[:, cols].T
        return 0

    lax.fori_loop(0, 4, turn, 0)
    count_swap.wait()
    per_count = 1.0 / (count[0] + count[1])
    per_count = per_count[0:1, 0:1]
    og_second.wait()

    def scale_rows(i, _):
        rows = pl.ds(pl.multiple_of(i * 64, 64), 64)
        og[rows, :] = (og[rows, :].astype(F32) * per_count).astype(BF16)
        return 0

    lax.fori_loop(0, 12, scale_rows, 0)

    down_x = [here * 2 + lax.rem(x + i, 2) for i in range(2)] + [there * 2 + lax.rem(x + i, 2) for i in range(2)]
    up_x = [lax.rem(x + i, 4) for i in (2, 1, 3, 0)]

    order = (0, 1, 4, 5, 6, 7, 2, 3)

    def fetch(turn_no):
        if turn_no >= 8:
            return
        slot = turn_no % 2
        step = order[turn_no]
        for kind, (down_source, up_source) in enumerate(((down_first, up_first), (down_second, up_second))):
            if step < 4:
                rows = pl.ds(pl.multiple_of(down_x[step] * 1024, 1024), 1024)
                pltpu.make_async_copy(
                    down_source.at[rows], mom.at[slot, kind], mom_sem.at[slot, kind]
                ).start()
            else:
                rows = pl.ds(pl.multiple_of(up_x[step - 4] * 256, 256), 256)
                for b in range(4):
                    pltpu.make_async_copy(
                        up_source.at[rows, pl.ds(b * 512, 512)],
                        mom.at[slot, kind, pl.ds(b * 256, 256)],
                        mom_sem.at[slot, kind],
                    ).start()

    def await_moments(turn_no):
        slot = turn_no % 2
        for kind in range(2):
            settle(mom.at[slot, kind], mom_sem.at[slot, kind])

    fetch(0)
    fetch(1)

    settle(wup, wu_recv)
    mine_cols = pl.ds(pl.multiple_of(here * HALF_D, HALF_D), HALF_D)
    their_cols = pl.ds(pl.multiple_of(there * HALF_D, HALF_D), HALF_D)

    def g_copy(chunk):
        rows = pl.ds(pl.multiple_of(chunk * 512, 512), 512)
        return remote(gsend.at[rows], grecv.at[rows], g_send.at[chunk], g_recv.at[chunk], path, there)

    def pre_act(i, half):
        cols = pl.ds(pl.multiple_of(i * 256, 256), 256)
        weights = wup[:, :, cols].reshape(D, 256)
        wide_a[half] = jnp.dot(nrm[...], weights, preferred_element_type=F32)

    pre_act(0, 0)

    def hidden(pair, _):
        for half in range(2):
            i = pair * 2 + half
            pre_act(jnp.minimum(i + 1, 7), 1 - half)
            cols = pl.ds(pl.multiple_of(i * 256, 256), 256)
            for strip in range(24):
                rows = pl.ds(strip * 32, 32)
                pre = wide_a[half, rows, :] * UP_SCALE
                sig = 0.5 * jnp.tanh(0.5 * pre) + 0.5
                out = pre * sig
                act_a[half, rows, :] = out.astype(BF16)
                gp[rows, cols] = (sig + out * (1.0 - sig)).astype(BF16)
            out_t = act_a[half].T
            theirs = jnp.dot(out_t, og[:, their_cols], preferred_element_type=F32)
            gsend[cols, :] = (theirs * DOWN_SCALE).astype(BF16)
            if half == 1:
                g_copy(pair).start()
            mine = jnp.dot(out_t, og[:, mine_cols], preferred_element_type=F32)
            gmine[cols, :] = (mine * DOWN_SCALE).astype(BF16)
        return 0

    lax.fori_loop(0, 4, hidden, 0)

    def down_delta(turn_no):
        step = order[turn_no]
        x_ = down_x[step]
        source = gmine if step < 2 else grecv
        first_row = lax.rem(x_, 2) * 1024
        if step >= 2:
            for half in range(2):
                g_copy(lax.rem(x_, 2) * 2 + half).wait_recv()
        await_moments(turn_no)
        slot = turn_no % 2

        def one(q, _):
            for b in range(4):
                rows = pl.ds(pl.multiple_of(q * 64 + b * 16, 16), 16)
                grad = source[pl.ds(pl.multiple_of(first_row + q * 64 + b * 16, 16), 16), :].astype(F32)
                delta = step_direction(grad, mom[slot, 0, rows, :], mom[slot, 1, rows, :])
                buf_a[x_ * 16 + q, :, pl.ds(b * 512, 512)] = delta
            return 0

        lax.fori_loop(0, 16, one, 0)
        fetch(turn_no + 2)

    def send_down_delta(step, side):
        x_ = down_x[step]

        def send(k, _):
            zc_ = zc_at(k)
            row = x_ * 16 + side * 8 + zc_
            away = (x_ * 8 + zc_) != group

            @pl.when(away)
            def _():
                remote(
                    buf_a.at[row], rdn.at[side, group], dd_send, dd_recv.at[side], place(x_, yl, zc_), here
                ).start()

            @pl.when(jnp.logical_not(away))
            def _():
                pltpu.make_async_copy(buf_a.at[row], rdn.at[side, group], dd_recv.at[side]).start()

            return 0

        lax.fori_loop(0, 8, send, 0)

    for turn_no in range(2):
        down_delta(turn_no)
        send_down_delta(turn_no, other_yl)
        send_down_delta(turn_no, yl)

    settle(wdn, wd_recv)

    def hidden_grad(i, _):
        cols = pl.ds(pl.multiple_of(i * 256, 256), 256)
        low = wdn[0, pl.ds(i * 4, 4)].reshape(256, HALF_D)
        high = wdn[1, pl.ds(i * 4, 4)].reshape(256, HALF_D)
        grad = lax.dot_general(og[:, pl.ds(0, HALF_D)], low, NT, preferred_element_type=F32)
        grad += lax.dot_general(og[:, pl.ds(HALF_D, HALF_D)], high, NT, preferred_element_type=F32)
        gp[:, cols] = (grad * DOWN_SCALE * gp[:, cols].astype(F32)).astype(BF16)
        return 0

    lax.fori_loop(0, 8, hidden_grad, 0)
    settle(buf_b.at[pl.ds(0, 2 * GROUP - 2)], wd_send)

    def send_up_delta(x_, zc_, side):
        row = x_ * 16 + side * 8 + zc_
        away = (x_ * 8 + zc_) != group

        @pl.when(away)
        def _():
            remote(
                buf_b.at[row], rup.at[side, group], du_send, du_recv.at[side], place(x_, yl, zc_), here
            ).start()

        @pl.when(jnp.logical_not(away))
        def _():
            pltpu.make_async_copy(buf_b.at[row], rup.at[side, group], du_recv.at[side]).start()

    def up_step(turn_no):
        x_ = up_x[order[turn_no] - 4]
        slot = turn_no % 2
        lhs = nrm_t[pl.ds(pl.multiple_of(x_ * 256, 256), 256), :]

        def up_grad(b):
            wide_b[b % 2] = jnp.dot(lhs, gp[:, pl.ds(b * 512, 512)], preferred_element_type=F32)

        up_grad(0)
        await_moments(turn_no)
        for b in range(4):
            if b < 3:
                up_grad(b + 1)
            for i in range(16):
                rows = pl.ds(b * 256 + i * 16, 16)
                grad = wide_b[b % 2, pl.ds(i * 16, 16), :] * UP_SCALE
                delta = step_direction(grad, mom[slot, 0, rows, :], mom[slot, 1, rows, :])
                buf_b[x_ * 16 + i, pl.ds(b * 16, 16), :] = delta
        fetch(turn_no + 2)

        def send(k, _):
            send_up_delta(x_, zc_at(k), other_yl)
            return 0

        lax.fori_loop(0, 8, send, 0)

    for turn_no in range(2, 6):
        up_step(turn_no)

    def send_rest(k, _):
        x_, zc_ = peer(lax.rem(k * 11, GROUP))
        send_up_delta(x_, zc_, yl)
        return 0

    lax.fori_loop(0, GROUP, send_rest, 0)

    for turn_no in range(6, 8):
        down_delta(turn_no)
        send_down_delta(order[turn_no], other_yl)
    for turn_no in range(6, 8):
        send_down_delta(order[turn_no], yl)

    lane = lax.broadcasted_iota(jnp.int32, (16, C * 16), 1)
    same_row = (lane & 15) == lax.broadcasted_iota(jnp.int32, (16, C * 16), 0)
    for level, pick in enumerate((pick_up, pick_dn)):

        def fill(k, _, level=level):
            module = table[lax.div(k, 8) * 16 + yl * 8 + lax.rem(k, 8), level]
            rows = pl.ds(pl.multiple_of(k * 16, 16), 16)
            pick_t[rows, :] = jnp.where(same_row & ((lane >> 4) == module), 1.0, 0.0)
            return 0

        lax.fori_loop(0, GROUP, fill, 0)
        pick[...] = pick_t[...].T.astype(BF16)

        def tally(k, counts, level=level):
            module = table[k, level]
            return tuple(n + jnp.where(module == m, 1, 0) for m, n in enumerate(counts))

        counts = lax.fori_loop(0, 64, tally, (jnp.int32(0),) * C)
        for m in range(C):
            used[level * C + m] = counts[m]

    def down_sum(side, b):
        block = rdn[side, :, :, pl.ds(b * 512, 512)].reshape(GROUP * 16, 512)
        return jnp.dot(pick_dn[...], block, preferred_element_type=F32).reshape(C, 16, 512)

    def up_sum(side, b):
        block = rup[side, :, pl.ds(b * 16, 16), :].reshape(GROUP * 16, 512)
        return jnp.dot(pick_up[...], block, preferred_element_type=F32).reshape(C, 16, 512)

    def finish(total, master, level, rows, cols):
        for m in range(C):
            number = jnp.broadcast_to(used[level * C + m].astype(F32), (8, 128))
            per_used = (1.0 / jnp.maximum(number, 1.0))[0:1, 0:1]
            decay = (0.01 * jnp.minimum(number, 1.0))[0:1, 0:1]
            weights = master[m, rows, cols].astype(BF16).astype(F32)
            master[m, rows, cols] = total[m] * per_used + decay * weights

    mate = place(x, other_yl, zc)
    stores = [
        pltpu.make_async_copy(src, dst, out_sem.at[i]) for i, (src, dst) in enumerate([(dm, dm_out), (um, um_out)])
    ]
    settle(rup.at[other_yl], du_recv.at[other_yl])
    for b in range(4):
        pup_send[:, pl.ds(b * 16, 16), :] = up_sum(other_yl, b).astype(BF16)
    up_part = remote(pup_send, pup_recv, y_send.at[5], y_recv.at[5], mate, here)
    up_part.start()
    settle(rup.at[yl], du_recv.at[yl])
    up_part.wait()
    for b in range(4):
        rows = pl.ds(b * 16, 16)
        total = up_sum(yl, b) + pup_recv[:, rows, :].astype(F32)
        finish(total, um, 0, pl.ds(0, 16), pl.ds(b * 512, 512))
    stores[1].start()

    settle(rdn.at[other_yl], dd_recv.at[other_yl])
    for b in range(4):
        pdn_send[:, :, pl.ds(b * 512, 512)] = down_sum(other_yl, b).astype(BF16)
    dn_part = remote(pdn_send, pdn_recv, y_send.at[4], y_recv.at[4], mate, here)
    dn_part.start()
    settle(rdn.at[yl], dd_recv.at[yl])
    dn_part.wait()
    for b in range(4):
        cols = pl.ds(b * 512, 512)
        total = down_sum(yl, b) + pdn_recv[:, :, cols].astype(F32)
        finish(total, dm, 1, pl.ds(b * 16, 16), pl.ds(0, 512))
    stores[0].start()

    dn_far.wait_send()

    @pl.when(cross == 1)
    def _():
        dn_near.wait_send()

    for chunk in range(4):
        g_copy(chunk).wait_send()
    settle(buf_a.at[pl.ds(0, 2 * GROUP - 2)], dd_send)
    settle(buf_b.at[pl.ds(0, 2 * GROUP - 2)], du_send)
    for store in stores:
        store.wait()


def shards(
    activations,
    cotangent,
    token_ids,
    path_table,
    up_master,
    down_master,
    up_momentum,
    down_momentum,
    up_first,
    up_second,
    down_first,
    down_second,
):
    anywhere = pl.BlockSpec(memory_space=pl.ANY)
    smem = pl.BlockSpec(memory_space=pltpu.SMEM)
    vmem = pl.BlockSpec(memory_space=pltpu.VMEM)
    dma = pltpu.SemaphoreType.DMA
    up_mean, down_mean = pl.pallas_call(
        kernel,
        out_shape=[jax.ShapeDtypeStruct(array.shape, F32) for array in (up_master, down_master)],
        in_specs=[smem, vmem] + [anywhere] * 8,
        out_specs=[anywhere] * 2,
        scratch_shapes=[
            pltpu.VMEM((C, 16, HALF_F), F32),
            pltpu.VMEM((C, 64, HALF_D), F32),
            pltpu.VMEM((TOK, D), BF16),
            pltpu.VMEM((TOK, D), BF16),
            pltpu.VMEM((C, 16, HALF_F), BF16),
            pltpu.VMEM((C, 16, HALF_F), BF16),
            pltpu.VMEM((C, 64, HALF_D), BF16),
            pltpu.VMEM((2, C, 64, HALF_D), BF16),
            pltpu.VMEM((2 * GROUP, 16, HALF_F), BF16),
            pltpu.VMEM((2 * GROUP, 64, HALF_D), BF16),
            pltpu.VMEM((2 * GROUP, 16, HALF_F), BF16),
            pltpu.VMEM((2, GROUP, 64, HALF_D), BF16),
            pltpu.VMEM((2, GROUP, 16, HALF_F), BF16),
            pltpu.VMEM((2, GROUP, 64, HALF_D), BF16),
            pltpu.VMEM((HALF_F, HALF_D), BF16),
            pltpu.VMEM((HALF_F, HALF_D), BF16),
            pltpu.VMEM((HALF_F, HALF_D), BF16),
            pltpu.VMEM((2 * TOK, D), BF16),
            pltpu.VMEM((D, 2 * TOK), BF16),
            pltpu.VMEM((2 * TOK, D), BF16),
            pltpu.VMEM((TOK, D), BF16),
            pltpu.VMEM((2, 8, 128), F32),
            pltpu.SMEM((2 * C,), jnp.int32),
            pltpu.VMEM((2 * TOK, HALF_F), BF16),
            pltpu.VMEM((2, 2 * TOK, 256), F32),
            pltpu.VMEM((2, 2 * TOK, 256), BF16),
            pltpu.VMEM((2, 256, 512), F32),
            pltpu.VMEM((2, 2, 1024, 512), BF16),
            pltpu.VMEM((C, 16, HALF_F), BF16),
            pltpu.VMEM((C, 16, HALF_F), BF16),
            pltpu.VMEM((C, 64, HALF_D), BF16),
            pltpu.VMEM((C, 64, HALF_D), BF16),
            pltpu.VMEM((GROUP * 16, C * 16), F32),
            pltpu.VMEM((C * 16, GROUP * 16), BF16),
            pltpu.VMEM((C * 16, GROUP * 16), BF16),
            dma((4,)),
            dma((2, 2)),
            dma((2,)),
            dma((7,)),
            dma((7,)),
            dma((2,)),
            dma,
            dma,
            dma,
            dma,
            dma,
            dma((4,)),
            dma((4,)),
            dma,
            dma((2,)),
            dma,
            dma((2,)),
        ],
        compiler_params=pltpu.CompilerParams(
            collective_id=0, has_side_effects=True, vmem_limit_bytes=62 * 1024 * 1024
        ),
        cost_estimate=pl.CostEstimate(flops=12_884_901_888, bytes_accessed=30_000_000, transcendentals=1_572_864),
    )(
        path_table,
        token_ids,
        activations[0],
        cotangent[0],
        up_master,
        down_master,
        up_first[0],
        up_second[0],
        down_first[0],
        down_second[0],
    )
    new_up_momentum = 0.9 * up_momentum + up_mean
    new_down_momentum = 0.9 * down_momentum + down_mean
    new_up_master = up_master - 0.7 * (up_mean + 0.9 * new_up_momentum)
    new_down_master = down_master - 0.7 * (down_mean + 0.9 * new_down_momentum)
    return (new_up_master, new_down_master, new_up_momentum, new_down_momentum)


def solution(mesh):
    placed = (
        P("path", "dp", None),
        P("path", "dp", None),
        P("path", "dp"),
        P(),
        P(None, "path", "dp"),
        P(None, "path", "dp"),
        P(None, "path", "dp"),
        P(None, "path", "dp"),
        P("path", None, "dp"),
        P("path", None, "dp"),
        P("path", None, "dp"),
        P("path", None, "dp"),
    )
    return jax.shard_map(
        shards,
        mesh=mesh,
        in_specs=placed,
        out_specs=(
            P(None, "path", "dp"),
            P(None, "path", "dp"),
            P(None, "path", "dp"),
            P(None, "path", "dp"),
        ),
        check_vma=False,
    )
```

```python
import jax
import jax.numpy as jnp
from jax import lax
from jax.experimental import pallas as pl
from jax.experimental.pallas import tpu as pltpu
from jax.sharding import PartitionSpec as P

D = 1024
F = 4096
C = 8
TOK = 384
HALF_F = F // 2
HALF_D = D // 2
GROUP = 32
MESH = pl.DeviceIdType.MESH
BF16 = jnp.bfloat16
F32 = jnp.float32
NT = (((1,), (1,)), ((), ()))
TN = (((0,), (0,)), ((), ()))
UP_SCALE = D ** (-0.5)
DOWN_SCALE = F ** (-0.5)


def step_direction(gradient, first_moment, second_moment):
    first_new = 0.9 * first_moment.astype(F32) + 0.1 * gradient
    second_new = 0.95 * second_moment.astype(F32) + 0.05 * gradient * gradient
    below = second_new * lax.rsqrt(second_new) + 1e-08
    over = pl.reciprocal(below, approx=True)
    over = over * (2.0 - below * over)
    return (0.1 * first_new * over).astype(BF16)


def kernel(
    table, ids, act_in, cot_in, um_in, dm_in, up_first, up_second, down_first, down_second, um_out, dm_out,
    um, dm, act, cot, upb, upf, dnb, blk, buf_a, buf_b, wup, wdn, rdn, rup,
    gsend, gmine, grecv, nrm, nrm_t, og, count, used, gp, wide_a, act_a, wide_b, mom,
    pdn_send, pdn_recv, pup_send, pup_recv, pick_t, pick_up, pick_dn,
    in_sem, mom_sem, out_sem, y_send, y_recv, dn_send, blk_recv, wu_send, wu_recv, wd_send, wd_recv,
    g_send, g_recv, dd_send, dd_recv, du_send, du_recv,
):
    path = lax.axis_index("path")
    here = lax.axis_index("dp")
    x = lax.div(path, 16)
    yl = lax.rem(lax.div(path, 8), 2)
    zc = lax.rem(path, 8)
    z = lax.div(zc, 2)
    core = lax.rem(zc, 2)
    group = x * 8 + zc
    other_yl = 1 - yl
    there = 1 - here

    def place(x_, yl_, zc_):
        return x_ * 16 + yl_ * 8 + zc_

    def zc_at(k):
        return lax.rem(z + lax.rem(lax.div(k, 2), 4), 4) * 2 + lax.rem(core + k, 2)

    def peer(k):
        return lax.rem(x + lax.div(k, 8), 4), zc_at(k)

    def remote(src, dst, send, recv, to_path, to_dp):
        return pltpu.make_async_remote_copy(
            src_ref=src, dst_ref=dst, send_sem=send, recv_sem=recv,
            device_id=(to_path, to_dp), device_id_type=MESH,
        )

    def settle(ref, sem):
        pltpu.make_async_copy(ref, ref, sem).wait()

    loads = [
        pltpu.make_async_copy(src, dst, in_sem.at[i])
        for i, (src, dst) in enumerate(
            [(um_in, um), (act_in, act), (dm_in, dm), (cot_in, cot)]
        )
    ]
    for load in loads:
        load.start()

    cross = lax.rem(lax.div(x, 2) + here, 2)
    barrier = pltpu.get_barrier_semaphore()

    def greet(k, _):
        x_, zc_ = peer(k)
        pl.semaphore_signal(barrier, inc=1, device_id=(place(x_, yl, zc_), here), device_id_type=MESH)
        return 0

    lax.fori_loop(1, GROUP, greet, 0)
    for to_path, to_dp in (
        (place(x, other_yl, zc), here),
        (path, there),
        (place(3 - x, yl, zc), there),
        (place(3 - x, other_yl, zc), there),
    ):
        pl.semaphore_signal(barrier, inc=1, device_id=(to_path, to_dp), device_id_type=MESH)

    def pick_up_rows(side, source):
        def one(k, _):
            module = table[lax.div(k, 8) * 16 + yl * 8 + lax.rem(k, 8), 0]
            buf_a[side * GROUP + k] = source[module]
            return 0

        lax.fori_loop(0, GROUP, one, 0)

    loads[0].wait()
    upb[...] = um[...].astype(BF16)
    pick_up_rows(yl, upb)
    pl.semaphore_wait(barrier, GROUP + 3)

    up_swap = remote(upb, upf, y_send.at[0], y_recv.at[0], place(x, other_yl, zc), here)
    up_swap.start()

    def send_up_rows(side, half):
        row = place(x, side, zc)
        pltpu.make_async_copy(buf_a.at[side * GROUP + group], wup.at[row], wu_recv).start()

        def one(k, _):
            x_, zc_ = peer(lax.rem(k * 11, GROUP))
            remote(
                buf_a.at[side * GROUP + x_ * 8 + zc_], wup.at[row], wu_send.at[half], wu_recv, place(x_, yl, zc_), here
            ).start()
            return 0

        lax.fori_loop(1, GROUP, one, 0)

    send_up_rows(yl, 0)

    own_rows = pl.ds(pl.multiple_of(here * TOK, TOK), TOK)
    loads[1].wait()
    for part in range(3):
        rows = pl.ds(part * 128, 128)
        wide = act[rows, :].astype(F32)
        mean_square = jnp.mean(wide * wide, axis=-1, keepdims=True)
        to_rows = pl.ds(pl.multiple_of(here * TOK + part * 128, 128), 128)
        nrm[to_rows, :] = (wide * lax.rsqrt(mean_square + 1e-06)).astype(BF16)
    nrm_swap = remote(nrm.at[own_rows], nrm.at[own_rows], y_send.at[1], y_recv.at[1], path, there)
    nrm_swap.start()

    loads[2].wait()
    dnb[...] = dm[...].astype(BF16)
    x_to = x + cross * (3 - 2 * x)
    dp_to = here + cross * (1 - 2 * here)
    dn_far = remote(dnb, blk.at[yl], dn_send.at[0], blk_recv, place(x_to, other_yl, zc), dp_to)
    dn_far.start()
    dn_near = remote(dnb, blk.at[yl], dn_send.at[1], blk_recv, place(3 - x, yl, zc), there)

    @pl.when(cross == 1)
    def _():
        dn_near.start()

    @pl.when(cross == 0)
    def _():
        pltpu.make_async_copy(dnb, blk.at[yl], blk_recv).start()

    loads[3].wait()
    live = jnp.sum((ids[...] != 0).astype(F32))
    for part in range(3):
        rows = pl.ds(part * 128, 128)
        to_rows = pl.ds(pl.multiple_of(here * TOK + part * 128, 128), 128)
        position = (lax.broadcasted_iota(jnp.int32, (128, D), 0) + part * 128).astype(F32)
        og[to_rows, :] = jnp.where(position < live, cot[rows, :].astype(F32), 0.0).astype(BF16)
    count[0] = jnp.broadcast_to(live, (8, 128))
    count_swap = remote(count.at[0], count.at[1], y_send.at[3], y_recv.at[3], path, there)
    count_swap.start()
    og_swap = remote(og.at[own_rows], og.at[own_rows], y_send.at[2], y_recv.at[2], path, there)
    og_swap.start()

    up_swap.wait()
    pick_up_rows(other_yl, upf)
    send_up_rows(other_yl, 1)

    settle(blk, blk_recv)

    def pick_down_rows(k, _):
        module = table[lax.div(k, 8) * 16 + yl * 8 + lax.rem(k, 8), 1]
        buf_b[k] = blk[0, module]
        buf_b[GROUP + k] = blk[1, module]
        return 0

    lax.fori_loop(0, GROUP, pick_down_rows, 0)

    settle(buf_a.at[pl.ds(0, GROUP - 1)], wu_send.at[0])
    from_x = x_to - 2 * here
    for side in range(2):
        row = from_x * 16 + side * 8 + zc
        pltpu.make_async_copy(buf_b.at[side * GROUP + group], wdn.at[dp_to, row], wd_recv).start()

        def one(k, _, side=side, row=row):
            x_, zc_ = peer(lax.rem(k * 11, GROUP))
            remote(
                buf_b.at[side * GROUP + x_ * 8 + zc_], wdn.at[dp_to, row], wd_send, wd_recv,
                place(x_, yl, zc_), here,
            ).start()
            return 0

        lax.fori_loop(1, GROUP, one, 0)

    nrm_swap.wait()

    def turn(i, _):
        cols = pl.ds(pl.multiple_of(i * 256, 256), 256)
        nrm_t[cols, :] = nrm[:, cols].T
        return 0

    lax.fori_loop(0, 4, turn, 0)
    count_swap.wait()
    per_count = 1.0 / (count[0] + count[1])
    per_count = per_count[0:1, 0:1]
    og_swap.wait()

    def scale_rows(i, _):
        rows = pl.ds(pl.multiple_of(i * 64, 64), 64)
        og[rows, :] = (og[rows, :].astype(F32) * per_count).astype(BF16)
        return 0

    lax.fori_loop(0, 12, scale_rows, 0)

    down_x = [here * 2 + lax.rem(x + i, 2) for i in range(2)] + [there * 2 + lax.rem(x + i, 2) for i in range(2)]
    up_x = [lax.rem(x + i, 4) for i in (2, 1, 3, 0)]

    order = (0, 1, 2, 3, 4, 5, 6, 7)

    def fetch(turn_no):
        if turn_no >= 8:
            return
        slot = turn_no % 2
        step = order[turn_no]
        for kind, (down_source, up_source) in enumerate(((down_first, up_first), (down_second, up_second))):
            if step < 4:
                rows = pl.ds(pl.multiple_of(down_x[step] * 1024, 1024), 1024)
                pltpu.make_async_copy(
                    down_source.at[rows], mom.at[slot, kind], mom_sem.at[slot, kind]
                ).start()
            else:
                rows = pl.ds(pl.multiple_of(up_x[step - 4] * 256, 256), 256)
                for b in range(4):
                    pltpu.make_async_copy(
                        up_source.at[rows, pl.ds(b * 512, 512)],
                        mom.at[slot, kind, pl.ds(b * 256, 256)],
                        mom_sem.at[slot, kind],
                    ).start()

    def await_moments(turn_no):
        slot = turn_no % 2
        for kind in range(2):
            settle(mom.at[slot, kind], mom_sem.at[slot, kind])

    fetch(0)
    fetch(1)

    settle(wup, wu_recv)
    mine_cols = pl.ds(pl.multiple_of(here * HALF_D, HALF_D), HALF_D)
    their_cols = pl.ds(pl.multiple_of(there * HALF_D, HALF_D), HALF_D)

    def g_copy(chunk):
        rows = pl.ds(pl.multiple_of(chunk * 512, 512), 512)
        return remote(gsend.at[rows], grecv.at[rows], g_send.at[chunk], g_recv.at[chunk], path, there)

    def pre_act(i, half):
        cols = pl.ds(pl.multiple_of(i * 256, 256), 256)
        weights = wup[:, :, cols].reshape(D, 256)
        wide_a[half] = jnp.dot(nrm[...], weights, preferred_element_type=F32)

    first_tile = 4 * lax.rem(x, 2)
    pre_act(first_tile, 0)

    def hidden(pair, _):
        for half in range(2):
            i = lax.rem(first_tile + pair * 2 + half, 8)
            pre_act(lax.rem(i + 1, 8), 1 - half)
            cols = pl.ds(pl.multiple_of(i * 256, 256), 256)
            for strip in range(24):
                rows = pl.ds(strip * 32, 32)
                pre = wide_a[half, rows, :] * UP_SCALE
                sig = 0.5 * jnp.tanh(0.5 * pre) + 0.5
                out = pre * sig
                act_a[half, rows, :] = out.astype(BF16)
                gp[rows, cols] = (sig + out * (1.0 - sig)).astype(BF16)
            out_t = act_a[half].T
            theirs = jnp.dot(out_t, og[:, their_cols], preferred_element_type=F32)
            gsend[cols, :] = (theirs * DOWN_SCALE).astype(BF16)
            if half == 1:
                g_copy(lax.div(i, 2)).start()
            mine = jnp.dot(out_t, og[:, mine_cols], preferred_element_type=F32)
            gmine[cols, :] = (mine * DOWN_SCALE).astype(BF16)
        return 0

    lax.fori_loop(0, 4, hidden, 0)

    def down_delta(turn_no):
        step = order[turn_no]
        x_ = down_x[step]
        source = gmine if step < 2 else grecv
        first_row = lax.rem(x_, 2) * 1024
        if step >= 2:
            for half in range(2):
                g_copy(lax.rem(x_, 2) * 2 + half).wait_recv()
        await_moments(turn_no)
        slot = turn_no % 2

        def one(q, _):
            for b in range(4):
                rows = pl.ds(pl.multiple_of(q * 64 + b * 16, 16), 16)
                grad = source[pl.ds(pl.multiple_of(first_row + q * 64 + b * 16, 16), 16), :].astype(F32)
                delta = step_direction(grad, mom[slot, 0, rows, :], mom[slot, 1, rows, :])
                buf_a[x_ * 16 + q, :, pl.ds(b * 512, 512)] = delta
            return 0

        lax.fori_loop(0, 16, one, 0)
        fetch(turn_no + 2)

    def send_down_delta(step, side):
        x_ = down_x[step]

        def send(k, _):
            zc_ = zc_at(k)
            row = x_ * 16 + side * 8 + zc_
            away = (x_ * 8 + zc_) != group

            @pl.when(away)
            def _():
                remote(
                    buf_a.at[row], rdn.at[side, group], dd_send, dd_recv.at[side], place(x_, yl, zc_), here
                ).start()

            @pl.when(jnp.logical_not(away))
            def _():
                pltpu.make_async_copy(buf_a.at[row], rdn.at[side, group], dd_recv.at[side]).start()

            return 0

        lax.fori_loop(0, 8, send, 0)

    settle(buf_a.at[pl.ds(0, GROUP - 1)], wu_send.at[1])
    for turn_no in range(4):
        down_delta(turn_no)
        send_down_delta(turn_no, other_yl)
        send_down_delta(turn_no, yl)

    settle(wdn, wd_recv)

    def hidden_grad(i, _):
        cols = pl.ds(pl.multiple_of(i * 256, 256), 256)
        low = wdn[0, pl.ds(i * 4, 4)].reshape(256, HALF_D)
        high = wdn[1, pl.ds(i * 4, 4)].reshape(256, HALF_D)
        grad = lax.dot_general(og[:, pl.ds(0, HALF_D)], low, NT, preferred_element_type=F32)
        grad += lax.dot_general(og[:, pl.ds(HALF_D, HALF_D)], high, NT, preferred_element_type=F32)
        gp[:, cols] = (grad * DOWN_SCALE * gp[:, cols].astype(F32)).astype(BF16)
        return 0

    lax.fori_loop(0, 8, hidden_grad, 0)
    settle(buf_b.at[pl.ds(0, 2 * GROUP - 2)], wd_send)

    def send_up_delta(x_, zc_, side):
        row = x_ * 16 + side * 8 + zc_
        away = (x_ * 8 + zc_) != group

        @pl.when(away)
        def _():
            remote(
                buf_b.at[row], rup.at[side, group], du_send, du_recv.at[side], place(x_, yl, zc_), here
            ).start()

        @pl.when(jnp.logical_not(away))
        def _():
            pltpu.make_async_copy(buf_b.at[row], rup.at[side, group], du_recv.at[side]).start()

    def up_step(turn_no):
        x_ = up_x[order[turn_no] - 4]
        slot = turn_no % 2
        lhs = nrm_t[pl.ds(pl.multiple_of(x_ * 256, 256), 256), :]

        def up_grad(b):
            wide_b[b % 2] = jnp.dot(lhs, gp[:, pl.ds(b * 512, 512)], preferred_element_type=F32)

        up_grad(0)
        await_moments(turn_no)
        for b in range(4):
            if b < 3:
                up_grad(b + 1)
            for i in range(16):
                rows = pl.ds(b * 256 + i * 16, 16)
                grad = wide_b[b % 2, pl.ds(i * 16, 16), :] * UP_SCALE
                delta = step_direction(grad, mom[slot, 0, rows, :], mom[slot, 1, rows, :])
                buf_b[x_ * 16 + i, pl.ds(b * 16, 16), :] = delta
        fetch(turn_no + 2)

        def send(k, _):
            send_up_delta(x_, zc_at(k), other_yl)
            return 0

        lax.fori_loop(0, 8, send, 0)

    for turn_no in range(4, 8):
        up_step(turn_no)

    def send_rest(k, _):
        x_, zc_ = peer(lax.rem(k * 11, GROUP))
        send_up_delta(x_, zc_, yl)
        return 0

    lax.fori_loop(0, GROUP, send_rest, 0)

    lane = lax.broadcasted_iota(jnp.int32, (16, C * 16), 1)
    same_row = (lane & 15) == lax.broadcasted_iota(jnp.int32, (16, C * 16), 0)
    for level, pick in enumerate((pick_up, pick_dn)):

        def fill(k, _, level=level):
            module = table[lax.div(k, 8) * 16 + yl * 8 + lax.rem(k, 8), level]
            rows = pl.ds(pl.multiple_of(k * 16, 16), 16)
            pick_t[rows, :] = jnp.where(same_row & ((lane >> 4) == module), 1.0, 0.0)
            return 0

        lax.fori_loop(0, GROUP, fill, 0)
        pick[...] = pick_t[...].T.astype(BF16)

        def tally(k, counts, level=level):
            module = table[k, level]
            return tuple(n + jnp.where(module == m, 1, 0) for m, n in enumerate(counts))

        counts = lax.fori_loop(0, 64, tally, (jnp.int32(0),) * C)
        for m in range(C):
            used[level * C + m] = counts[m]

    def down_sum(side, b):
        block = rdn[side, :, :, pl.ds(b * 512, 512)].reshape(GROUP * 16, 512)
        return jnp.dot(pick_dn[...], block, preferred_element_type=F32).reshape(C, 16, 512)

    def up_sum(side, b):
        block = rup[side, :, pl.ds(b * 16, 16), :].reshape(GROUP * 16, 512)
        return jnp.dot(pick_up[...], block, preferred_element_type=F32).reshape(C, 16, 512)

    def finish(total, master, level, rows, cols):
        for m in range(C):
            number = jnp.broadcast_to(used[level * C + m].astype(F32), (8, 128))
            per_used = (1.0 / jnp.maximum(number, 1.0))[0:1, 0:1]
            decay = (0.01 * jnp.minimum(number, 1.0))[0:1, 0:1]
            weights = master[m, rows, cols].astype(BF16).astype(F32)
            master[m, rows, cols] = total[m] * per_used + decay * weights

    mate = place(x, other_yl, zc)
    stores = [
        pltpu.make_async_copy(src, dst, out_sem.at[i]) for i, (src, dst) in enumerate([(dm, dm_out), (um, um_out)])
    ]
    settle(rdn.at[other_yl], dd_recv.at[other_yl])
    for b in range(4):
        pdn_send[:, :, pl.ds(b * 512, 512)] = down_sum(other_yl, b).astype(BF16)
    dn_part = remote(pdn_send, pdn_recv, y_send.at[4], y_recv.at[4], mate, here)
    dn_part.start()
    settle(rdn.at[yl], dd_recv.at[yl])
    dn_part.wait()
    for b in range(4):
        cols = pl.ds(b * 512, 512)
        total = down_sum(yl, b) + pdn_recv[:, :, cols].astype(F32)
        finish(total, dm, 1, pl.ds(b * 16, 16), pl.ds(0, 512))
    stores[0].start()

    settle(rup.at[other_yl], du_recv.at[other_yl])
    for b in range(4):
        pup_send[:, pl.ds(b * 16, 16), :] = up_sum(other_yl, b).astype(BF16)
    up_part = remote(pup_send, pup_recv, y_send.at[5], y_recv.at[5], mate, here)
    up_part.start()
    settle(rup.at[yl], du_recv.at[yl])
    up_part.wait()
    for b in range(4):
        rows = pl.ds(b * 16, 16)
        total = up_sum(yl, b) + pup_recv[:, rows, :].astype(F32)
        finish(total, um, 0, pl.ds(0, 16), pl.ds(b * 512, 512))
    stores[1].start()

    dn_far.wait_send()

    @pl.when(cross == 1)
    def _():
        dn_near.wait_send()

    for chunk in range(4):
        g_copy(chunk).wait_send()
    settle(buf_a.at[pl.ds(0, 2 * GROUP - 2)], dd_send)
    settle(buf_b.at[pl.ds(0, 2 * GROUP - 2)], du_send)
    for store in stores:
        store.wait()


def shards(
    activations,
    cotangent,
    token_ids,
    path_table,
    up_master,
    down_master,
    up_momentum,
    down_momentum,
    up_first,
    up_second,
    down_first,
    down_second,
):
    anywhere = pl.BlockSpec(memory_space=pl.ANY)
    smem = pl.BlockSpec(memory_space=pltpu.SMEM)
    vmem = pl.BlockSpec(memory_space=pltpu.VMEM)
    dma = pltpu.SemaphoreType.DMA
    up_mean, down_mean = pl.pallas_call(
        kernel,
        out_shape=[jax.ShapeDtypeStruct(array.shape, F32) for array in (up_master, down_master)],
        in_specs=[smem, vmem] + [anywhere] * 8,
        out_specs=[anywhere] * 2,
        scratch_shapes=[
            pltpu.VMEM((C, 16, HALF_F), F32),
            pltpu.VMEM((C, 64, HALF_D), F32),
            pltpu.VMEM((TOK, D), BF16),
            pltpu.VMEM((TOK, D), BF16),
            pltpu.VMEM((C, 16, HALF_F), BF16),
            pltpu.VMEM((C, 16, HALF_F), BF16),
            pltpu.VMEM((C, 64, HALF_D), BF16),
            pltpu.VMEM((2, C, 64, HALF_D), BF16),
            pltpu.VMEM((2 * GROUP, 16, HALF_F), BF16),
            pltpu.VMEM((2 * GROUP, 64, HALF_D), BF16),
            pltpu.VMEM((2 * GROUP, 16, HALF_F), BF16),
            pltpu.VMEM((2, GROUP, 64, HALF_D), BF16),
            pltpu.VMEM((2, GROUP, 16, HALF_F), BF16),
            pltpu.VMEM((2, GROUP, 64, HALF_D), BF16),
            pltpu.VMEM((HALF_F, HALF_D), BF16),
            pltpu.VMEM((HALF_F, HALF_D), BF16),
            pltpu.VMEM((HALF_F, HALF_D), BF16),
            pltpu.VMEM((2 * TOK, D), BF16),
            pltpu.VMEM((D, 2 * TOK), BF16),
            pltpu.VMEM((2 * TOK, D), BF16),
            pltpu.VMEM((2, 8, 128), F32),
            pltpu.SMEM((2 * C,), jnp.int32),
            pltpu.VMEM((2 * TOK, HALF_F), BF16),
            pltpu.VMEM((2, 2 * TOK, 256), F32),
            pltpu.VMEM((2, 2 * TOK, 256), BF16),
            pltpu.VMEM((2, 256, 512), F32),
            pltpu.VMEM((2, 2, 1024, 512), BF16),
            pltpu.VMEM((C, 16, HALF_F), BF16),
            pltpu.VMEM((C, 16, HALF_F), BF16),
            pltpu.VMEM((C, 64, HALF_D), BF16),
            pltpu.VMEM((C, 64, HALF_D), BF16),
            pltpu.VMEM((GROUP * 16, C * 16), F32),
            pltpu.VMEM((C * 16, GROUP * 16), BF16),
            pltpu.VMEM((C * 16, GROUP * 16), BF16),
            dma((4,)),
            dma((2, 2)),
            dma((2,)),
            dma((6,)),
            dma((6,)),
            dma((2,)),
            dma,
            dma((2,)),
            dma,
            dma,
            dma,
            dma((4,)),
            dma((4,)),
            dma,
            dma((2,)),
            dma,
            dma((2,)),
        ],
        compiler_params=pltpu.CompilerParams(
            collective_id=0, has_side_effects=True, vmem_limit_bytes=62 * 1024 * 1024
        ),
        cost_estimate=pl.CostEstimate(flops=12_884_901_888, bytes_accessed=30_000_000, transcendentals=1_572_864),
    )(
        path_table,
        token_ids,
        activations[0],
        cotangent[0],
        up_master,
        down_master,
        up_first[0],
        up_second[0],
        down_first[0],
        down_second[0],
    )
    new_up_momentum = 0.9 * up_momentum + up_mean
    new_down_momentum = 0.9 * down_momentum + down_mean
    new_up_master = up_master - 0.7 * (up_mean + 0.9 * new_up_momentum)
    new_down_master = down_master - 0.7 * (down_mean + 0.9 * new_down_momentum)
    return (new_up_master, new_down_master, new_up_momentum, new_down_momentum)


def solution(mesh):
    placed = (
        P("path", "dp", None),
        P("path", "dp", None),
        P("path", "dp"),
        P(),
        P(None, "path", "dp"),
        P(None, "path", "dp"),
        P(None, "path", "dp"),
        P(None, "path", "dp"),
        P("path", None, "dp"),
        P("path", None, "dp"),
        P("path", None, "dp"),
        P("path", None, "dp"),
    )
    return jax.shard_map(
        shards,
        mesh=mesh,
        in_specs=placed,
        out_specs=(
            P(None, "path", "dp"),
            P(None, "path", "dp"),
            P(None, "path", "dp"),
            P(None, "path", "dp"),
        ),
        check_vma=False,
    )
```

```python
import jax
import jax.numpy as jnp
from jax import lax
from jax.experimental import pallas as pl
from jax.experimental.pallas import tpu as pltpu
from jax.sharding import PartitionSpec as P

D = 1024
F = 4096
C = 8
TOK = 384
HALF_F = F // 2
HALF_D = D // 2
GROUP = 32
MESH = pl.DeviceIdType.MESH
BF16 = jnp.bfloat16
F32 = jnp.float32
NT = (((1,), (1,)), ((), ()))
TN = (((0,), (0,)), ((), ()))
UP_SCALE = D ** (-0.5)
DOWN_SCALE = F ** (-0.5)


def step_direction(gradient, first_moment, second_moment):
    first_new = 0.9 * first_moment.astype(F32) + 0.1 * gradient
    second_new = 0.95 * second_moment.astype(F32) + 0.05 * gradient * gradient
    below = second_new * lax.rsqrt(second_new) + 1e-08
    over = pl.reciprocal(below, approx=True)
    over = over * (2.0 - below * over)
    return (0.1 * first_new * over).astype(BF16)


def kernel(
    table, ids, act_in, cot_in, um_in, dm_in, up_first, up_second, down_first, down_second, um_out, dm_out,
    um, dm, up_x0, up_x1, up_x2, up_x3, up_z0, up_z1, up_z2, up_z3,
    dn_x0, dn_x1, dn_x2, dn_x3, dn_z0, dn_z1, dn_z2, dn_z3, dnb, buf_a, buf_b, wup, wdn, rdn, rup,
    gsend, gmine, grecv, nrm, nrm_t, og, count, used, gp, wide_a, act_a, wide_b, mom,
    pdn_send, pdn_recv, pup_send, pup_recv, pick_t, pick_up, pick_dn,
    in_sem, mom_sem, out_sem, y_send, y_recv, ring_send, ring_recv, dn_send, blk_recv, wu_send, wu_recv, wd_send, wd_recv,
    g_send, g_recv, dd_send, dd_recv, du_send, du_recv,
):
    path = lax.axis_index("path")
    here = lax.axis_index("dp")
    x = lax.div(path, 16)
    yl = lax.rem(lax.div(path, 8), 2)
    zc = lax.rem(path, 8)
    z = lax.div(zc, 2)
    core = lax.rem(zc, 2)
    group = x * 8 + zc
    other_yl = 1 - yl
    there = 1 - here

    def place(x_, yl_, zc_):
        return x_ * 16 + yl_ * 8 + zc_

    def zc_at(k):
        return lax.rem(z + lax.rem(lax.div(k, 2), 4), 4) * 2 + lax.rem(core + k, 2)

    def peer(k):
        return lax.rem(x + lax.div(k, 8), 4), zc_at(k)

    def remote(src, dst, send, recv, to_path, to_dp):
        return pltpu.make_async_remote_copy(
            src_ref=src, dst_ref=dst, send_sem=send, recv_sem=recv,
            device_id=(to_path, to_dp), device_id_type=MESH,
        )

    def settle(ref, sem):
        pltpu.make_async_copy(ref, ref, sem).wait()

    own_rows = pl.ds(pl.multiple_of(here * TOK, TOK), TOK)
    loads = [
        pltpu.make_async_copy(src, dst, in_sem.at[i])
        for i, (src, dst) in enumerate(
            [(um_in, um), (act_in, nrm.at[own_rows]), (dm_in, dm), (cot_in, og.at[own_rows])]
        )
    ]
    for load in loads:
        load.start()

    cross = lax.rem(lax.div(x, 2) + here, 2)
    barrier = pltpu.get_barrier_semaphore()

    def greet(k, _):
        x_, zc_ = peer(k)
        pl.semaphore_signal(barrier, inc=1, device_id=(place(x_, yl, zc_), here), device_id_type=MESH)
        return 0

    lax.fori_loop(1, GROUP, greet, 0)
    for to_path, to_dp in (
        (place(x, other_yl, zc), here),
        (path, there),
        (place(3 - x, yl, zc), there),
        (place(3 - x, other_yl, zc), there),
    ):
        pl.semaphore_signal(barrier, inc=1, device_id=(to_path, to_dp), device_id_type=MESH)

    def ring(row, blocks, minus, plus):
        own, from_minus, from_plus, opposite = blocks
        halves = pl.ds(0, C // 2), pl.ds(C // 2, C // 2)
        hops = [
            (own, from_minus, plus),
            (own, from_plus, minus),
            (from_minus.at[halves[0]], opposite.at[halves[0]], plus),
            (from_plus.at[halves[1]], opposite.at[halves[1]], minus),
        ]
        return [
            remote(src, dst, ring_send.at[row, n], ring_recv.at[row, n], to, here)
            for n, (src, dst, to) in enumerate(hops)
        ]

    x_minus, x_plus = place(lax.rem(x + 3, 4), yl, zc), place(lax.rem(x + 1, 4), yl, zc)
    z_minus = place(x, yl, lax.rem(z + 3, 4) * 2 + core)
    z_plus = place(x, yl, lax.rem(z + 1, 4) * 2 + core)
    up_x, up_z = (up_x0, up_x1, up_x2, up_x3), (up_z0, up_z1, up_z2, up_z3)
    dn_x, dn_z = (dn_x0, dn_x1, dn_x2, dn_x3), (dn_z0, dn_z1, dn_z2, dn_z3)
    rings = [
        ring(0, up_x, x_minus, x_plus),
        ring(1, up_z, z_minus, z_plus),
        ring(2, dn_x, x_minus, x_plus),
        ring(3, dn_z, z_minus, z_plus),
    ]
    shift = (0, 3, 1, 2)

    def along_z(k):
        return x, zc_at(k)

    def along_x(k):
        return lax.rem(x + lax.div(k, 2), 4), z * 2 + lax.rem(core + k, 2)

    def pick_and_send(level, blocks, part, first_slot, peers, buf, landing, send, recv):
        def make(k):
            x_, zc_ = peers(k)
            slot = first_slot + part * 8 + k
            buf[slot] = blocks[part][table[place(x_, yl, zc_), level]]
            return buf.at[slot], place(x_, yl, zc_)

        source, _ = make(0)
        pltpu.make_async_copy(source, landing, recv).start()

        def one(k, _):
            source, to_path = make(k)
            remote(source, landing, send, recv, to_path, here).start()
            return 0

        lax.fori_loop(1, 8, one, 0)

    def up_picks_x(part):
        from_x = lax.rem(x + shift[part], 4)
        pick_and_send(0, up_x, part, 0, along_z, buf_a, wup.at[from_x, yl, zc], wu_send, wu_recv)

    def up_picks_z(part):
        from_zc = lax.rem(z + shift[part], 4) * 2 + core
        pick_and_send(0, up_z, part, GROUP, along_x, buf_a, wup.at[x, other_yl, from_zc], wu_send, wu_recv)

    def dn_landing(x_, side, zc_):
        crossed = lax.rem(lax.div(x_, 2) + here, 2)
        owner_x = x_ + crossed * (3 - 2 * x_)
        owner_dp = here + crossed * (1 - 2 * here)
        return wdn.at[owner_dp, (owner_x - 2 * here) * 16 + side * 8 + zc_]

    def dn_picks_x(part):
        landing = dn_landing(lax.rem(x + shift[part], 4), 0, zc)
        pick_and_send(1, dn_x, part, 0, along_z, buf_b, landing, wd_send, wd_recv)

    def dn_picks_z(part):
        landing = dn_landing(x, 1, lax.rem(z + shift[part], 4) * 2 + core)
        pick_and_send(1, dn_z, part, GROUP, along_x, buf_b, landing, wd_send, wd_recv)

    loads[0].wait()
    up_x0[...] = um[...].astype(BF16)
    pl.semaphore_wait(barrier, GROUP + 3)
    up_swap = remote(up_x0, up_z0, y_send.at[0], y_recv.at[0], place(x, other_yl, zc), here)
    up_swap.start()
    rings[0][0].start()
    rings[0][1].start()
    up_picks_x(0)

    loads[2].wait()
    dnb[...] = dm[...].astype(BF16)
    x_to = x + cross * (3 - 2 * x)
    dp_to = here + cross * (1 - 2 * here)

    def dn_copies(side):
        own = (dn_x0, dn_z0)[side]
        far = remote(dnb, own, dn_send.at[0], blk_recv.at[side], place(x_to, other_yl, zc), dp_to)
        near = remote(dnb, own, dn_send.at[1], blk_recv.at[side], place(3 - x, yl, zc), there)
        return far, near, pltpu.make_async_copy(dnb, own, blk_recv.at[side])

    for side in range(2):

        @pl.when(yl == side)
        def _(side=side):
            far, near, local = dn_copies(side)
            far.start()
            pl.when(cross == 1)(near.start)
            pl.when(cross == 0)(local.start)

    loads[1].wait()
    for part in range(3):
        rows = pl.ds(pl.multiple_of(here * TOK + part * 128, 128), 128)
        wide = nrm[rows, :].astype(F32)
        mean_square = jnp.mean(wide * wide, axis=-1, keepdims=True)
        nrm[rows, :] = (wide * lax.rsqrt(mean_square + 1e-06)).astype(BF16)
    nrm_swap = remote(nrm.at[own_rows], nrm.at[own_rows], y_send.at[1], y_recv.at[1], path, there)
    nrm_swap.start()
    loads[3].wait()
    live = jnp.sum((ids[...] != 0).astype(F32))
    for part in range(3):
        rows = pl.ds(pl.multiple_of(here * TOK + part * 128, 128), 128)
        position = (lax.broadcasted_iota(jnp.int32, (128, D), 0) + part * 128).astype(F32)
        og[rows, :] = jnp.where(position < live, og[rows, :].astype(F32), 0.0).astype(BF16)
    count[0] = jnp.broadcast_to(live, (8, 128))
    count_swap = remote(count.at[0], count.at[1], y_send.at[3], y_recv.at[3], path, there)
    count_swap.start()
    og_swap = remote(og.at[own_rows], og.at[own_rows], y_send.at[2], y_recv.at[2], path, there)
    og_swap.start()

    up_swap.wait()
    rings[1][0].start()
    rings[1][1].start()
    up_picks_z(0)

    def pass_on(row):
        for n in range(2):
            rings[row][n].wait_recv()
            rings[row][n + 2].start()

    def await_opposite(row):
        for n in range(2, 4):
            rings[row][n].wait_recv()

    pass_on(0)
    up_picks_x(1)
    up_picks_x(2)
    for side in range(2):
        dn_copies(side)[0].wait_recv()
        rings[2 + side][0].start()
        rings[2 + side][1].start()
    pass_on(1)
    up_picks_z(1)
    up_picks_z(2)
    await_opposite(0)
    up_picks_x(3)
    await_opposite(1)
    up_picks_z(3)
    dn_picks_x(0)
    dn_picks_z(0)
    pass_on(2)
    dn_picks_x(1)
    dn_picks_x(2)
    pass_on(3)
    dn_picks_z(1)
    dn_picks_z(2)

    nrm_swap.wait()

    def turn(i, _):
        cols = pl.ds(pl.multiple_of(i * 256, 256), 256)
        nrm_t[cols, :] = nrm[:, cols].T
        return 0

    lax.fori_loop(0, 4, turn, 0)
    count_swap.wait()
    per_count = 1.0 / (count[0] + count[1])
    per_count = per_count[0:1, 0:1]
    og_swap.wait()

    def scale_rows(i, _):
        rows = pl.ds(pl.multiple_of(i * 64, 64), 64)
        og[rows, :] = (og[rows, :].astype(F32) * per_count).astype(BF16)
        return 0

    lax.fori_loop(0, 12, scale_rows, 0)

    down_x = [here * 2 + lax.rem(x + i, 2) for i in range(2)] + [there * 2 + lax.rem(x + i, 2) for i in range(2)]
    up_block = [lax.rem(x + i, 4) for i in (2, 1, 3, 0)]

    order = (0, 1, 2, 3, 4, 5, 6, 7)

    def fetch(turn_no):
        if turn_no >= 8:
            return
        slot = turn_no % 2
        step = order[turn_no]
        for kind, (down_source, up_source) in enumerate(((down_first, up_first), (down_second, up_second))):
            if step < 4:
                rows = pl.ds(pl.multiple_of(down_x[step] * 1024, 1024), 1024)
                pltpu.make_async_copy(
                    down_source.at[rows], mom.at[slot, kind], mom_sem.at[slot, kind]
                ).start()
            else:
                rows = pl.ds(pl.multiple_of(up_block[step - 4] * 256, 256), 256)
                for b in range(4):
                    pltpu.make_async_copy(
                        up_source.at[rows, pl.ds(b * 512, 512)],
                        mom.at[slot, kind, pl.ds(b * 256, 256)],
                        mom_sem.at[slot, kind],
                    ).start()

    def await_moments(turn_no):
        slot = turn_no % 2
        for kind in range(2):
            settle(mom.at[slot, kind], mom_sem.at[slot, kind])

    fetch(0)
    fetch(1)

    settle(wup, wu_recv)
    mine_cols = pl.ds(pl.multiple_of(here * HALF_D, HALF_D), HALF_D)
    their_cols = pl.ds(pl.multiple_of(there * HALF_D, HALF_D), HALF_D)

    def g_copy(chunk):
        rows = pl.ds(pl.multiple_of(chunk * 512, 512), 512)
        return remote(gsend.at[rows], grecv.at[rows], g_send.at[chunk], g_recv.at[chunk], path, there)

    def pre_act(i, half):
        cols = pl.ds(pl.multiple_of(i * 256, 256), 256)
        weights = wup[:, :, :, :, cols].reshape(D, 256)
        wide_a[half] = jnp.dot(nrm[...], weights, preferred_element_type=F32)

    first_tile = 4 * lax.rem(x, 2)
    pre_act(first_tile, 0)

    def hidden(pair, _):
        for half in range(2):
            i = lax.rem(first_tile + pair * 2 + half, 8)
            pre_act(lax.rem(i + 1, 8), 1 - half)
            cols = pl.ds(pl.multiple_of(i * 256, 256), 256)
            for strip in range(24):
                rows = pl.ds(strip * 32, 32)
                pre = wide_a[half, rows, :] * UP_SCALE
                sig = 0.5 * jnp.tanh(0.5 * pre) + 0.5
                out = pre * sig
                act_a[half, rows, :] = out.astype(BF16)
                gp[rows, cols] = (sig + out * (1.0 - sig)).astype(BF16)
            out_t = act_a[half].T
            theirs = jnp.dot(out_t, og[:, their_cols], preferred_element_type=F32)
            gsend[cols, :] = (theirs * DOWN_SCALE).astype(BF16)
            if half == 1:
                g_copy(lax.div(i, 2)).start()
            mine = jnp.dot(out_t, og[:, mine_cols], preferred_element_type=F32)
            gmine[cols, :] = (mine * DOWN_SCALE).astype(BF16)
        return 0

    lax.fori_loop(0, 4, hidden, 0)

    await_opposite(2)
    dn_picks_x(3)
    await_opposite(3)
    dn_picks_z(3)

    def down_delta(turn_no):
        step = order[turn_no]
        x_ = down_x[step]
        source = gmine if step < 2 else grecv
        first_row = lax.rem(x_, 2) * 1024
        if step >= 2:
            for half in range(2):
                g_copy(lax.rem(x_, 2) * 2 + half).wait_recv()
        await_moments(turn_no)
        slot = turn_no % 2

        def one(q, _):
            for b in range(4):
                rows = pl.ds(pl.multiple_of(q * 64 + b * 16, 16), 16)
                grad = source[pl.ds(pl.multiple_of(first_row + q * 64 + b * 16, 16), 16), :].astype(F32)
                delta = step_direction(grad, mom[slot, 0, rows, :], mom[slot, 1, rows, :])
                buf_a[x_ * 16 + q, :, pl.ds(b * 512, 512)] = delta
            return 0

        lax.fori_loop(0, 16, one, 0)
        fetch(turn_no + 2)

    def send_down_delta(step, side):
        x_ = down_x[step]

        def send(k, _):
            zc_ = zc_at(k)
            row = x_ * 16 + side * 8 + zc_
            away = (x_ * 8 + zc_) != group

            @pl.when(away)
            def _():
                remote(
                    buf_a.at[row], rdn.at[side, group], dd_send, dd_recv.at[side], place(x_, yl, zc_), here
                ).start()

            @pl.when(jnp.logical_not(away))
            def _():
                pltpu.make_async_copy(buf_a.at[row], rdn.at[side, group], dd_recv.at[side]).start()

            return 0

        lax.fori_loop(0, 8, send, 0)

    settle(buf_a.at[pl.ds(0, 2 * GROUP - 8)], wu_send)
    for turn_no in range(4):
        down_delta(turn_no)
        send_down_delta(turn_no, other_yl)
        send_down_delta(turn_no, yl)

    settle(wdn, wd_recv)

    def hidden_grad(i, _):
        cols = pl.ds(pl.multiple_of(i * 256, 256), 256)
        low = wdn[0, pl.ds(i * 4, 4)].reshape(256, HALF_D)
        high = wdn[1, pl.ds(i * 4, 4)].reshape(256, HALF_D)
        grad = lax.dot_general(og[:, pl.ds(0, HALF_D)], low, NT, preferred_element_type=F32)
        grad += lax.dot_general(og[:, pl.ds(HALF_D, HALF_D)], high, NT, preferred_element_type=F32)
        gp[:, cols] = (grad * DOWN_SCALE * gp[:, cols].astype(F32)).astype(BF16)
        return 0

    lax.fori_loop(0, 8, hidden_grad, 0)
    settle(buf_b.at[pl.ds(0, 2 * GROUP - 8)], wd_send)

    def send_up_delta(x_, zc_, side):
        row = x_ * 16 + side * 8 + zc_
        away = (x_ * 8 + zc_) != group

        @pl.when(away)
        def _():
            remote(
                buf_b.at[row], rup.at[side, group], du_send, du_recv.at[side], place(x_, yl, zc_), here
            ).start()

        @pl.when(jnp.logical_not(away))
        def _():
            pltpu.make_async_copy(buf_b.at[row], rup.at[side, group], du_recv.at[side]).start()

    def up_step(turn_no):
        x_ = up_block[order[turn_no] - 4]
        slot = turn_no % 2
        lhs = nrm_t[pl.ds(pl.multiple_of(x_ * 256, 256), 256), :]

        def up_grad(b):
            wide_b[b % 2] = jnp.dot(lhs, gp[:, pl.ds(b * 512, 512)], preferred_element_type=F32)

        up_grad(0)
        await_moments(turn_no)
        for b in range(4):
            if b < 3:
                up_grad(b + 1)
            for i in range(16):
                rows = pl.ds(b * 256 + i * 16, 16)
                grad = wide_b[b % 2, pl.ds(i * 16, 16), :] * UP_SCALE
                delta = step_direction(grad, mom[slot, 0, rows, :], mom[slot, 1, rows, :])
                buf_b[x_ * 16 + i, pl.ds(b * 16, 16), :] = delta
        fetch(turn_no + 2)

        def send(k, _):
            send_up_delta(x_, zc_at(k), other_yl)
            return 0

        lax.fori_loop(0, 8, send, 0)

    for turn_no in range(4, 8):
        up_step(turn_no)

    def send_rest(k, _):
        x_, zc_ = peer(lax.rem(k * 11, GROUP))
        send_up_delta(x_, zc_, yl)
        return 0

    lax.fori_loop(0, GROUP, send_rest, 0)

    lane = lax.broadcasted_iota(jnp.int32, (16, C * 16), 1)
    same_row = (lane & 15) == lax.broadcasted_iota(jnp.int32, (16, C * 16), 0)
    for level, pick in enumerate((pick_up, pick_dn)):

        def fill(k, _, level=level):
            module = table[lax.div(k, 8) * 16 + yl * 8 + lax.rem(k, 8), level]
            rows = pl.ds(pl.multiple_of(k * 16, 16), 16)
            pick_t[rows, :] = jnp.where(same_row & ((lane >> 4) == module), 1.0, 0.0)
            return 0

        lax.fori_loop(0, GROUP, fill, 0)
        pick[...] = pick_t[...].T.astype(BF16)

        def tally(k, counts, level=level):
            module = table[k, level]
            return tuple(n + jnp.where(module == m, 1, 0) for m, n in enumerate(counts))

        counts = lax.fori_loop(0, 64, tally, (jnp.int32(0),) * C)
        for m in range(C):
            used[level * C + m] = counts[m]

    def down_sum(side, b):
        block = rdn[side, :, :, pl.ds(b * 512, 512)].reshape(GROUP * 16, 512)
        return jnp.dot(pick_dn[...], block, preferred_element_type=F32).reshape(C, 16, 512)

    def up_sum(side, b):
        block = rup[side, :, pl.ds(b * 16, 16), :].reshape(GROUP * 16, 512)
        return jnp.dot(pick_up[...], block, preferred_element_type=F32).reshape(C, 16, 512)

    def finish(total, master, level, rows, cols):
        for m in range(C):
            number = jnp.broadcast_to(used[level * C + m].astype(F32), (8, 128))
            per_used = (1.0 / jnp.maximum(number, 1.0))[0:1, 0:1]
            decay = (0.01 * jnp.minimum(number, 1.0))[0:1, 0:1]
            weights = master[m, rows, cols].astype(BF16).astype(F32)
            master[m, rows, cols] = total[m] * per_used + decay * weights

    mate = place(x, other_yl, zc)
    stores = [
        pltpu.make_async_copy(src, dst, out_sem.at[i]) for i, (src, dst) in enumerate([(dm, dm_out), (um, um_out)])
    ]
    settle(rdn.at[other_yl], dd_recv.at[other_yl])
    for b in range(4):
        pdn_send[:, :, pl.ds(b * 512, 512)] = down_sum(other_yl, b).astype(BF16)
    dn_part = remote(pdn_send, pdn_recv, y_send.at[4], y_recv.at[4], mate, here)
    dn_part.start()
    settle(rdn.at[yl], dd_recv.at[yl])
    dn_part.wait()
    for b in range(4):
        cols = pl.ds(b * 512, 512)
        total = down_sum(yl, b) + pdn_recv[:, :, cols].astype(F32)
        finish(total, dm, 1, pl.ds(b * 16, 16), pl.ds(0, 512))
    stores[0].start()

    settle(rup.at[other_yl], du_recv.at[other_yl])
    for b in range(4):
        pup_send[:, pl.ds(b * 16, 16), :] = up_sum(other_yl, b).astype(BF16)
    up_part = remote(pup_send, pup_recv, y_send.at[5], y_recv.at[5], mate, here)
    up_part.start()
    settle(rup.at[yl], du_recv.at[yl])
    up_part.wait()
    for b in range(4):
        rows = pl.ds(b * 16, 16)
        total = up_sum(yl, b) + pup_recv[:, rows, :].astype(F32)
        finish(total, um, 0, pl.ds(0, 16), pl.ds(b * 512, 512))
    stores[1].start()

    far, near, _ = dn_copies(0)
    far.wait_send()
    pl.when(cross == 1)(near.wait_send)
    for hops in rings:
        for hop in hops:
            hop.wait_send()
    for chunk in range(4):
        g_copy(chunk).wait_send()
    settle(buf_a.at[pl.ds(0, 2 * GROUP - 2)], dd_send)
    settle(buf_b.at[pl.ds(0, 2 * GROUP - 2)], du_send)
    for store in stores:
        store.wait()


def shards(
    activations,
    cotangent,
    token_ids,
    path_table,
    up_master,
    down_master,
    up_momentum,
    down_momentum,
    up_first,
    up_second,
    down_first,
    down_second,
):
    anywhere = pl.BlockSpec(memory_space=pl.ANY)
    smem = pl.BlockSpec(memory_space=pltpu.SMEM)
    vmem = pl.BlockSpec(memory_space=pltpu.VMEM)
    dma = pltpu.SemaphoreType.DMA
    up_mean, down_mean = pl.pallas_call(
        kernel,
        out_shape=[jax.ShapeDtypeStruct(array.shape, F32) for array in (up_master, down_master)],
        in_specs=[smem, vmem] + [anywhere] * 8,
        out_specs=[anywhere] * 2,
        scratch_shapes=[
            pltpu.VMEM((C, 16, HALF_F), F32),
            pltpu.VMEM((C, 64, HALF_D), F32),
            *[pltpu.VMEM((C, 16, HALF_F), BF16)] * 8,
            *[pltpu.VMEM((C, 64, HALF_D), BF16)] * 8,
            pltpu.VMEM((C, 64, HALF_D), BF16),
            pltpu.VMEM((2 * GROUP, 16, HALF_F), BF16),
            pltpu.VMEM((2 * GROUP, 64, HALF_D), BF16),
            pltpu.VMEM((4, 2, 8, 16, HALF_F), BF16),
            pltpu.VMEM((2, GROUP, 64, HALF_D), BF16),
            pltpu.VMEM((2, GROUP, 16, HALF_F), BF16),
            pltpu.VMEM((2, GROUP, 64, HALF_D), BF16),
            pltpu.VMEM((HALF_F, HALF_D), BF16),
            pltpu.VMEM((HALF_F, HALF_D), BF16),
            pltpu.VMEM((HALF_F, HALF_D), BF16),
            pltpu.VMEM((2 * TOK, D), BF16),
            pltpu.VMEM((D, 2 * TOK), BF16),
            pltpu.VMEM((2 * TOK, D), BF16),
            pltpu.VMEM((2, 8, 128), F32),
            pltpu.SMEM((2 * C,), jnp.int32),
            pltpu.VMEM((2 * TOK, HALF_F), BF16),
            pltpu.VMEM((2, 2 * TOK, 256), F32),
            pltpu.VMEM((2, 2 * TOK, 256), BF16),
            pltpu.VMEM((2, 256, 512), F32),
            pltpu.VMEM((2, 2, 1024, 512), BF16),
            pltpu.VMEM((C, 16, HALF_F), BF16),
            pltpu.VMEM((C, 16, HALF_F), BF16),
            pltpu.VMEM((C, 64, HALF_D), BF16),
            pltpu.VMEM((C, 64, HALF_D), BF16),
            pltpu.VMEM((GROUP * 16, C * 16), F32),
            pltpu.VMEM((C * 16, GROUP * 16), BF16),
            pltpu.VMEM((C * 16, GROUP * 16), BF16),
            dma((4,)),
            dma((2, 2)),
            dma((2,)),
            dma((6,)),
            dma((6,)),
            dma((4, 4)),
            dma((4, 4)),
            dma((2,)),
            dma((2,)),
            dma,
            dma,
            dma,
            dma,
            dma((4,)),
            dma((4,)),
            dma,
            dma((2,)),
            dma,
            dma((2,)),
        ],
        compiler_params=pltpu.CompilerParams(
            collective_id=0, has_side_effects=True, vmem_limit_bytes=62 * 1024 * 1024
        ),
        cost_estimate=pl.CostEstimate(flops=12_884_901_888, bytes_accessed=30_000_000, transcendentals=1_572_864),
    )(
        path_table,
        token_ids,
        activations[0],
        cotangent[0],
        up_master,
        down_master,
        up_first[0],
        up_second[0],
        down_first[0],
        down_second[0],
    )
    new_up_momentum = 0.9 * up_momentum + up_mean
    new_down_momentum = 0.9 * down_momentum + down_mean
    new_up_master = up_master - 0.7 * (up_mean + 0.9 * new_up_momentum)
    new_down_master = down_master - 0.7 * (down_mean + 0.9 * new_down_momentum)
    return (new_up_master, new_down_master, new_up_momentum, new_down_momentum)


def solution(mesh):
    placed = (
        P("path", "dp", None),
        P("path", "dp", None),
        P("path", "dp"),
        P(),
        P(None, "path", "dp"),
        P(None, "path", "dp"),
        P(None, "path", "dp"),
        P(None, "path", "dp"),
        P("path", None, "dp"),
        P("path", None, "dp"),
        P("path", None, "dp"),
        P("path", None, "dp"),
    )
    return jax.shard_map(
        shards,
        mesh=mesh,
        in_specs=placed,
        out_specs=(
            P(None, "path", "dp"),
            P(None, "path", "dp"),
            P(None, "path", "dp"),
            P(None, "path", "dp"),
        ),
        check_vma=False,
    )
```

```python
import jax
import jax.numpy as jnp
from jax import lax
from jax.experimental import pallas as pl
from jax.experimental.pallas import tpu as pltpu
from jax.sharding import PartitionSpec as P

D = 1024
F = 4096
C = 8
TOK = 384
HALF_F = F // 2
HALF_D = D // 2
GROUP = 32
MESH = pl.DeviceIdType.MESH
BF16 = jnp.bfloat16
F32 = jnp.float32
NT = (((1,), (1,)), ((), ()))
TN = (((0,), (0,)), ((), ()))
UP_SCALE = D ** (-0.5)
DOWN_SCALE = F ** (-0.5)


def step_direction(gradient, first_moment, second_moment):
    first_new = 0.9 * first_moment.astype(F32) + 0.1 * gradient
    second_new = 0.95 * second_moment.astype(F32) + 0.05 * gradient * gradient
    below = second_new * lax.rsqrt(second_new) + 1e-08
    over = pl.reciprocal(below, approx=True)
    over = over * (2.0 - below * over)
    return (0.1 * first_new * over).astype(BF16)


def kernel(
    table, ids, act_in, cot_in, um_in, dm_in, up_first, up_second, down_first, down_second, um_out, dm_out,
    um, dm, up_x0, up_x1, up_x2, up_x3, up_z0, up_z1, up_z2, up_z3,
    dn_x0, dn_x1, dn_x2, dn_x3, dn_z0, dn_z1, dn_z2, dn_z3, dnb, buf_a, buf_b, wup, wdn, rdn, rup,
    gsend, gmine, grecv, nrm, nrm_t, og, count, used, gp, wide_a, act_a, wide_b, mom,
    pdn_send, pdn_recv, pup_send, pup_recv, pick_t, pick_up, pick_dn,
    in_sem, mom_sem, out_sem, y_send, y_recv, ring_send, ring_recv, dn_send, blk_recv, wu_send, wu_recv, wd_send, wd_recv,
    g_send, g_recv, dd_send, dd_recv, du_send, du_recv,
):
    path = lax.axis_index("path")
    here = lax.axis_index("dp")
    x = lax.div(path, 16)
    yl = lax.rem(lax.div(path, 8), 2)
    zc = lax.rem(path, 8)
    z = lax.div(zc, 2)
    core = lax.rem(zc, 2)
    group = x * 8 + zc
    other_yl = 1 - yl
    there = 1 - here

    def place(x_, yl_, zc_):
        return x_ * 16 + yl_ * 8 + zc_

    def zc_at(k):
        return lax.rem(z + lax.rem(lax.div(k, 2), 4), 4) * 2 + lax.rem(core + k, 2)

    def peer(k):
        return lax.rem(x + lax.div(k, 8), 4), zc_at(k)

    def remote(src, dst, send, recv, to_path, to_dp):
        return pltpu.make_async_remote_copy(
            src_ref=src, dst_ref=dst, send_sem=send, recv_sem=recv,
            device_id=(to_path, to_dp), device_id_type=MESH,
        )

    def settle(ref, sem):
        pltpu.make_async_copy(ref, ref, sem).wait()

    own_rows = pl.ds(pl.multiple_of(here * TOK, TOK), TOK)
    loads = [
        pltpu.make_async_copy(src, dst, in_sem.at[i])
        for i, (src, dst) in enumerate(
            [(um_in, um), (act_in, nrm.at[own_rows]), (dm_in, dm), (cot_in, og.at[own_rows])]
        )
    ]
    for load in loads:
        load.start()

    cross = lax.rem(lax.div(x, 2) + here, 2)
    barrier = pltpu.get_barrier_semaphore()

    def greet(k, _):
        x_, zc_ = peer(k)
        pl.semaphore_signal(barrier, inc=1, device_id=(place(x_, yl, zc_), here), device_id_type=MESH)
        return 0

    lax.fori_loop(1, GROUP, greet, 0)
    for to_path, to_dp in (
        (place(x, other_yl, zc), here),
        (path, there),
        (place(3 - x, yl, zc), there),
        (place(3 - x, other_yl, zc), there),
    ):
        pl.semaphore_signal(barrier, inc=1, device_id=(to_path, to_dp), device_id_type=MESH)

    def ring(row, blocks, minus, plus):
        own, from_minus, from_plus, opposite = blocks
        halves = pl.ds(0, C // 2), pl.ds(C // 2, C // 2)
        hops = [
            (own, from_minus, plus),
            (own, from_plus, minus),
            (from_minus.at[halves[0]], opposite.at[halves[0]], plus),
            (from_plus.at[halves[1]], opposite.at[halves[1]], minus),
        ]
        return [
            remote(src, dst, ring_send.at[row, n], ring_recv.at[row, n], to, here)
            for n, (src, dst, to) in enumerate(hops)
        ]

    x_minus, x_plus = place(lax.rem(x + 3, 4), yl, zc), place(lax.rem(x + 1, 4), yl, zc)
    z_minus = place(x, yl, lax.rem(z + 3, 4) * 2 + core)
    z_plus = place(x, yl, lax.rem(z + 1, 4) * 2 + core)
    up_x, up_z = (up_x0, up_x1, up_x2, up_x3), (up_z0, up_z1, up_z2, up_z3)
    dn_x, dn_z = (dn_x0, dn_x1, dn_x2, dn_x3), (dn_z0, dn_z1, dn_z2, dn_z3)
    rings = [
        ring(0, up_x, x_minus, x_plus),
        ring(1, up_z, z_minus, z_plus),
        ring(2, dn_x, x_minus, x_plus),
        ring(3, dn_z, z_minus, z_plus),
    ]
    shift = (0, 3, 1, 2)

    def along_z(k):
        return x, zc_at(k)

    def along_x(k):
        return lax.rem(x + lax.div(k, 2), 4), z * 2 + lax.rem(core + k, 2)

    def pick_and_send(level, blocks, part, first_slot, peers, buf, landing, send, recv):
        def make(k):
            x_, zc_ = peers(k)
            slot = first_slot + part * 8 + k
            buf[slot] = blocks[part][table[place(x_, yl, zc_), level]]
            return buf.at[slot], place(x_, yl, zc_)

        source, _ = make(0)
        pltpu.make_async_copy(source, landing, recv).start()

        def one(k, _):
            source, to_path = make(k)
            remote(source, landing, send, recv, to_path, here).start()
            return 0

        lax.fori_loop(1, 8, one, 0)

    def up_picks_x(part):
        from_x = lax.rem(x + shift[part], 4)
        pick_and_send(0, up_x, part, 0, along_z, buf_a, wup.at[from_x, yl, zc], wu_send, wu_recv)

    def up_picks_z(part):
        from_zc = lax.rem(z + shift[part], 4) * 2 + core
        pick_and_send(0, up_z, part, GROUP, along_x, buf_a, wup.at[x, other_yl, from_zc], wu_send, wu_recv)

    def dn_landing(x_, side, zc_):
        crossed = lax.rem(lax.div(x_, 2) + here, 2)
        owner_x = x_ + crossed * (3 - 2 * x_)
        owner_dp = here + crossed * (1 - 2 * here)
        return wdn.at[owner_dp, (owner_x - 2 * here) * 16 + side * 8 + zc_]

    def dn_picks_x(part):
        landing = dn_landing(lax.rem(x + shift[part], 4), 0, zc)
        pick_and_send(1, dn_x, part, 0, along_z, buf_b, landing, wd_send, wd_recv)

    def dn_picks_z(part):
        landing = dn_landing(x, 1, lax.rem(z + shift[part], 4) * 2 + core)
        pick_and_send(1, dn_z, part, GROUP, along_x, buf_b, landing, wd_send, wd_recv)

    loads[0].wait()
    up_x0[...] = um[...].astype(BF16)
    pl.semaphore_wait(barrier, GROUP + 3)
    up_swap = remote(up_x0, up_z0, y_send.at[0], y_recv.at[0], place(x, other_yl, zc), here)
    up_swap.start()
    rings[0][0].start()
    rings[0][1].start()
    up_picks_x(0)

    loads[2].wait()
    dnb[...] = dm[...].astype(BF16)
    x_to = x + cross * (3 - 2 * x)
    dp_to = here + cross * (1 - 2 * here)

    def dn_copies(side):
        own = (dn_x0, dn_z0)[side]
        far = remote(dnb, own, dn_send.at[0], blk_recv.at[side], place(x_to, other_yl, zc), dp_to)
        near = remote(dnb, own, dn_send.at[1], blk_recv.at[side], place(3 - x, yl, zc), there)
        return far, near, pltpu.make_async_copy(dnb, own, blk_recv.at[side])

    for side in range(2):

        @pl.when(yl == side)
        def _(side=side):
            far, near, local = dn_copies(side)
            far.start()
            pl.when(cross == 1)(near.start)
            pl.when(cross == 0)(local.start)

    loads[1].wait()
    for part in range(3):
        rows = pl.ds(pl.multiple_of(here * TOK + part * 128, 128), 128)
        wide = nrm[rows, :].astype(F32)
        mean_square = jnp.mean(wide * wide, axis=-1, keepdims=True)
        nrm[rows, :] = (wide * lax.rsqrt(mean_square + 1e-06)).astype(BF16)
    nrm_swap = remote(nrm.at[own_rows], nrm.at[own_rows], y_send.at[1], y_recv.at[1], path, there)
    nrm_swap.start()
    loads[3].wait()
    live = jnp.sum((ids[...] != 0).astype(F32))
    for part in range(3):
        rows = pl.ds(pl.multiple_of(here * TOK + part * 128, 128), 128)
        position = (lax.broadcasted_iota(jnp.int32, (128, D), 0) + part * 128).astype(F32)
        og[rows, :] = jnp.where(position < live, og[rows, :].astype(F32), 0.0).astype(BF16)
    count[0] = jnp.broadcast_to(live, (8, 128))
    count_swap = remote(count.at[0], count.at[1], y_send.at[3], y_recv.at[3], path, there)
    count_swap.start()
    og_swap = remote(og.at[own_rows], og.at[own_rows], y_send.at[2], y_recv.at[2], path, there)
    og_swap.start()

    up_swap.wait()
    rings[1][0].start()
    rings[1][1].start()
    up_picks_z(0)

    def pass_on(row):
        for n in range(2):
            rings[row][n].wait_recv()
            rings[row][n + 2].start()

    def await_opposite(row):
        for n in range(2, 4):
            rings[row][n].wait_recv()

    pass_on(0)
    up_picks_x(1)
    up_picks_x(2)
    for side in range(2):
        dn_copies(side)[0].wait_recv()
        rings[2 + side][0].start()
        rings[2 + side][1].start()
    pass_on(1)
    up_picks_z(1)
    up_picks_z(2)
    await_opposite(0)
    up_picks_x(3)
    await_opposite(1)
    up_picks_z(3)
    dn_picks_x(0)
    dn_picks_z(0)
    pass_on(2)
    dn_picks_x(1)
    dn_picks_x(2)
    pass_on(3)
    dn_picks_z(1)
    dn_picks_z(2)

    nrm_swap.wait()

    def turn(i, _):
        cols = pl.ds(pl.multiple_of(i * 256, 256), 256)
        nrm_t[cols, :] = nrm[:, cols].T
        return 0

    lax.fori_loop(0, 4, turn, 0)
    count_swap.wait()
    per_count = 1.0 / (count[0] + count[1])
    per_count = per_count[0:1, 0:1]
    og_swap.wait()

    def scale_rows(i, _):
        rows = pl.ds(pl.multiple_of(i * 64, 64), 64)
        og[rows, :] = (og[rows, :].astype(F32) * per_count).astype(BF16)
        return 0

    lax.fori_loop(0, 12, scale_rows, 0)

    down_x = [half * 2 + lax.rem(x + i, 2) for half in (here, there) for i in range(2)]
    up_block = [lax.rem(x + i, 4) for i in (2, 1, 3, 0)]

    order = (0, 1, 2, 4, 5, 6, 7, 3)

    def fetch(turn_no):
        if turn_no >= 8:
            return
        slot = turn_no % 2
        step = order[turn_no]
        for kind, (down_source, up_source) in enumerate(((down_first, up_first), (down_second, up_second))):
            if step < 4:
                rows = pl.ds(pl.multiple_of(down_x[step] * 1024, 1024), 1024)
                pltpu.make_async_copy(
                    down_source.at[rows], mom.at[slot, kind], mom_sem.at[slot, kind]
                ).start()
            else:
                rows = pl.ds(pl.multiple_of(up_block[step - 4] * 256, 256), 256)
                for b in range(4):
                    pltpu.make_async_copy(
                        up_source.at[rows, pl.ds(b * 512, 512)],
                        mom.at[slot, kind, pl.ds(b * 256, 256)],
                        mom_sem.at[slot, kind],
                    ).start()

    def await_moments(turn_no):
        slot = turn_no % 2
        for kind in range(2):
            settle(mom.at[slot, kind], mom_sem.at[slot, kind])

    fetch(0)
    fetch(1)

    settle(wup, wu_recv)
    mine_cols = pl.ds(pl.multiple_of(here * HALF_D, HALF_D), HALF_D)
    their_cols = pl.ds(pl.multiple_of(there * HALF_D, HALF_D), HALF_D)

    def g_copy(chunk):
        rows = pl.ds(pl.multiple_of(chunk * 512, 512), 512)
        return remote(gsend.at[rows], grecv.at[rows], g_send.at[chunk], g_recv.at[chunk], path, there)

    def pre_act(i, half):
        cols = pl.ds(pl.multiple_of(i * 256, 256), 256)
        weights = wup[:, :, :, :, cols].reshape(D, 256)
        wide_a[half] = jnp.dot(nrm[...], weights, preferred_element_type=F32)

    first_tile = 4 * lax.rem(x, 2)
    pre_act(first_tile, 0)

    def hidden(pair, _):
        for half in range(2):
            i = lax.rem(first_tile + pair * 2 + half, 8)
            pre_act(lax.rem(i + 1, 8), 1 - half)
            cols = pl.ds(pl.multiple_of(i * 256, 256), 256)
            for strip in range(24):
                rows = pl.ds(strip * 32, 32)
                pre = wide_a[half, rows, :] * UP_SCALE
                sig = 0.5 * jnp.tanh(0.5 * pre) + 0.5
                out = pre * sig
                act_a[half, rows, :] = out.astype(BF16)
                gp[rows, cols] = (sig + out * (1.0 - sig)).astype(BF16)
            out_t = act_a[half].T
            theirs = jnp.dot(out_t, og[:, their_cols], preferred_element_type=F32)
            gsend[cols, :] = (theirs * DOWN_SCALE).astype(BF16)
            if half == 1:
                g_copy(lax.div(i, 2)).start()
            mine = jnp.dot(out_t, og[:, mine_cols], preferred_element_type=F32)
            gmine[cols, :] = (mine * DOWN_SCALE).astype(BF16)
        return 0

    lax.fori_loop(0, 4, hidden, 0)

    await_opposite(2)
    dn_picks_x(3)
    await_opposite(3)
    dn_picks_z(3)

    def down_delta(turn_no):
        step = order[turn_no]
        x_ = down_x[step]
        source = gmine if step < 2 else grecv
        first_row = lax.rem(x_, 2) * 1024
        if step >= 2:
            for half in range(2):
                g_copy(lax.rem(x_, 2) * 2 + half).wait_recv()
        await_moments(turn_no)
        slot = turn_no % 2

        def one(q, _):
            for b in range(4):
                rows = pl.ds(pl.multiple_of(q * 64 + b * 16, 16), 16)
                grad = source[pl.ds(pl.multiple_of(first_row + q * 64 + b * 16, 16), 16), :].astype(F32)
                delta = step_direction(grad, mom[slot, 0, rows, :], mom[slot, 1, rows, :])
                buf_a[x_ * 16 + q, :, pl.ds(b * 512, 512)] = delta
            return 0

        lax.fori_loop(0, 16, one, 0)
        fetch(turn_no + 2)

    def send_down_delta(step, side):
        x_ = down_x[step]

        def send(k, _):
            zc_ = zc_at(k)
            row = x_ * 16 + side * 8 + zc_
            away = (x_ * 8 + zc_) != group

            @pl.when(away)
            def _():
                remote(
                    buf_a.at[row], rdn.at[side, group], dd_send, dd_recv.at[side], place(x_, yl, zc_), here
                ).start()

            @pl.when(jnp.logical_not(away))
            def _():
                pltpu.make_async_copy(buf_a.at[row], rdn.at[side, group], dd_recv.at[side]).start()

            return 0

        lax.fori_loop(0, 8, send, 0)

    settle(buf_a.at[pl.ds(0, 2 * GROUP - 8)], wu_send)
    for turn_no in range(3):
        down_delta(turn_no)
        if turn_no != 1:
            send_down_delta(order[turn_no], other_yl)
            send_down_delta(order[turn_no], yl)

    settle(wdn, wd_recv)

    def hidden_grad(i, _):
        cols = pl.ds(pl.multiple_of(i * 256, 256), 256)
        low = wdn[0, pl.ds(i * 4, 4)].reshape(256, HALF_D)
        high = wdn[1, pl.ds(i * 4, 4)].reshape(256, HALF_D)
        grad = lax.dot_general(og[:, pl.ds(0, HALF_D)], low, NT, preferred_element_type=F32)
        grad += lax.dot_general(og[:, pl.ds(HALF_D, HALF_D)], high, NT, preferred_element_type=F32)
        gp[:, cols] = (grad * DOWN_SCALE * gp[:, cols].astype(F32)).astype(BF16)
        return 0

    lax.fori_loop(0, 8, hidden_grad, 0)
    settle(buf_b.at[pl.ds(0, 2 * GROUP - 8)], wd_send)

    def send_up_delta(x_, zc_, side):
        row = x_ * 16 + side * 8 + zc_
        away = (x_ * 8 + zc_) != group

        @pl.when(away)
        def _():
            remote(
                buf_b.at[row], rup.at[side, group], du_send, du_recv.at[side], place(x_, yl, zc_), here
            ).start()

        @pl.when(jnp.logical_not(away))
        def _():
            pltpu.make_async_copy(buf_b.at[row], rup.at[side, group], du_recv.at[side]).start()

    def up_step(turn_no):
        x_ = up_block[order[turn_no] - 4]
        slot = turn_no % 2
        lhs = nrm_t[pl.ds(pl.multiple_of(x_ * 256, 256), 256), :]

        def up_grad(b):
            wide_b[b % 2] = jnp.dot(lhs, gp[:, pl.ds(b * 512, 512)], preferred_element_type=F32)

        up_grad(0)
        await_moments(turn_no)
        for b in range(4):
            if b < 3:
                up_grad(b + 1)
            for i in range(16):
                rows = pl.ds(b * 256 + i * 16, 16)
                grad = wide_b[b % 2, pl.ds(i * 16, 16), :] * UP_SCALE
                delta = step_direction(grad, mom[slot, 0, rows, :], mom[slot, 1, rows, :])
                buf_b[x_ * 16 + i, pl.ds(b * 16, 16), :] = delta
        fetch(turn_no + 2)

        def send(k, _):
            send_up_delta(x_, zc_at(k), other_yl)
            return 0

        lax.fori_loop(0, 8, send, 0)

    for turn_no in range(3, 7):
        up_step(turn_no)

    def send_rest(k, _):
        x_, zc_ = peer(lax.rem(k * 11, GROUP))
        send_up_delta(x_, zc_, yl)
        return 0

    lax.fori_loop(0, GROUP, send_rest, 0)
    down_delta(7)
    for side in (other_yl, yl):
        send_down_delta(1, side)
        send_down_delta(3, side)

    lane = lax.broadcasted_iota(jnp.int32, (16, C * 16), 1)
    same_row = (lane & 15) == lax.broadcasted_iota(jnp.int32, (16, C * 16), 0)
    for level, pick in enumerate((pick_up, pick_dn)):

        def fill(k, _, level=level):
            module = table[lax.div(k, 8) * 16 + yl * 8 + lax.rem(k, 8), level]
            rows = pl.ds(pl.multiple_of(k * 16, 16), 16)
            pick_t[rows, :] = jnp.where(same_row & ((lane >> 4) == module), 1.0, 0.0)
            return 0

        lax.fori_loop(0, GROUP, fill, 0)
        pick[...] = pick_t[...].T.astype(BF16)

        def tally(k, counts, level=level):
            module = table[k, level]
            return tuple(n + jnp.where(module == m, 1, 0) for m, n in enumerate(counts))

        counts = lax.fori_loop(0, 64, tally, (jnp.int32(0),) * C)
        for m in range(C):
            used[level * C + m] = counts[m]

    def down_sum(side, b):
        block = rdn[side, :, :, pl.ds(b * 512, 512)].reshape(GROUP * 16, 512)
        return jnp.dot(pick_dn[...], block, preferred_element_type=F32).reshape(C, 16, 512)

    def up_sum(side, b):
        block = rup[side, :, pl.ds(b * 16, 16), :].reshape(GROUP * 16, 512)
        return jnp.dot(pick_up[...], block, preferred_element_type=F32).reshape(C, 16, 512)

    def finish(total, master, level, rows, cols):
        for m in range(C):
            number = jnp.broadcast_to(used[level * C + m].astype(F32), (8, 128))
            per_used = (1.0 / jnp.maximum(number, 1.0))[0:1, 0:1]
            decay = (0.01 * jnp.minimum(number, 1.0))[0:1, 0:1]
            weights = master[m, rows, cols].astype(BF16).astype(F32)
            master[m, rows, cols] = total[m] * per_used + decay * weights

    mate = place(x, other_yl, zc)
    stores = [
        pltpu.make_async_copy(src, dst, out_sem.at[i]) for i, (src, dst) in enumerate([(dm, dm_out), (um, um_out)])
    ]
    settle(rup.at[other_yl], du_recv.at[other_yl])
    for b in range(4):
        pup_send[:, pl.ds(b * 16, 16), :] = up_sum(other_yl, b).astype(BF16)
    up_part = remote(pup_send, pup_recv, y_send.at[5], y_recv.at[5], mate, here)
    up_part.start()
    settle(rup.at[yl], du_recv.at[yl])
    up_part.wait()
    for b in range(4):
        rows = pl.ds(b * 16, 16)
        total = up_sum(yl, b) + pup_recv[:, rows, :].astype(F32)
        finish(total, um, 0, pl.ds(0, 16), pl.ds(b * 512, 512))
    stores[1].start()

    settle(rdn.at[other_yl], dd_recv.at[other_yl])
    for b in range(4):
        pdn_send[:, :, pl.ds(b * 512, 512)] = down_sum(other_yl, b).astype(BF16)
    dn_part = remote(pdn_send, pdn_recv, y_send.at[4], y_recv.at[4], mate, here)
    dn_part.start()
    settle(rdn.at[yl], dd_recv.at[yl])
    dn_part.wait()
    for b in range(4):
        cols = pl.ds(b * 512, 512)
        total = down_sum(yl, b) + pdn_recv[:, :, cols].astype(F32)
        finish(total, dm, 1, pl.ds(b * 16, 16), pl.ds(0, 512))
    stores[0].start()

    far, near, _ = dn_copies(0)
    far.wait_send()
    pl.when(cross == 1)(near.wait_send)
    for hops in rings:
        for hop in hops:
            hop.wait_send()
    for chunk in range(4):
        g_copy(chunk).wait_send()
    settle(buf_a.at[pl.ds(0, 2 * GROUP - 2)], dd_send)
    settle(buf_b.at[pl.ds(0, 2 * GROUP - 2)], du_send)
    for store in stores:
        store.wait()


def shards(
    activations,
    cotangent,
    token_ids,
    path_table,
    up_master,
    down_master,
    up_momentum,
    down_momentum,
    up_first,
    up_second,
    down_first,
    down_second,
):
    anywhere = pl.BlockSpec(memory_space=pl.ANY)
    smem = pl.BlockSpec(memory_space=pltpu.SMEM)
    vmem = pl.BlockSpec(memory_space=pltpu.VMEM)
    dma = pltpu.SemaphoreType.DMA
    up_mean, down_mean = pl.pallas_call(
        kernel,
        out_shape=[jax.ShapeDtypeStruct(array.shape, F32) for array in (up_master, down_master)],
        in_specs=[smem, vmem] + [anywhere] * 8,
        out_specs=[anywhere] * 2,
        scratch_shapes=[
            pltpu.VMEM((C, 16, HALF_F), F32),
            pltpu.VMEM((C, 64, HALF_D), F32),
            *[pltpu.VMEM((C, 16, HALF_F), BF16)] * 8,
            *[pltpu.VMEM((C, 64, HALF_D), BF16)] * 8,
            pltpu.VMEM((C, 64, HALF_D), BF16),
            pltpu.VMEM((2 * GROUP, 16, HALF_F), BF16),
            pltpu.VMEM((2 * GROUP, 64, HALF_D), BF16),
            pltpu.VMEM((4, 2, 8, 16, HALF_F), BF16),
            pltpu.VMEM((2, GROUP, 64, HALF_D), BF16),
            pltpu.VMEM((2, GROUP, 16, HALF_F), BF16),
            pltpu.VMEM((2, GROUP, 64, HALF_D), BF16),
            pltpu.VMEM((HALF_F, HALF_D), BF16),
            pltpu.VMEM((HALF_F, HALF_D), BF16),
            pltpu.VMEM((HALF_F, HALF_D), BF16),
            pltpu.VMEM((2 * TOK, D), BF16),
            pltpu.VMEM((D, 2 * TOK), BF16),
            pltpu.VMEM((2 * TOK, D), BF16),
            pltpu.VMEM((2, 8, 128), F32),
            pltpu.SMEM((2 * C,), jnp.int32),
            pltpu.VMEM((2 * TOK, HALF_F), BF16),
            pltpu.VMEM((2, 2 * TOK, 256), F32),
            pltpu.VMEM((2, 2 * TOK, 256), BF16),
            pltpu.VMEM((2, 256, 512), F32),
            pltpu.VMEM((2, 2, 1024, 512), BF16),
            pltpu.VMEM((C, 16, HALF_F), BF16),
            pltpu.VMEM((C, 16, HALF_F), BF16),
            pltpu.VMEM((C, 64, HALF_D), BF16),
            pltpu.VMEM((C, 64, HALF_D), BF16),
            pltpu.VMEM((GROUP * 16, C * 16), F32),
            pltpu.VMEM((C * 16, GROUP * 16), BF16),
            pltpu.VMEM((C * 16, GROUP * 16), BF16),
            dma((4,)),
            dma((2, 2)),
            dma((2,)),
            dma((6,)),
            dma((6,)),
            dma((4, 4)),
            dma((4, 4)),
            dma((2,)),
            dma((2,)),
            dma,
            dma,
            dma,
            dma,
            dma((4,)),
            dma((4,)),
            dma,
            dma((2,)),
            dma,
            dma((2,)),
        ],
        compiler_params=pltpu.CompilerParams(
            collective_id=0, has_side_effects=True, vmem_limit_bytes=62 * 1024 * 1024
        ),
        cost_estimate=pl.CostEstimate(flops=12_884_901_888, bytes_accessed=30_000_000, transcendentals=1_572_864),
    )(
        path_table,
        token_ids,
        activations[0],
        cotangent[0],
        up_master,
        down_master,
        up_first[0],
        up_second[0],
        down_first[0],
        down_second[0],
    )
    new_up_momentum = 0.9 * up_momentum + up_mean
    new_down_momentum = 0.9 * down_momentum + down_mean
    new_up_master = up_master - 0.7 * (up_mean + 0.9 * new_up_momentum)
    new_down_master = down_master - 0.7 * (down_mean + 0.9 * new_down_momentum)
    return (new_up_master, new_down_master, new_up_momentum, new_down_momentum)


def solution(mesh):
    placed = (
        P("path", "dp", None),
        P("path", "dp", None),
        P("path", "dp"),
        P(),
        P(None, "path", "dp"),
        P(None, "path", "dp"),
        P(None, "path", "dp"),
        P(None, "path", "dp"),
        P("path", None, "dp"),
        P("path", None, "dp"),
        P("path", None, "dp"),
        P("path", None, "dp"),
    )
    return jax.shard_map(
        shards,
        mesh=mesh,
        in_specs=placed,
        out_specs=(
            P(None, "path", "dp"),
            P(None, "path", "dp"),
            P(None, "path", "dp"),
            P(None, "path", "dp"),
        ),
        check_vma=False,
    )
```

```python
import jax
import jax.numpy as jnp
from jax import lax
from jax.experimental import pallas as pl
from jax.experimental.pallas import tpu as pltpu
from jax.sharding import PartitionSpec as P

D = 1024
F = 4096
C = 8
TOK = 384
HALF_F = F // 2
HALF_D = D // 2
GROUP = 32
MESH = pl.DeviceIdType.MESH
BF16 = jnp.bfloat16
F32 = jnp.float32
NT = (((1,), (1,)), ((), ()))
TN = (((0,), (0,)), ((), ()))
UP_SCALE = D ** (-0.5)
DOWN_SCALE = F ** (-0.5)


def step_direction(gradient, first_moment, second_moment):
    first_new = 0.9 * first_moment.astype(F32) + 0.1 * gradient
    second_new = 0.95 * second_moment.astype(F32) + 0.05 * gradient * gradient
    below = second_new * lax.rsqrt(second_new) + 1e-08
    over = pl.reciprocal(below, approx=True)
    over = over * (2.0 - below * over)
    return (0.1 * first_new * over).astype(BF16)


def kernel(
    table, ids, act_in, cot_in, um_in, dm_in, up_first, up_second, down_first, down_second, um_out, dm_out,
    um, dm, up_x0, up_x1, up_x2, up_x3, up_z0, up_z1, up_z2, up_z3,
    dn_x0, dn_x1, dn_x2, dn_x3, dn_z0, dn_z1, dn_z2, dn_z3, dnb, buf_a, buf_b, wup, wdn, rdn, rup,
    gsend, gmine, grecv, nrm, nrm_t, og, count, used, gp, wide_a, act_a, wide_b, mom,
    pdn_send, pdn_recv, pup_send, pup_recv, pick_t, pick_up, pick_dn,
    in_sem, mom_sem, out_sem, y_send, y_recv, ring_send, ring_recv, dn_send, blk_recv, wu_send, wu_recv, wd_send, wd_recv,
    g_send, g_recv, dd_send, dd_recv, du_send, du_recv,
):
    path = lax.axis_index("path")
    here = lax.axis_index("dp")
    x = lax.div(path, 16)
    yl = lax.rem(lax.div(path, 8), 2)
    zc = lax.rem(path, 8)
    z = lax.div(zc, 2)
    core = lax.rem(zc, 2)
    group = x * 8 + zc
    other_yl = 1 - yl
    there = 1 - here

    def place(x_, yl_, zc_):
        return x_ * 16 + yl_ * 8 + zc_

    def zc_at(k):
        return lax.rem(z + lax.rem(lax.div(k, 2), 4), 4) * 2 + lax.rem(core + k, 2)

    def peer(k):
        return lax.rem(x + lax.div(k, 8), 4), zc_at(k)

    def remote(src, dst, send, recv, to_path, to_dp):
        return pltpu.make_async_remote_copy(
            src_ref=src, dst_ref=dst, send_sem=send, recv_sem=recv,
            device_id=(to_path, to_dp), device_id_type=MESH,
        )

    def settle(ref, sem):
        pltpu.make_async_copy(ref, ref, sem).wait()

    own_rows = pl.ds(pl.multiple_of(here * TOK, TOK), TOK)
    loads = [
        pltpu.make_async_copy(src, dst, in_sem.at[i])
        for i, (src, dst) in enumerate(
            [(um_in, um), (act_in, nrm.at[own_rows]), (dm_in, dm), (cot_in, og.at[own_rows])]
        )
    ]
    for load in loads:
        load.start()

    down_x = [half * 2 + lax.rem(x + i, 2) for half in (here, there) for i in range(2)]
    up_block = [lax.rem(x + (2 + 3 * i) % 4, 4) for i in range(4)]

    order = (0, 1, 4, 5, 2, 6, 7, 3)

    def fetch(turn_no):
        if turn_no >= 8:
            return
        slot = turn_no % 3
        step = order[turn_no]
        for kind, (down_source, up_source) in enumerate(((down_first, up_first), (down_second, up_second))):
            if step < 4:
                rows = pl.ds(pl.multiple_of(down_x[step] * 1024, 1024), 1024)
                pltpu.make_async_copy(
                    down_source.at[rows], mom.at[slot, kind], mom_sem.at[slot, kind]
                ).start()
            else:
                rows = pl.ds(pl.multiple_of(up_block[step - 4] * 256, 256), 256)
                for b in range(4):
                    pltpu.make_async_copy(
                        up_source.at[rows, pl.ds(b * 512, 512)],
                        mom.at[slot, kind, pl.ds(b * 256, 256)],
                        mom_sem.at[slot, kind],
                    ).start()

    def await_moments(slot):
        for kind in range(2):
            settle(mom.at[slot, kind], mom_sem.at[slot, kind])

    for turn_no in range(3):
        fetch(turn_no)

    cross = lax.rem(lax.div(x, 2) + here, 2)
    barrier = pltpu.get_barrier_semaphore()

    def greet(k, _):
        x_, zc_ = peer(k)
        pl.semaphore_signal(barrier, inc=1, device_id=(place(x_, yl, zc_), here), device_id_type=MESH)
        return 0

    lax.fori_loop(1, GROUP, greet, 0)
    for to_path, to_dp in (
        (place(x, other_yl, zc), here),
        (path, there),
        (place(3 - x, yl, zc), there),
        (place(3 - x, other_yl, zc), there),
    ):
        pl.semaphore_signal(barrier, inc=1, device_id=(to_path, to_dp), device_id_type=MESH)

    loads[1].wait()
    for part in range(3):
        rows = pl.ds(pl.multiple_of(here * TOK + part * 128, 128), 128)
        wide = nrm[rows, :].astype(F32)
        mean_square = jnp.mean(wide * wide, axis=-1, keepdims=True)
        nrm[rows, :] = (wide * lax.rsqrt(mean_square + 1e-06)).astype(BF16)
    loads[0].wait()
    up_x0[...] = um[...].astype(BF16)
    loads[3].wait()
    live = jnp.sum((ids[...] != 0).astype(F32))
    for part in range(3):
        rows = pl.ds(pl.multiple_of(here * TOK + part * 128, 128), 128)
        position = (lax.broadcasted_iota(jnp.int32, (128, D), 0) + part * 128).astype(F32)
        og[rows, :] = jnp.where(position < live, og[rows, :].astype(F32), 0.0).astype(BF16)
    count[0] = jnp.broadcast_to(live, (8, 128))
    loads[2].wait()
    dnb[...] = dm[...].astype(BF16)

    def ring(row, blocks, minus, plus):
        own, from_minus, from_plus, opposite = blocks
        halves = pl.ds(0, C // 2), pl.ds(C // 2, C // 2)
        hops = [
            (own, from_minus, plus),
            (own, from_plus, minus),
            (from_minus.at[halves[0]], opposite.at[halves[0]], plus),
            (from_plus.at[halves[1]], opposite.at[halves[1]], minus),
        ]
        return [
            remote(src, dst, ring_send.at[row, n], ring_recv.at[row, n], to, here)
            for n, (src, dst, to) in enumerate(hops)
        ]

    x_minus, x_plus = place(lax.rem(x + 3, 4), yl, zc), place(lax.rem(x + 1, 4), yl, zc)
    z_minus = place(x, yl, lax.rem(z + 3, 4) * 2 + core)
    z_plus = place(x, yl, lax.rem(z + 1, 4) * 2 + core)
    up_x, up_z = (up_x0, up_x1, up_x2, up_x3), (up_z0, up_z1, up_z2, up_z3)
    dn_x, dn_z = (dn_x0, dn_x1, dn_x2, dn_x3), (dn_z0, dn_z1, dn_z2, dn_z3)
    rings = [
        ring(0, up_x, x_minus, x_plus),
        ring(1, up_z, z_minus, z_plus),
        ring(2, dn_x, x_minus, x_plus),
        ring(3, dn_z, z_minus, z_plus),
    ]
    shift = (0, 3, 1, 2)

    def along_z(k):
        return x, zc_at(k)

    def along_x(k):
        return lax.rem(x + lax.div(k, 2), 4), z * 2 + lax.rem(core + k, 2)

    def pick_and_send(level, blocks, part, first_slot, peers, buf, landing, send, recv):
        def make(k):
            x_, zc_ = peers(k)
            slot = first_slot + part * 8 + k
            buf[slot] = blocks[part][table[place(x_, yl, zc_), level]]
            return buf.at[slot], place(x_, yl, zc_)

        source, _ = make(0)
        pltpu.make_async_copy(source, landing, recv).start()

        def one(k, _):
            source, to_path = make(k)
            remote(source, landing, send, recv, to_path, here).start()
            return 0

        lax.fori_loop(1, 8, one, 0)

    def up_picks_x(part):
        from_x = lax.rem(x + shift[part], 4)
        pick_and_send(0, up_x, part, 0, along_z, buf_a, wup.at[from_x, yl, zc], wu_send, wu_recv)

    def up_picks_z(part):
        from_zc = lax.rem(z + shift[part], 4) * 2 + core
        pick_and_send(0, up_z, part, GROUP, along_x, buf_a, wup.at[x, other_yl, from_zc], wu_send, wu_recv)

    def dn_landing(x_, side, zc_):
        crossed = lax.rem(lax.div(x_, 2) + here, 2)
        owner_x = x_ + crossed * (3 - 2 * x_)
        owner_dp = here + crossed * (1 - 2 * here)
        return wdn.at[owner_dp, (owner_x - 2 * here) * 16 + side * 8 + zc_]

    def dn_picks_x(part):
        landing = dn_landing(lax.rem(x + shift[part], 4), 0, zc)
        pick_and_send(1, dn_x, part, 0, along_z, buf_b, landing, wd_send, wd_recv)

    def dn_picks_z(part):
        landing = dn_landing(x, 1, lax.rem(z + shift[part], 4) * 2 + core)
        pick_and_send(1, dn_z, part, GROUP, along_x, buf_b, landing, wd_send, wd_recv)

    pl.semaphore_wait(barrier, GROUP + 3)
    up_swap = remote(up_x0, up_z0, y_send.at[0], y_recv.at[0], place(x, other_yl, zc), here)
    up_swap.start()
    count_swap = remote(count.at[0], count.at[1], y_send.at[3], y_recv.at[3], path, there)
    count_swap.start()
    x_to = x + cross * (3 - 2 * x)
    dp_to = here + cross * (1 - 2 * here)

    def dn_copies(side):
        own = (dn_x0, dn_z0)[side]
        far = remote(dnb, own, dn_send.at[0], blk_recv.at[side], place(x_to, other_yl, zc), dp_to)
        near = remote(dnb, own, dn_send.at[1], blk_recv.at[side], place(3 - x, yl, zc), there)
        return far, near, pltpu.make_async_copy(dnb, own, blk_recv.at[side])

    for side in range(2):

        @pl.when(yl == side)
        def _(side=side):
            far, near, local = dn_copies(side)
            far.start()
            pl.when(cross == 1)(near.start)
            pl.when(cross == 0)(local.start)

    nrm_swap = remote(nrm.at[own_rows], nrm.at[own_rows], y_send.at[1], y_recv.at[1], path, there)
    nrm_swap.start()
    og_swap = remote(og.at[own_rows], og.at[own_rows], y_send.at[2], y_recv.at[2], path, there)
    og_swap.start()

    def pass_on(row):
        for n in range(2):
            rings[row][n].wait_recv()
            rings[row][n + 2].start()

    def await_opposite(row):
        for n in range(2, 4):
            rings[row][n].wait_recv()

    rings[0][0].start()
    rings[0][1].start()
    up_picks_x(0)
    pass_on(0)
    up_picks_x(1)
    up_picks_x(2)
    up_swap.wait()
    rings[1][0].start()
    rings[1][1].start()
    up_picks_z(0)
    await_opposite(0)
    up_picks_x(3)
    pass_on(1)
    up_picks_z(1)
    up_picks_z(2)
    await_opposite(1)
    up_picks_z(3)
    for side in range(2):
        dn_copies(side)[0].wait_recv()
        rings[2 + side][0].start()
        rings[2 + side][1].start()
    dn_picks_x(0)
    dn_picks_z(0)
    pass_on(2)
    pass_on(3)
    dn_picks_x(1)
    dn_picks_z(1)
    dn_picks_x(2)
    dn_picks_z(2)
    await_opposite(2)
    dn_picks_x(3)
    await_opposite(3)
    dn_picks_z(3)

    lane = lax.broadcasted_iota(jnp.int32, (16, C * 16), 1)
    same_row = (lane & 15) == lax.broadcasted_iota(jnp.int32, (16, C * 16), 0)
    for level, pick in enumerate((pick_up, pick_dn)):

        def fill(k, _, level=level):
            module = table[lax.div(k, 8) * 16 + yl * 8 + lax.rem(k, 8), level]
            rows = pl.ds(pl.multiple_of(k * 16, 16), 16)
            pick_t[rows, :] = jnp.where(same_row & ((lane >> 4) == module), 1.0, 0.0)
            return 0

        lax.fori_loop(0, GROUP, fill, 0)
        pick[...] = pick_t[...].T.astype(BF16)

        def tally(k, counts, level=level):
            module = table[k, level]
            return tuple(n + jnp.where(module == m, 1, 0) for m, n in enumerate(counts))

        counts = lax.fori_loop(0, 64, tally, (jnp.int32(0),) * C)
        for m in range(C):
            used[level * C + m] = counts[m]

    nrm_swap.wait()

    def turn(i, _):
        cols = pl.ds(pl.multiple_of(i * 256, 256), 256)
        nrm_t[cols, :] = nrm[:, cols].T
        return 0

    lax.fori_loop(0, 4, turn, 0)
    count_swap.wait()
    per_count = 1.0 / (count[0] + count[1])
    per_count = per_count[0:1, 0:1]
    og_swap.wait()

    def scale_rows(i, _):
        rows = pl.ds(pl.multiple_of(i * 64, 64), 64)
        og[rows, :] = (og[rows, :].astype(F32) * per_count).astype(BF16)
        return 0

    lax.fori_loop(0, 12, scale_rows, 0)

    settle(wup, wu_recv)
    mine_cols = pl.ds(pl.multiple_of(here * HALF_D, HALF_D), HALF_D)
    their_cols = pl.ds(pl.multiple_of(there * HALF_D, HALF_D), HALF_D)

    def g_copy(chunk):
        rows = pl.ds(pl.multiple_of(chunk * 512, 512), 512)
        return remote(gsend.at[rows], grecv.at[rows], g_send.at[chunk], g_recv.at[chunk], path, there)

    def pre_act(i, half):
        cols = pl.ds(pl.multiple_of(i * 256, 256), 256)
        weights = wup[:, :, :, :, cols].reshape(D, 256)
        wide_a[half] = jnp.dot(nrm[...], weights, preferred_element_type=F32)

    first_tile = 4 * lax.rem(x, 2)
    pre_act(first_tile, 0)

    def hidden(pair, _):
        for half in range(2):
            i = lax.rem(first_tile + pair * 2 + half, 8)
            pre_act(lax.rem(i + 1, 8), 1 - half)
            cols = pl.ds(pl.multiple_of(i * 256, 256), 256)
            for strip in range(24):
                rows = pl.ds(strip * 32, 32)
                pre = wide_a[half, rows, :] * UP_SCALE
                sig = 0.5 * jnp.tanh(0.5 * pre) + 0.5
                out = pre * sig
                act_a[half, rows, :] = out.astype(BF16)
                gp[rows, cols] = (sig + out * (1.0 - sig)).astype(BF16)
            out_t = act_a[half].T
            theirs = jnp.dot(out_t, og[:, their_cols], preferred_element_type=F32)
            gsend[cols, :] = (theirs * DOWN_SCALE).astype(BF16)
            if half == 1:
                g_copy(lax.div(i, 2)).start()
            mine = jnp.dot(out_t, og[:, mine_cols], preferred_element_type=F32)
            gmine[cols, :] = (mine * DOWN_SCALE).astype(BF16)
        return 0

    lax.fori_loop(0, 4, hidden, 0)

    def down_delta(turn_no):
        step = order[turn_no]
        x_ = down_x[step]
        source = gmine if step < 2 else grecv
        first_row = lax.rem(x_, 2) * 1024
        if step >= 2:
            for half in range(2):
                g_copy(lax.rem(x_, 2) * 2 + half).wait_recv()
        slot = turn_no % 3
        await_moments(slot)

        def one(q, _):
            for b in range(4):
                rows = pl.ds(pl.multiple_of(q * 64 + b * 16, 16), 16)
                grad = source[pl.ds(pl.multiple_of(first_row + q * 64 + b * 16, 16), 16), :].astype(F32)
                delta = step_direction(grad, mom[slot, 0, rows, :], mom[slot, 1, rows, :])
                buf_a[x_ * 16 + q, :, pl.ds(b * 512, 512)] = delta
            return 0

        lax.fori_loop(0, 16, one, 0)
        fetch(turn_no + 3)

    def send_down_delta(step, side):
        x_ = down_x[step]

        def send(k, _):
            zc_ = zc_at(k)
            row = x_ * 16 + side * 8 + zc_
            away = (x_ * 8 + zc_) != group

            @pl.when(away)
            def _():
                remote(
                    buf_a.at[row], rdn.at[side, group], dd_send, dd_recv.at[side], place(x_, yl, zc_), here
                ).start()

            @pl.when(jnp.logical_not(away))
            def _():
                pltpu.make_async_copy(buf_a.at[row], rdn.at[side, group], dd_recv.at[side]).start()

            return 0

        lax.fori_loop(0, 8, send, 0)

    settle(buf_a.at[pl.ds(0, 2 * GROUP - 8)], wu_send)
    down_delta(0)
    send_down_delta(0, other_yl)
    send_down_delta(0, yl)
    down_delta(1)

    settle(wdn, wd_recv)

    def hidden_grad(i, _):
        cols = pl.ds(pl.multiple_of(i * 256, 256), 256)
        low = wdn[0, pl.ds(i * 4, 4)].reshape(256, HALF_D)
        high = wdn[1, pl.ds(i * 4, 4)].reshape(256, HALF_D)
        grad = lax.dot_general(og[:, pl.ds(0, HALF_D)], low, NT, preferred_element_type=F32)
        grad += lax.dot_general(og[:, pl.ds(HALF_D, HALF_D)], high, NT, preferred_element_type=F32)
        gp[:, cols] = (grad * DOWN_SCALE * gp[:, cols].astype(F32)).astype(BF16)
        return 0

    lax.fori_loop(0, 8, hidden_grad, 0)
    settle(buf_b.at[pl.ds(0, 2 * GROUP - 8)], wd_send)

    def send_up_delta(x_, zc_, side):
        row = x_ * 16 + side * 8 + zc_
        away = (x_ * 8 + zc_) != group

        @pl.when(away)
        def _():
            remote(
                buf_b.at[row], rup.at[side, group], du_send, du_recv.at[side], place(x_, yl, zc_), here
            ).start()

        @pl.when(jnp.logical_not(away))
        def _():
            pltpu.make_async_copy(buf_b.at[row], rup.at[side, group], du_recv.at[side]).start()

    def up_step(step, even):
        x_ = lax.rem(x + lax.rem(2 + 3 * step, 4), 4)
        slot = lax.rem(2 + even, 3)
        lhs = nrm_t[pl.ds(pl.multiple_of(x_ * 256, 256), 256), :]
        await_moments(slot)

        def up_grad(b, half):
            cols = pl.ds(pl.multiple_of(b * 512, 512), 512)
            wide_b[half] = jnp.dot(lhs, gp[:, cols], preferred_element_type=F32)

        def strips(b, half):
            for i in range(16):
                rows = pl.ds(pl.multiple_of(b * 256 + i * 16, 16), 16)
                grad = wide_b[half, pl.ds(i * 16, 16), :] * UP_SCALE
                delta = step_direction(grad, mom[slot, 0, rows, :], mom[slot, 1, rows, :])
                buf_b[x_ * 16 + i, pl.ds(pl.multiple_of(b * 16, 16), 16), :] = delta

        up_grad(0, 0)

        def pair(n, _):
            up_grad(2 * n + 1, 1)
            strips(2 * n, 0)
            up_grad(lax.rem(2 * n + 2, 4), 0)
            strips(2 * n + 1, 1)
            return 0

        lax.fori_loop(0, 2, pair, 0)

        def send(k, _):
            send_up_delta(x_, zc_at(k), lax.rem(other_yl + lax.div(k, 8), 2))
            return 0

        lax.fori_loop(0, 16, send, 0)

    def early(n, _):
        up_step(n, n)
        pl.when(n == 0)(lambda: fetch(5))
        pl.when(n == 1)(lambda: fetch(6))
        return 0

    def late(n, _):
        up_step(n + 2, n)
        return 0

    lax.fori_loop(0, 2, early, 0)
    down_delta(4)
    send_down_delta(2, other_yl)
    send_down_delta(2, yl)
    lax.fori_loop(0, 2, late, 0)
    down_delta(7)
    for side in (other_yl, yl):
        send_down_delta(1, side)
        send_down_delta(3, side)

    def wide_cols(b):
        return pl.ds(pl.multiple_of(b * 512, 512), 512)

    def row_block(b):
        return pl.ds(pl.multiple_of(b * 16, 16), 16)

    def down_sum(side, b):
        block = rdn[side, :, :, wide_cols(b)].reshape(GROUP * 16, 512)
        return jnp.dot(pick_dn[...], block, preferred_element_type=F32).reshape(C, 16, 512)

    def up_sum(side, b):
        block = rup[side, :, row_block(b), :].reshape(GROUP * 16, 512)
        return jnp.dot(pick_up[...], block, preferred_element_type=F32).reshape(C, 16, 512)

    def four(body):
        def one(b, _):
            body(b)
            return 0

        lax.fori_loop(0, 4, one, 0)

    def finish(total, master, level, rows, cols):
        for m in range(C):
            number = jnp.broadcast_to(used[level * C + m].astype(F32), (8, 128))
            per_used = (1.0 / jnp.maximum(number, 1.0))[0:1, 0:1]
            decay = (0.01 * jnp.minimum(number, 1.0))[0:1, 0:1]
            weights = master[m, rows, cols].astype(BF16).astype(F32)
            master[m, rows, cols] = total[m] * per_used + decay * weights

    mate = place(x, other_yl, zc)
    stores = [
        pltpu.make_async_copy(src, dst, out_sem.at[i]) for i, (src, dst) in enumerate([(dm, dm_out), (um, um_out)])
    ]
    settle(rup.at[other_yl], du_recv.at[other_yl])

    @four
    def _(b):
        pup_send[:, row_block(b), :] = up_sum(other_yl, b).astype(BF16)

    up_part = remote(pup_send, pup_recv, y_send.at[5], y_recv.at[5], mate, here)
    up_part.start()
    settle(rup.at[yl], du_recv.at[yl])
    up_part.wait()

    @four
    def _(b):
        total = up_sum(yl, b) + pup_recv[:, row_block(b), :].astype(F32)
        finish(total, um, 0, pl.ds(0, 16), wide_cols(b))

    stores[1].start()

    settle(rdn.at[other_yl], dd_recv.at[other_yl])

    @four
    def _(b):
        pdn_send[:, :, wide_cols(b)] = down_sum(other_yl, b).astype(BF16)

    dn_part = remote(pdn_send, pdn_recv, y_send.at[4], y_recv.at[4], mate, here)
    dn_part.start()
    settle(rdn.at[yl], dd_recv.at[yl])
    dn_part.wait()

    @four
    def _(b):
        total = down_sum(yl, b) + pdn_recv[:, :, wide_cols(b)].astype(F32)
        finish(total, dm, 1, row_block(b), pl.ds(0, 512))

    stores[0].start()

    far, near, _ = dn_copies(0)
    far.wait_send()
    pl.when(cross == 1)(near.wait_send)
    for hops in rings:
        for hop in hops:
            hop.wait_send()
    for chunk in range(4):
        g_copy(chunk).wait_send()
    settle(buf_a.at[pl.ds(0, 2 * GROUP - 2)], dd_send)
    settle(buf_b.at[pl.ds(0, 2 * GROUP - 2)], du_send)
    for store in stores:
        store.wait()


def shards(
    activations,
    cotangent,
    token_ids,
    path_table,
    up_master,
    down_master,
    up_momentum,
    down_momentum,
    up_first,
    up_second,
    down_first,
    down_second,
):
    anywhere = pl.BlockSpec(memory_space=pl.ANY)
    smem = pl.BlockSpec(memory_space=pltpu.SMEM)
    vmem = pl.BlockSpec(memory_space=pltpu.VMEM)
    dma = pltpu.SemaphoreType.DMA
    up_mean, down_mean = pl.pallas_call(
        kernel,
        out_shape=[jax.ShapeDtypeStruct(array.shape, F32) for array in (up_master, down_master)],
        in_specs=[smem, vmem] + [anywhere] * 8,
        out_specs=[anywhere] * 2,
        scratch_shapes=[
            pltpu.VMEM((C, 16, HALF_F), F32),
            pltpu.VMEM((C, 64, HALF_D), F32),
            *[pltpu.VMEM((C, 16, HALF_F), BF16)] * 8,
            *[pltpu.VMEM((C, 64, HALF_D), BF16)] * 8,
            pltpu.VMEM((C, 64, HALF_D), BF16),
            pltpu.VMEM((2 * GROUP, 16, HALF_F), BF16),
            pltpu.VMEM((2 * GROUP, 64, HALF_D), BF16),
            pltpu.VMEM((4, 2, 8, 16, HALF_F), BF16),
            pltpu.VMEM((2, GROUP, 64, HALF_D), BF16),
            pltpu.VMEM((2, GROUP, 16, HALF_F), BF16),
            pltpu.VMEM((2, GROUP, 64, HALF_D), BF16),
            pltpu.VMEM((HALF_F, HALF_D), BF16),
            pltpu.VMEM((HALF_F, HALF_D), BF16),
            pltpu.VMEM((HALF_F, HALF_D), BF16),
            pltpu.VMEM((2 * TOK, D), BF16),
            pltpu.VMEM((D, 2 * TOK), BF16),
            pltpu.VMEM((2 * TOK, D), BF16),
            pltpu.VMEM((2, 8, 128), F32),
            pltpu.SMEM((2 * C,), jnp.int32),
            pltpu.VMEM((2 * TOK, HALF_F), BF16),
            pltpu.VMEM((2, 2 * TOK, 256), F32),
            pltpu.VMEM((2, 2 * TOK, 256), BF16),
            pltpu.VMEM((2, 256, 512), F32),
            pltpu.VMEM((3, 2, 1024, 512), BF16),
            pltpu.VMEM((C, 16, HALF_F), BF16),
            pltpu.VMEM((C, 16, HALF_F), BF16),
            pltpu.VMEM((C, 64, HALF_D), BF16),
            pltpu.VMEM((C, 64, HALF_D), BF16),
            pltpu.VMEM((GROUP * 16, C * 16), F32),
            pltpu.VMEM((C * 16, GROUP * 16), BF16),
            pltpu.VMEM((C * 16, GROUP * 16), BF16),
            dma((4,)),
            dma((3, 2)),
            dma((2,)),
            dma((6,)),
            dma((6,)),
            dma((4, 4)),
            dma((4, 4)),
            dma((2,)),
            dma((2,)),
            dma,
            dma,
            dma,
            dma,
            dma((4,)),
            dma((4,)),
            dma,
            dma((2,)),
            dma,
            dma((2,)),
        ],
        compiler_params=pltpu.CompilerParams(
            collective_id=0, has_side_effects=True, vmem_limit_bytes=62 * 1024 * 1024
        ),
        cost_estimate=pl.CostEstimate(flops=12_884_901_888, bytes_accessed=30_000_000, transcendentals=1_572_864),
    )(
        path_table,
        token_ids,
        activations[0],
        cotangent[0],
        up_master,
        down_master,
        up_first[0],
        up_second[0],
        down_first[0],
        down_second[0],
    )
    new_up_momentum = 0.9 * up_momentum + up_mean
    new_down_momentum = 0.9 * down_momentum + down_mean
    new_up_master = up_master - 0.7 * (up_mean + 0.9 * new_up_momentum)
    new_down_master = down_master - 0.7 * (down_mean + 0.9 * new_down_momentum)
    return (new_up_master, new_down_master, new_up_momentum, new_down_momentum)


def solution(mesh):
    placed = (
        P("path", "dp", None),
        P("path", "dp", None),
        P("path", "dp"),
        P(),
        P(None, "path", "dp"),
        P(None, "path", "dp"),
        P(None, "path", "dp"),
        P(None, "path", "dp"),
        P("path", None, "dp"),
        P("path", None, "dp"),
        P("path", None, "dp"),
        P("path", None, "dp"),
    )
    return jax.shard_map(
        shards,
        mesh=mesh,
        in_specs=placed,
        out_specs=(
            P(None, "path", "dp"),
            P(None, "path", "dp"),
            P(None, "path", "dp"),
            P(None, "path", "dp"),
        ),
        check_vma=False,
    )
```

```python
import jax
import jax.numpy as jnp
from jax import lax
from jax.experimental import pallas as pl
from jax.experimental.pallas import tpu as pltpu
from jax.sharding import PartitionSpec as P

D = 1024
F = 4096
C = 8
TOK = 384
HALF_F = F // 2
HALF_D = D // 2
GROUP = 32
MESH = pl.DeviceIdType.MESH
BF16 = jnp.bfloat16
F32 = jnp.float32
NT = (((1,), (1,)), ((), ()))
TN = (((0,), (0,)), ((), ()))
UP_SCALE = D ** (-0.5)
DOWN_SCALE = F ** (-0.5)


def step_direction(gradient, first_moment, second_moment):
    first_new = 0.9 * first_moment.astype(F32) + 0.1 * gradient
    second_new = 0.95 * second_moment.astype(F32) + 0.05 * gradient * gradient
    below = second_new * lax.rsqrt(second_new) + 1e-08
    over = pl.reciprocal(below, approx=True)
    over = over * (2.0 - below * over)
    return (0.1 * first_new * over).astype(BF16)


def kernel(
    table, ids, act_in, cot_in, um_in, dm_in, up_first, up_second, down_first, down_second, um_out, dm_out,
    um, dm, up_x0, up_x1, up_x2, up_x3, up_z0, up_z1, up_z2, up_z3,
    dn_x0, dn_x1, dn_x2, dn_x3, dn_z0, dn_z1, dn_z2, dn_z3, dnb, buf_a, buf_b, wup, wdn, rdn, rup,
    gsend, gmine, grecv, nrm, nrm_t, og, count, used, gp, wide_a, act_a, wide_b, mom,
    pdn_send, pdn_recv, pup_send, pup_recv, pick_t, pick_up, pick_dn,
    in_sem, mom_sem, out_sem, y_send, y_recv, ring_send, ring_recv, dn_send, blk_recv, wu_send, wu_recv, wd_send, wd_recv,
    g_send, g_recv, dd_send, dd_recv, du_send, du_recv,
):
    path = lax.axis_index("path")
    here = lax.axis_index("dp")
    x = lax.div(path, 16)
    yl = lax.rem(lax.div(path, 8), 2)
    zc = lax.rem(path, 8)
    z = lax.div(zc, 2)
    core = lax.rem(zc, 2)
    group = x * 8 + zc
    other_yl = 1 - yl
    there = 1 - here

    def place(x_, yl_, zc_):
        return x_ * 16 + yl_ * 8 + zc_

    def zc_at(k):
        return lax.rem(z + lax.rem(lax.div(k, 2), 4), 4) * 2 + lax.rem(core + k, 2)

    def peer(k):
        return lax.rem(x + lax.div(k, 8), 4), zc_at(k)

    def remote(src, dst, send, recv, to_path, to_dp):
        return pltpu.make_async_remote_copy(
            src_ref=src, dst_ref=dst, send_sem=send, recv_sem=recv,
            device_id=(to_path, to_dp), device_id_type=MESH,
        )

    def settle(ref, sem):
        pltpu.make_async_copy(ref, ref, sem).wait()

    own_rows = pl.ds(pl.multiple_of(here * TOK, TOK), TOK)
    loads = [
        pltpu.make_async_copy(src, dst, in_sem.at[i])
        for i, (src, dst) in enumerate(
            [(um_in, um), (act_in, nrm.at[own_rows]), (dm_in, dm), (cot_in, og.at[own_rows])]
        )
    ]
    for load in loads:
        load.start()

    down_x = [half * 2 + lax.rem(x + i, 2) for half in (here, there) for i in range(2)]
    up_block = [lax.rem(x + (2 + 3 * i) % 4, 4) for i in range(4)]

    order = (0, 1, 4, 5, 2, 6, 7, 3)

    def fetch(turn_no):
        if turn_no >= 8:
            return
        slot = turn_no % 3
        step = order[turn_no]
        for kind, (down_source, up_source) in enumerate(((down_first, up_first), (down_second, up_second))):
            if step < 4:
                rows = pl.ds(pl.multiple_of(down_x[step] * 1024, 1024), 1024)
                pltpu.make_async_copy(
                    down_source.at[rows], mom.at[slot, kind], mom_sem.at[slot, kind]
                ).start()
            else:
                rows = pl.ds(pl.multiple_of(up_block[step - 4] * 256, 256), 256)
                for b in range(4):
                    pltpu.make_async_copy(
                        up_source.at[rows, pl.ds(b * 512, 512)],
                        mom.at[slot, kind, pl.ds(b * 256, 256)],
                        mom_sem.at[slot, kind],
                    ).start()

    def await_moments(slot):
        for kind in range(2):
            settle(mom.at[slot, kind], mom_sem.at[slot, kind])


    cross = lax.rem(lax.div(x, 2) + here, 2)
    barrier = pltpu.get_barrier_semaphore()

    def greet(k, _):
        x_, zc_ = peer(k)
        pl.semaphore_signal(barrier, inc=1, device_id=(place(x_, yl, zc_), here), device_id_type=MESH)
        return 0

    lax.fori_loop(1, GROUP, greet, 0)
    for to_path, to_dp in (
        (place(x, other_yl, zc), here),
        (path, there),
        (place(3 - x, yl, zc), there),
        (place(3 - x, other_yl, zc), there),
    ):
        pl.semaphore_signal(barrier, inc=1, device_id=(to_path, to_dp), device_id_type=MESH)

    loads[1].wait()
    for part in range(3):
        rows = pl.ds(pl.multiple_of(here * TOK + part * 128, 128), 128)
        wide = nrm[rows, :].astype(F32)
        mean_square = jnp.mean(wide * wide, axis=-1, keepdims=True)
        nrm[rows, :] = (wide * lax.rsqrt(mean_square + 1e-06)).astype(BF16)
    loads[0].wait()
    up_x0[...] = um[...].astype(BF16)
    loads[3].wait()
    live = jnp.sum((ids[...] != 0).astype(F32))
    for part in range(3):
        rows = pl.ds(pl.multiple_of(here * TOK + part * 128, 128), 128)
        position = (lax.broadcasted_iota(jnp.int32, (128, D), 0) + part * 128).astype(F32)
        og[rows, :] = jnp.where(position < live, og[rows, :].astype(F32), 0.0).astype(BF16)
    count[0] = jnp.broadcast_to(live, (8, 128))
    loads[2].wait()
    dnb[...] = dm[...].astype(BF16)

    def ring(row, blocks, minus, plus):
        own, from_minus, from_plus, opposite = blocks
        halves = pl.ds(0, C // 2), pl.ds(C // 2, C // 2)
        hops = [
            (own, from_minus, plus),
            (own, from_plus, minus),
            (from_minus.at[halves[0]], opposite.at[halves[0]], plus),
            (from_plus.at[halves[1]], opposite.at[halves[1]], minus),
        ]
        return [
            remote(src, dst, ring_send.at[row, n], ring_recv.at[row, n], to, here)
            for n, (src, dst, to) in enumerate(hops)
        ]

    x_minus, x_plus = place(lax.rem(x + 3, 4), yl, zc), place(lax.rem(x + 1, 4), yl, zc)
    z_minus = place(x, yl, lax.rem(z + 3, 4) * 2 + core)
    z_plus = place(x, yl, lax.rem(z + 1, 4) * 2 + core)
    up_x, up_z = (up_x0, up_x1, up_x2, up_x3), (up_z0, up_z1, up_z2, up_z3)
    dn_x, dn_z = (dn_x0, dn_x1, dn_x2, dn_x3), (dn_z0, dn_z1, dn_z2, dn_z3)
    rings = [
        ring(0, up_x, x_minus, x_plus),
        ring(1, up_z, z_minus, z_plus),
        ring(2, dn_x, x_minus, x_plus),
        ring(3, dn_z, z_minus, z_plus),
    ]
    shift = (0, 3, 1, 2)

    def along_z(k):
        return x, zc_at(k)

    def along_x(k):
        return lax.rem(x + lax.div(k, 2), 4), z * 2 + lax.rem(core + k, 2)

    def pick_and_send(level, blocks, part, first_slot, peers, buf, landing, send, recv):
        def make(k):
            x_, zc_ = peers(k)
            slot = first_slot + part * 8 + k
            buf[slot] = blocks[part][table[place(x_, yl, zc_), level]]
            return buf.at[slot], place(x_, yl, zc_)

        source, _ = make(0)
        pltpu.make_async_copy(source, landing, recv).start()

        def one(k, _):
            source, to_path = make(k)
            remote(source, landing, send, recv, to_path, here).start()
            return 0

        lax.fori_loop(1, 8, one, 0)

    def up_picks_x(part):
        from_x = lax.rem(x + shift[part], 4)
        pick_and_send(0, up_x, part, 0, along_z, buf_a, wup.at[from_x, yl, zc], wu_send, wu_recv)

    def up_picks_z(part):
        from_zc = lax.rem(z + shift[part], 4) * 2 + core
        pick_and_send(0, up_z, part, GROUP, along_x, buf_a, wup.at[x, other_yl, from_zc], wu_send, wu_recv)

    def dn_landing(x_, side, zc_):
        crossed = lax.rem(lax.div(x_, 2) + here, 2)
        owner_x = x_ + crossed * (3 - 2 * x_)
        owner_dp = here + crossed * (1 - 2 * here)
        return wdn.at[owner_dp, (owner_x - 2 * here) * 16 + side * 8 + zc_]

    def dn_picks_x(part):
        landing = dn_landing(lax.rem(x + shift[part], 4), 0, zc)
        pick_and_send(1, dn_x, part, 0, along_z, buf_b, landing, wd_send, wd_recv)

    def dn_picks_z(part):
        landing = dn_landing(x, 1, lax.rem(z + shift[part], 4) * 2 + core)
        pick_and_send(1, dn_z, part, GROUP, along_x, buf_b, landing, wd_send, wd_recv)

    pl.semaphore_wait(barrier, GROUP + 3)
    up_swap = remote(up_x0, up_z0, y_send.at[0], y_recv.at[0], place(x, other_yl, zc), here)
    up_swap.start()
    count_swap = remote(count.at[0], count.at[1], y_send.at[3], y_recv.at[3], path, there)
    count_swap.start()
    x_to = x + cross * (3 - 2 * x)
    dp_to = here + cross * (1 - 2 * here)

    def dn_copies(side):
        own = (dn_x0, dn_z0)[side]
        far = remote(dnb, own, dn_send.at[0], blk_recv.at[side], place(x_to, other_yl, zc), dp_to)
        near = remote(dnb, own, dn_send.at[1], blk_recv.at[side], place(3 - x, yl, zc), there)
        return far, near, pltpu.make_async_copy(dnb, own, blk_recv.at[side])

    for side in range(2):

        @pl.when(yl == side)
        def _(side=side):
            far, near, local = dn_copies(side)
            far.start()
            pl.when(cross == 1)(near.start)
            pl.when(cross == 0)(local.start)

    nrm_swap = remote(nrm.at[own_rows], nrm.at[own_rows], y_send.at[1], y_recv.at[1], path, there)
    nrm_swap.start()
    og_swap = remote(og.at[own_rows], og.at[own_rows], y_send.at[2], y_recv.at[2], path, there)
    og_swap.start()

    def pass_on(row):
        for n in range(2):
            rings[row][n].wait_recv()
            rings[row][n + 2].start()

    def await_opposite(row):
        for n in range(2, 4):
            rings[row][n].wait_recv()

    rings[0][0].start()
    rings[0][1].start()
    up_picks_x(0)
    pass_on(0)
    up_picks_x(1)
    up_picks_x(2)
    up_swap.wait()
    rings[1][0].start()
    rings[1][1].start()
    up_picks_z(0)
    await_opposite(0)
    up_picks_x(3)
    pass_on(1)
    up_picks_z(1)
    up_picks_z(2)
    await_opposite(1)
    up_picks_z(3)
    for side in range(2):
        dn_copies(side)[0].wait_recv()
        rings[2 + side][0].start()
        rings[2 + side][1].start()
    dn_picks_x(0)
    dn_picks_z(0)
    pass_on(2)
    pass_on(3)
    dn_picks_x(1)
    dn_picks_z(1)
    dn_picks_x(2)
    dn_picks_z(2)
    await_opposite(2)
    dn_picks_x(3)
    await_opposite(3)
    dn_picks_z(3)

    lane = lax.broadcasted_iota(jnp.int32, (16, C * 16), 1)
    same_row = (lane & 15) == lax.broadcasted_iota(jnp.int32, (16, C * 16), 0)
    for level, pick in enumerate((pick_up, pick_dn)):

        def fill(k, _, level=level):
            module = table[lax.div(k, 8) * 16 + yl * 8 + lax.rem(k, 8), level]
            rows = pl.ds(pl.multiple_of(k * 16, 16), 16)
            pick_t[rows, :] = jnp.where(same_row & ((lane >> 4) == module), 1.0, 0.0)
            return 0

        lax.fori_loop(0, GROUP, fill, 0)
        pick[...] = pick_t[...].T.astype(BF16)

        def tally(k, counts, level=level):
            module = table[k, level]
            return tuple(n + jnp.where(module == m, 1, 0) for m, n in enumerate(counts))

        counts = lax.fori_loop(0, 64, tally, (jnp.int32(0),) * C)
        for m in range(C):
            used[level * C + m] = counts[m]

    nrm_swap.wait()

    def turn(i, _):
        cols = pl.ds(pl.multiple_of(i * 256, 256), 256)
        nrm_t[cols, :] = nrm[:, cols].T
        return 0

    lax.fori_loop(0, 4, turn, 0)
    count_swap.wait()
    per_count = 1.0 / (count[0] + count[1])
    per_count = per_count[0:1, 0:1]
    og_swap.wait()

    def scale_rows(i, _):
        rows = pl.ds(pl.multiple_of(i * 64, 64), 64)
        og[rows, :] = (og[rows, :].astype(F32) * per_count).astype(BF16)
        return 0

    lax.fori_loop(0, 12, scale_rows, 0)

    for turn_no in range(3):
        fetch(turn_no)

    settle(wup, wu_recv)
    mine_cols = pl.ds(pl.multiple_of(here * HALF_D, HALF_D), HALF_D)
    their_cols = pl.ds(pl.multiple_of(there * HALF_D, HALF_D), HALF_D)

    def g_copy(chunk):
        rows = pl.ds(pl.multiple_of(chunk * 512, 512), 512)
        return remote(gsend.at[rows], grecv.at[rows], g_send.at[chunk], g_recv.at[chunk], path, there)

    def pre_act(i, half):
        cols = pl.ds(pl.multiple_of(i * 256, 256), 256)
        weights = wup[:, :, :, :, cols].reshape(D, 256)
        wide_a[half] = jnp.dot(nrm[...], weights, preferred_element_type=F32)

    first_tile = 4 * lax.rem(x, 2)
    pre_act(first_tile, 0)

    def hidden(pair, _):
        for half in range(2):
            i = lax.rem(first_tile + pair * 2 + half, 8)
            pre_act(lax.rem(i + 1, 8), 1 - half)
            cols = pl.ds(pl.multiple_of(i * 256, 256), 256)
            for strip in range(24):
                rows = pl.ds(strip * 32, 32)
                pre = wide_a[half, rows, :] * UP_SCALE
                sig = 0.5 * jnp.tanh(0.5 * pre) + 0.5
                out = pre * sig
                act_a[half, rows, :] = out.astype(BF16)
                gp[rows, cols] = (sig + out * (1.0 - sig)).astype(BF16)
            out_t = act_a[half].T
            theirs = jnp.dot(out_t, og[:, their_cols], preferred_element_type=F32)
            gsend[cols, :] = (theirs * DOWN_SCALE).astype(BF16)
            if half == 1:
                g_copy(lax.div(i, 2)).start()
            mine = jnp.dot(out_t, og[:, mine_cols], preferred_element_type=F32)
            gmine[cols, :] = (mine * DOWN_SCALE).astype(BF16)
        return 0

    lax.fori_loop(0, 4, hidden, 0)

    def down_delta(turn_no):
        step = order[turn_no]
        x_ = down_x[step]
        source = gmine if step < 2 else grecv
        first_row = lax.rem(x_, 2) * 1024
        if step >= 2:
            for half in range(2):
                g_copy(lax.rem(x_, 2) * 2 + half).wait_recv()
        slot = turn_no % 3
        await_moments(slot)

        def one(q, _):
            for b in range(4):
                rows = pl.ds(pl.multiple_of(q * 64 + b * 16, 16), 16)
                grad = source[pl.ds(pl.multiple_of(first_row + q * 64 + b * 16, 16), 16), :].astype(F32)
                delta = step_direction(grad, mom[slot, 0, rows, :], mom[slot, 1, rows, :])
                buf_a[x_ * 16 + q, :, pl.ds(b * 512, 512)] = delta
            return 0

        lax.fori_loop(0, 16, one, 0)
        fetch(turn_no + 3)

    def send_down_delta(step, side):
        x_ = down_x[step]

        def send(k, _):
            zc_ = zc_at(k)
            row = x_ * 16 + side * 8 + zc_
            away = (x_ * 8 + zc_) != group

            @pl.when(away)
            def _():
                remote(
                    buf_a.at[row], rdn.at[side, group], dd_send, dd_recv.at[side], place(x_, yl, zc_), here
                ).start()

            @pl.when(jnp.logical_not(away))
            def _():
                pltpu.make_async_copy(buf_a.at[row], rdn.at[side, group], dd_recv.at[side]).start()

            return 0

        lax.fori_loop(0, 8, send, 0)

    settle(buf_a.at[pl.ds(0, 2 * GROUP - 8)], wu_send)
    down_delta(0)
    send_down_delta(0, other_yl)
    send_down_delta(0, yl)
    down_delta(1)

    settle(wdn, wd_recv)

    def hidden_grad(i, _):
        cols = pl.ds(pl.multiple_of(i * 256, 256), 256)
        low = wdn[0, pl.ds(i * 4, 4)].reshape(256, HALF_D)
        high = wdn[1, pl.ds(i * 4, 4)].reshape(256, HALF_D)
        grad = lax.dot_general(og[:, pl.ds(0, HALF_D)], low, NT, preferred_element_type=F32)
        grad += lax.dot_general(og[:, pl.ds(HALF_D, HALF_D)], high, NT, preferred_element_type=F32)
        gp[:, cols] = (grad * DOWN_SCALE * gp[:, cols].astype(F32)).astype(BF16)
        return 0

    lax.fori_loop(0, 8, hidden_grad, 0)
    settle(buf_b.at[pl.ds(0, 2 * GROUP - 8)], wd_send)

    def send_up_delta(x_, zc_, side):
        row = x_ * 16 + side * 8 + zc_
        away = (x_ * 8 + zc_) != group

        @pl.when(away)
        def _():
            remote(
                buf_b.at[row], rup.at[side, group], du_send, du_recv.at[side], place(x_, yl, zc_), here
            ).start()

        @pl.when(jnp.logical_not(away))
        def _():
            pltpu.make_async_copy(buf_b.at[row], rup.at[side, group], du_recv.at[side]).start()

    def up_step(turn_no):
        x_ = up_block[order[turn_no] - 4]
        slot = turn_no % 3
        lhs = nrm_t[pl.ds(pl.multiple_of(x_ * 256, 256), 256), :]

        def up_grad(b):
            wide_b[b % 2] = jnp.dot(lhs, gp[:, pl.ds(b * 512, 512)], preferred_element_type=F32)

        up_grad(0)
        await_moments(slot)
        for b in range(4):
            if b < 3:
                up_grad(b + 1)
            for i in range(16):
                rows = pl.ds(b * 256 + i * 16, 16)
                grad = wide_b[b % 2, pl.ds(i * 16, 16), :] * UP_SCALE
                delta = step_direction(grad, mom[slot, 0, rows, :], mom[slot, 1, rows, :])
                buf_b[x_ * 16 + i, pl.ds(b * 16, 16), :] = delta
        fetch(turn_no + 3)

        def send(k, _):
            send_up_delta(x_, zc_at(k), lax.rem(other_yl + lax.div(k, 8), 2))
            return 0

        lax.fori_loop(0, 16, send, 0)

    up_step(2)
    up_step(3)
    down_delta(4)
    send_down_delta(2, other_yl)
    send_down_delta(2, yl)
    up_step(5)
    up_step(6)
    down_delta(7)
    for side in (other_yl, yl):
        send_down_delta(1, side)
        send_down_delta(3, side)

    def down_sum(side, b):
        block = rdn[side, :, :, pl.ds(b * 512, 512)].reshape(GROUP * 16, 512)
        return jnp.dot(pick_dn[...], block, preferred_element_type=F32).reshape(C, 16, 512)

    def up_sum(side, b):
        block = rup[side, :, pl.ds(b * 16, 16), :].reshape(GROUP * 16, 512)
        return jnp.dot(pick_up[...], block, preferred_element_type=F32).reshape(C, 16, 512)

    def finish(total, master, level, rows, cols):
        for m in range(C):
            number = jnp.broadcast_to(used[level * C + m].astype(F32), (8, 128))
            per_used = (1.0 / jnp.maximum(number, 1.0))[0:1, 0:1]
            decay = (0.01 * jnp.minimum(number, 1.0))[0:1, 0:1]
            weights = master[m, rows, cols].astype(BF16).astype(F32)
            master[m, rows, cols] = total[m] * per_used + decay * weights

    mate = place(x, other_yl, zc)
    stores = [
        pltpu.make_async_copy(src, dst, out_sem.at[i]) for i, (src, dst) in enumerate([(dm, dm_out), (um, um_out)])
    ]
    settle(rup.at[other_yl], du_recv.at[other_yl])
    for b in range(4):
        pup_send[:, pl.ds(b * 16, 16), :] = up_sum(other_yl, b).astype(BF16)
    up_part = remote(pup_send, pup_recv, y_send.at[5], y_recv.at[5], mate, here)
    up_part.start()
    settle(rup.at[yl], du_recv.at[yl])
    up_part.wait()
    for b in range(4):
        rows = pl.ds(b * 16, 16)
        total = up_sum(yl, b) + pup_recv[:, rows, :].astype(F32)
        finish(total, um, 0, pl.ds(0, 16), pl.ds(b * 512, 512))
    stores[1].start()

    settle(rdn.at[other_yl], dd_recv.at[other_yl])
    for b in range(4):
        pdn_send[:, :, pl.ds(b * 512, 512)] = down_sum(other_yl, b).astype(BF16)
    dn_part = remote(pdn_send, pdn_recv, y_send.at[4], y_recv.at[4], mate, here)
    dn_part.start()
    settle(rdn.at[yl], dd_recv.at[yl])
    dn_part.wait()
    for b in range(4):
        cols = pl.ds(b * 512, 512)
        total = down_sum(yl, b) + pdn_recv[:, :, cols].astype(F32)
        finish(total, dm, 1, pl.ds(b * 16, 16), pl.ds(0, 512))
    stores[0].start()

    far, near, _ = dn_copies(0)
    far.wait_send()
    pl.when(cross == 1)(near.wait_send)
    for hops in rings:
        for hop in hops:
            hop.wait_send()
    for chunk in range(4):
        g_copy(chunk).wait_send()
    settle(buf_a.at[pl.ds(0, 2 * GROUP - 2)], dd_send)
    settle(buf_b.at[pl.ds(0, 2 * GROUP - 2)], du_send)
    for store in stores:
        store.wait()


def shards(
    activations,
    cotangent,
    token_ids,
    path_table,
    up_master,
    down_master,
    up_momentum,
    down_momentum,
    up_first,
    up_second,
    down_first,
    down_second,
):
    anywhere = pl.BlockSpec(memory_space=pl.ANY)
    smem = pl.BlockSpec(memory_space=pltpu.SMEM)
    vmem = pl.BlockSpec(memory_space=pltpu.VMEM)
    dma = pltpu.SemaphoreType.DMA
    up_mean, down_mean = pl.pallas_call(
        kernel,
        out_shape=[jax.ShapeDtypeStruct(array.shape, F32) for array in (up_master, down_master)],
        in_specs=[smem, vmem] + [anywhere] * 8,
        out_specs=[anywhere] * 2,
        scratch_shapes=[
            pltpu.VMEM((C, 16, HALF_F), F32),
            pltpu.VMEM((C, 64, HALF_D), F32),
            *[pltpu.VMEM((C, 16, HALF_F), BF16)] * 8,
            *[pltpu.VMEM((C, 64, HALF_D), BF16)] * 8,
            pltpu.VMEM((C, 64, HALF_D), BF16),
            pltpu.VMEM((2 * GROUP, 16, HALF_F), BF16),
            pltpu.VMEM((2 * GROUP, 64, HALF_D), BF16),
            pltpu.VMEM((4, 2, 8, 16, HALF_F), BF16),
            pltpu.VMEM((2, GROUP, 64, HALF_D), BF16),
            pltpu.VMEM((2, GROUP, 16, HALF_F), BF16),
            pltpu.VMEM((2, GROUP, 64, HALF_D), BF16),
            pltpu.VMEM((HALF_F, HALF_D), BF16),
            pltpu.VMEM((HALF_F, HALF_D), BF16),
            pltpu.VMEM((HALF_F, HALF_D), BF16),
            pltpu.VMEM((2 * TOK, D), BF16),
            pltpu.VMEM((D, 2 * TOK), BF16),
            pltpu.VMEM((2 * TOK, D), BF16),
            pltpu.VMEM((2, 8, 128), F32),
            pltpu.SMEM((2 * C,), jnp.int32),
            pltpu.VMEM((2 * TOK, HALF_F), BF16),
            pltpu.VMEM((2, 2 * TOK, 256), F32),
            pltpu.VMEM((2, 2 * TOK, 256), BF16),
            pltpu.VMEM((2, 256, 512), F32),
            pltpu.VMEM((3, 2, 1024, 512), BF16),
            pltpu.VMEM((C, 16, HALF_F), BF16),
            pltpu.VMEM((C, 16, HALF_F), BF16),
            pltpu.VMEM((C, 64, HALF_D), BF16),
            pltpu.VMEM((C, 64, HALF_D), BF16),
            pltpu.VMEM((GROUP * 16, C * 16), F32),
            pltpu.VMEM((C * 16, GROUP * 16), BF16),
            pltpu.VMEM((C * 16, GROUP * 16), BF16),
            dma((4,)),
            dma((3, 2)),
            dma((2,)),
            dma((6,)),
            dma((6,)),
            dma((4, 4)),
            dma((4, 4)),
            dma((2,)),
            dma((2,)),
            dma,
            dma,
            dma,
            dma,
            dma((4,)),
            dma((4,)),
            dma,
            dma((2,)),
            dma,
            dma((2,)),
        ],
        compiler_params=pltpu.CompilerParams(
            collective_id=0, has_side_effects=True, vmem_limit_bytes=62 * 1024 * 1024
        ),
        cost_estimate=pl.CostEstimate(flops=12_884_901_888, bytes_accessed=30_000_000, transcendentals=1_572_864),
    )(
        path_table,
        token_ids,
        activations[0],
        cotangent[0],
        up_master,
        down_master,
        up_first[0],
        up_second[0],
        down_first[0],
        down_second[0],
    )
    new_up_momentum = 0.9 * up_momentum + up_mean
    new_down_momentum = 0.9 * down_momentum + down_mean
    new_up_master = up_master - 0.7 * (up_mean + 0.9 * new_up_momentum)
    new_down_master = down_master - 0.7 * (down_mean + 0.9 * new_down_momentum)
    return (new_up_master, new_down_master, new_up_momentum, new_down_momentum)


def solution(mesh):
    placed = (
        P("path", "dp", None),
        P("path", "dp", None),
        P("path", "dp"),
        P(),
        P(None, "path", "dp"),
        P(None, "path", "dp"),
        P(None, "path", "dp"),
        P(None, "path", "dp"),
        P("path", None, "dp"),
        P("path", None, "dp"),
        P("path", None, "dp"),
        P("path", None, "dp"),
    )
    return jax.shard_map(
        shards,
        mesh=mesh,
        in_specs=placed,
        out_specs=(
            P(None, "path", "dp"),
            P(None, "path", "dp"),
            P(None, "path", "dp"),
            P(None, "path", "dp"),
        ),
        check_vma=False,
    )
```

```python
import jax
import jax.numpy as jnp
from jax import lax
from jax.experimental import pallas as pl
from jax.experimental.pallas import tpu as pltpu
from jax.sharding import PartitionSpec as P

D = 1024
F = 4096
C = 8
TOK = 384
HALF_F = F // 2
HALF_D = D // 2
GROUP = 32
MESH = pl.DeviceIdType.MESH
BF16 = jnp.bfloat16
F32 = jnp.float32
NT = (((1,), (1,)), ((), ()))
TN = (((0,), (0,)), ((), ()))
UP_SCALE = D ** (-0.5)
DOWN_SCALE = F ** (-0.5)


def step_direction(gradient, first_moment, second_moment):
    first_new = 0.9 * first_moment.astype(F32) + 0.1 * gradient
    second_new = 0.95 * second_moment.astype(F32) + 0.05 * gradient * gradient
    below = second_new * lax.rsqrt(second_new) + 1e-08
    over = pl.reciprocal(below, approx=True)
    over = over * (2.0 - below * over)
    return (0.1 * first_new * over).astype(BF16)


def kernel(
    table, ids, act_in, cot_in, um_in, dm_in, up_first, up_second, down_first, down_second, um_out, dm_out,
    um, dm, act, cot, upb, upf, dnb, blk, buf_a, buf_b, wup, wdn, rdn, rup,
    gsend, gmine, grecv, nrm, nrm_t, og, count, used, gp, wide_a, act_a, wide_b, mom,
    pdn_send, pdn_recv, pup_send, pup_recv, pick_t, pick_up, pick_dn,
    in_sem, mom_sem, out_sem, y_send, y_recv, dn_send, blk_recv, wu_send, wu_recv, wd_send, wd_recv,
    g_send, g_recv, dd_send, dd_recv, du_send, du_recv,
):
    path = lax.axis_index("path")
    here = lax.axis_index("dp")
    x = lax.div(path, 16)
    yl = lax.rem(lax.div(path, 8), 2)
    zc = lax.rem(path, 8)
    z = lax.div(zc, 2)
    core = lax.rem(zc, 2)
    group = x * 8 + zc
    other_yl = 1 - yl
    there = 1 - here

    def place(x_, yl_, zc_):
        return x_ * 16 + yl_ * 8 + zc_

    def zc_at(k):
        return lax.rem(z + lax.rem(lax.div(k, 2), 4), 4) * 2 + lax.rem(core + k, 2)

    def peer(k):
        return lax.rem(x + lax.div(k, 8), 4), zc_at(k)

    def remote(src, dst, send, recv, to_path, to_dp):
        return pltpu.make_async_remote_copy(
            src_ref=src, dst_ref=dst, send_sem=send, recv_sem=recv,
            device_id=(to_path, to_dp), device_id_type=MESH,
        )

    def settle(ref, sem):
        pltpu.make_async_copy(ref, ref, sem).wait()

    loads = [
        pltpu.make_async_copy(src, dst, in_sem.at[i])
        for i, (src, dst) in enumerate(
            [(um_in, um), (act_in, act), (dm_in, dm), (cot_in, cot)]
        )
    ]
    for load in loads:
        load.start()

    cross = lax.rem(lax.div(x, 2) + here, 2)
    barrier = pltpu.get_barrier_semaphore()

    def greet(k, _):
        x_, zc_ = peer(k)
        pl.semaphore_signal(barrier, inc=1, device_id=(place(x_, yl, zc_), here), device_id_type=MESH)
        return 0

    lax.fori_loop(1, GROUP, greet, 0)
    for to_path, to_dp in (
        (place(x, other_yl, zc), here),
        (path, there),
        (place(3 - x, yl, zc), there),
        (place(3 - x, other_yl, zc), there),
    ):
        pl.semaphore_signal(barrier, inc=1, device_id=(to_path, to_dp), device_id_type=MESH)

    def pick_up_rows(side, source):
        def one(k, _):
            module = table[lax.div(k, 8) * 16 + yl * 8 + lax.rem(k, 8), 0]
            buf_a[side * GROUP + k] = source[module]
            return 0

        lax.fori_loop(0, GROUP, one, 0)

    loads[0].wait()
    upb[...] = um[...].astype(BF16)
    pick_up_rows(yl, upb)
    pl.semaphore_wait(barrier, GROUP + 3)

    up_swap = remote(upb, upf, y_send.at[0], y_recv.at[0], place(x, other_yl, zc), here)
    up_swap.start()

    def send_up_rows(side, half):
        row = place(x, side, zc)
        pltpu.make_async_copy(buf_a.at[side * GROUP + group], wup.at[row], wu_recv).start()

        def one(k, _):
            x_, zc_ = peer(lax.rem(k * 11, GROUP))
            remote(
                buf_a.at[side * GROUP + x_ * 8 + zc_], wup.at[row], wu_send.at[half], wu_recv, place(x_, yl, zc_), here
            ).start()
            return 0

        lax.fori_loop(1, GROUP, one, 0)

    send_up_rows(yl, 0)

    own_rows = pl.ds(pl.multiple_of(here * TOK, TOK), TOK)
    loads[1].wait()
    for part in range(3):
        rows = pl.ds(part * 128, 128)
        wide = act[rows, :].astype(F32)
        mean_square = jnp.mean(wide * wide, axis=-1, keepdims=True)
        to_rows = pl.ds(pl.multiple_of(here * TOK + part * 128, 128), 128)
        nrm[to_rows, :] = (wide * lax.rsqrt(mean_square + 1e-06)).astype(BF16)
    nrm_swap = remote(nrm.at[own_rows], nrm.at[own_rows], y_send.at[1], y_recv.at[1], path, there)
    nrm_swap.start()

    loads[2].wait()
    dnb[...] = dm[...].astype(BF16)
    x_to = x + cross * (3 - 2 * x)
    dp_to = here + cross * (1 - 2 * here)
    dn_far = remote(dnb, blk.at[yl], dn_send.at[0], blk_recv, place(x_to, other_yl, zc), dp_to)
    dn_far.start()
    dn_near = remote(dnb, blk.at[yl], dn_send.at[1], blk_recv, place(3 - x, yl, zc), there)

    @pl.when(cross == 1)
    def _():
        dn_near.start()

    @pl.when(cross == 0)
    def _():
        pltpu.make_async_copy(dnb, blk.at[yl], blk_recv).start()

    loads[3].wait()
    live = jnp.sum((ids[...] != 0).astype(F32))
    for part in range(3):
        rows = pl.ds(part * 128, 128)
        to_rows = pl.ds(pl.multiple_of(here * TOK + part * 128, 128), 128)
        position = (lax.broadcasted_iota(jnp.int32, (128, D), 0) + part * 128).astype(F32)
        og[to_rows, :] = jnp.where(position < live, cot[rows, :].astype(F32), 0.0).astype(BF16)
    count[0] = jnp.broadcast_to(live, (8, 128))
    count_swap = remote(count.at[0], count.at[1], y_send.at[3], y_recv.at[3], path, there)
    count_swap.start()
    og_swap = remote(og.at[own_rows], og.at[own_rows], y_send.at[2], y_recv.at[2], path, there)
    og_swap.start()

    up_swap.wait()
    pick_up_rows(other_yl, upf)
    send_up_rows(other_yl, 1)

    settle(blk, blk_recv)

    def pick_down_rows(k, _):
        module = table[lax.div(k, 8) * 16 + yl * 8 + lax.rem(k, 8), 1]
        buf_b[k] = blk[0, module]
        buf_b[GROUP + k] = blk[1, module]
        return 0

    lax.fori_loop(0, GROUP, pick_down_rows, 0)

    settle(buf_a.at[pl.ds(0, GROUP - 1)], wu_send.at[0])
    from_x = x_to - 2 * here
    for side in range(2):
        row = from_x * 16 + side * 8 + zc
        pltpu.make_async_copy(buf_b.at[side * GROUP + group], wdn.at[dp_to, row], wd_recv).start()

        def one(k, _, side=side, row=row):
            x_, zc_ = peer(lax.rem(k * 11, GROUP))
            remote(
                buf_b.at[side * GROUP + x_ * 8 + zc_], wdn.at[dp_to, row], wd_send, wd_recv,
                place(x_, yl, zc_), here,
            ).start()
            return 0

        lax.fori_loop(1, GROUP, one, 0)

    nrm_swap.wait()

    def turn(i, _):
        cols = pl.ds(pl.multiple_of(i * 256, 256), 256)
        nrm_t[cols, :] = nrm[:, cols].T
        return 0

    lax.fori_loop(0, 4, turn, 0)
    count_swap.wait()
    per_count = 1.0 / (count[0] + count[1])
    per_count = per_count[0:1, 0:1]
    og_swap.wait()

    def scale_rows(i, _):
        rows = pl.ds(pl.multiple_of(i * 64, 64), 64)
        og[rows, :] = (og[rows, :].astype(F32) * per_count).astype(BF16)
        return 0

    lax.fori_loop(0, 12, scale_rows, 0)

    down_x = [here * 2 + lax.rem(x + i, 2) for i in range(2)] + [there * 2 + lax.rem(x + i, 2) for i in range(2)]
    up_x = [lax.rem(x + i, 4) for i in (2, 1, 3, 0)]

    order = (0, 1, 2, 3, 4, 5, 6, 7)

    def fetch(turn_no):
        if turn_no >= 8:
            return
        slot = turn_no % 2
        step = order[turn_no]
        for kind, (down_source, up_source) in enumerate(((down_first, up_first), (down_second, up_second))):
            if step < 4:
                rows = pl.ds(pl.multiple_of(down_x[step] * 1024, 1024), 1024)
                pltpu.make_async_copy(
                    down_source.at[rows], mom.at[slot, kind], mom_sem.at[slot, kind]
                ).start()
            else:
                rows = pl.ds(pl.multiple_of(up_x[step - 4] * 256, 256), 256)
                for b in range(4):
                    pltpu.make_async_copy(
                        up_source.at[rows, pl.ds(b * 512, 512)],
                        mom.at[slot, kind, pl.ds(b * 256, 256)],
                        mom_sem.at[slot, kind],
                    ).start()

    def await_moments(turn_no):
        slot = turn_no % 2
        for kind in range(2):
            settle(mom.at[slot, kind], mom_sem.at[slot, kind])

    fetch(0)
    fetch(1)

    settle(wup, wu_recv)
    mine_cols = pl.ds(pl.multiple_of(here * HALF_D, HALF_D), HALF_D)
    their_cols = pl.ds(pl.multiple_of(there * HALF_D, HALF_D), HALF_D)

    def g_copy(chunk):
        rows = pl.ds(pl.multiple_of(chunk * 512, 512), 512)
        return remote(gsend.at[rows], grecv.at[rows], g_send.at[chunk], g_recv.at[chunk], path, there)

    def pre_act(i, half):
        cols = pl.ds(pl.multiple_of(i * 256, 256), 256)
        weights = wup[:, :, cols].reshape(D, 256)
        wide_a[half] = jnp.dot(nrm[...], weights, preferred_element_type=F32)

    first_tile = 4 * lax.rem(x, 2)
    pre_act(first_tile, 0)

    def hidden(pair, _):
        for half in range(2):
            i = lax.rem(first_tile + pair * 2 + half, 8)
            pre_act(lax.rem(i + 1, 8), 1 - half)
            cols = pl.ds(pl.multiple_of(i * 256, 256), 256)
            for strip in range(24):
                rows = pl.ds(strip * 32, 32)
                pre = wide_a[half, rows, :] * UP_SCALE
                sig = 0.5 * jnp.tanh(0.5 * pre) + 0.5
                out = pre * sig
                act_a[half, rows, :] = out.astype(BF16)
                gp[rows, cols] = (sig + out * (1.0 - sig)).astype(BF16)
            out_t = act_a[half].T
            theirs = jnp.dot(out_t, og[:, their_cols], preferred_element_type=F32)
            gsend[cols, :] = (theirs * DOWN_SCALE).astype(BF16)
            if half == 1:
                g_copy(lax.div(i, 2)).start()
            mine = jnp.dot(out_t, og[:, mine_cols], preferred_element_type=F32)
            gmine[cols, :] = (mine * DOWN_SCALE).astype(BF16)
        return 0

    lax.fori_loop(0, 4, hidden, 0)

    def down_delta(turn_no):
        step = order[turn_no]
        x_ = down_x[step]
        source = gmine if step < 2 else grecv
        first_row = lax.rem(x_, 2) * 1024
        if step >= 2:
            for half in range(2):
                g_copy(lax.rem(x_, 2) * 2 + half).wait_recv()
        await_moments(turn_no)
        slot = turn_no % 2

        def one(q, _):
            for b in range(4):
                rows = pl.ds(pl.multiple_of(q * 64 + b * 16, 16), 16)
                grad = source[pl.ds(pl.multiple_of(first_row + q * 64 + b * 16, 16), 16), :].astype(F32)
                delta = step_direction(grad, mom[slot, 0, rows, :], mom[slot, 1, rows, :])
                buf_a[x_ * 16 + q, :, pl.ds(b * 512, 512)] = delta
            return 0

        lax.fori_loop(0, 16, one, 0)
        fetch(turn_no + 2)

    def send_down_delta(step, side):
        x_ = down_x[step]

        def send(k, _):
            zc_ = zc_at(k)
            row = x_ * 16 + side * 8 + zc_
            away = (x_ * 8 + zc_) != group

            @pl.when(away)
            def _():
                remote(
                    buf_a.at[row], rdn.at[side, group], dd_send, dd_recv.at[side], place(x_, yl, zc_), here
                ).start()

            @pl.when(jnp.logical_not(away))
            def _():
                pltpu.make_async_copy(buf_a.at[row], rdn.at[side, group], dd_recv.at[side]).start()

            return 0

        lax.fori_loop(0, 8, send, 0)

    settle(buf_a.at[pl.ds(0, GROUP - 1)], wu_send.at[1])
    down_delta(0)
    down_delta(1)
    settle(buf_b.at[pl.ds(0, 2 * GROUP - 2)], wd_send)
    for turn_no in range(4):
        if turn_no >= 2:
            down_delta(turn_no)
        send_down_delta(turn_no, other_yl)
        send_down_delta(turn_no, yl)

    settle(wdn, wd_recv)

    def hidden_grad(i, _):
        cols = pl.ds(pl.multiple_of(i * 256, 256), 256)
        low = wdn[0, pl.ds(i * 4, 4)].reshape(256, HALF_D)
        high = wdn[1, pl.ds(i * 4, 4)].reshape(256, HALF_D)
        grad = lax.dot_general(og[:, pl.ds(0, HALF_D)], low, NT, preferred_element_type=F32)
        grad += lax.dot_general(og[:, pl.ds(HALF_D, HALF_D)], high, NT, preferred_element_type=F32)
        gp[:, cols] = (grad * DOWN_SCALE * gp[:, cols].astype(F32)).astype(BF16)
        return 0

    lax.fori_loop(0, 8, hidden_grad, 0)

    def send_up_delta(x_, zc_, side):
        row = x_ * 16 + side * 8 + zc_
        away = (x_ * 8 + zc_) != group

        @pl.when(away)
        def _():
            remote(
                buf_b.at[row], rup.at[side, group], du_send, du_recv.at[side], place(x_, yl, zc_), here
            ).start()

        @pl.when(jnp.logical_not(away))
        def _():
            pltpu.make_async_copy(buf_b.at[row], rup.at[side, group], du_recv.at[side]).start()

    def up_step(turn_no):
        x_ = up_x[order[turn_no] - 4]
        slot = turn_no % 2
        lhs = nrm_t[pl.ds(pl.multiple_of(x_ * 256, 256), 256), :]

        def up_grad(b):
            wide_b[b % 2] = jnp.dot(lhs, gp[:, pl.ds(b * 512, 512)], preferred_element_type=F32)

        up_grad(0)
        await_moments(turn_no)
        for b in range(4):
            if b < 3:
                up_grad(b + 1)
            for i in range(16):
                rows = pl.ds(b * 256 + i * 16, 16)
                grad = wide_b[b % 2, pl.ds(i * 16, 16), :] * UP_SCALE
                delta = step_direction(grad, mom[slot, 0, rows, :], mom[slot, 1, rows, :])
                buf_b[x_ * 16 + i, pl.ds(b * 16, 16), :] = delta
        fetch(turn_no + 2)

    for turn_no in range(4, 8):
        up_step(turn_no)

    settle(buf_a.at[pl.ds(0, 2 * GROUP - 2)], dd_send)
    for side in (other_yl, yl):

        def send_side(k, _, side=side):
            x_, zc_ = peer(lax.rem(k * 11, GROUP))
            send_up_delta(x_, zc_, side)
            return 0

        lax.fori_loop(0, GROUP, send_side, 0)

    lane = lax.broadcasted_iota(jnp.int32, (16, C * 16), 1)
    same_row = (lane & 15) == lax.broadcasted_iota(jnp.int32, (16, C * 16), 0)
    for level, pick in enumerate((pick_up, pick_dn)):

        def fill(k, _, level=level):
            module = table[lax.div(k, 8) * 16 + yl * 8 + lax.rem(k, 8), level]
            rows = pl.ds(pl.multiple_of(k * 16, 16), 16)
            pick_t[rows, :] = jnp.where(same_row & ((lane >> 4) == module), 1.0, 0.0)
            return 0

        lax.fori_loop(0, GROUP, fill, 0)
        pick[...] = pick_t[...].T.astype(BF16)

        def tally(k, counts, level=level):
            module = table[k, level]
            return tuple(n + jnp.where(module == m, 1, 0) for m, n in enumerate(counts))

        counts = lax.fori_loop(0, 64, tally, (jnp.int32(0),) * C)
        for m in range(C):
            used[level * C + m] = counts[m]

    def down_sum(side, b):
        block = rdn[side, :, :, pl.ds(b * 512, 512)].reshape(GROUP * 16, 512)
        return jnp.dot(pick_dn[...], block, preferred_element_type=F32).reshape(C, 16, 512)

    def up_sum(side, b):
        block = rup[side, :, pl.ds(b * 16, 16), :].reshape(GROUP * 16, 512)
        return jnp.dot(pick_up[...], block, preferred_element_type=F32).reshape(C, 16, 512)

    def finish(total, master, level, rows, cols):
        for m in range(C):
            number = jnp.broadcast_to(used[level * C + m].astype(F32), (8, 128))
            per_used = (1.0 / jnp.maximum(number, 1.0))[0:1, 0:1]
            decay = (0.01 * jnp.minimum(number, 1.0))[0:1, 0:1]
            weights = master[m, rows, cols].astype(BF16).astype(F32)
            master[m, rows, cols] = total[m] * per_used + decay * weights

    mate = place(x, other_yl, zc)
    stores = [
        pltpu.make_async_copy(src, dst, out_sem.at[i]) for i, (src, dst) in enumerate([(dm, dm_out), (um, um_out)])
    ]
    settle(rdn.at[other_yl], dd_recv.at[other_yl])
    for b in range(4):
        pdn_send[:, :, pl.ds(b * 512, 512)] = down_sum(other_yl, b).astype(BF16)
    dn_part = remote(pdn_send, pdn_recv, y_send.at[4], y_recv.at[4], mate, here)
    dn_part.start()
    settle(rdn.at[yl], dd_recv.at[yl])
    dn_part.wait()
    for b in range(4):
        cols = pl.ds(b * 512, 512)
        total = down_sum(yl, b) + pdn_recv[:, :, cols].astype(F32)
        finish(total, dm, 1, pl.ds(b * 16, 16), pl.ds(0, 512))
    stores[0].start()

    settle(rup.at[other_yl], du_recv.at[other_yl])
    for b in range(4):
        pup_send[:, pl.ds(b * 16, 16), :] = up_sum(other_yl, b).astype(BF16)
    up_part = remote(pup_send, pup_recv, y_send.at[5], y_recv.at[5], mate, here)
    up_part.start()
    settle(rup.at[yl], du_recv.at[yl])
    up_part.wait()
    for b in range(4):
        rows = pl.ds(b * 16, 16)
        total = up_sum(yl, b) + pup_recv[:, rows, :].astype(F32)
        finish(total, um, 0, pl.ds(0, 16), pl.ds(b * 512, 512))
    stores[1].start()

    dn_far.wait_send()

    @pl.when(cross == 1)
    def _():
        dn_near.wait_send()

    for chunk in range(4):
        g_copy(chunk).wait_send()
    settle(buf_b.at[pl.ds(0, 2 * GROUP - 2)], du_send)
    for store in stores:
        store.wait()


def shards(
    activations,
    cotangent,
    token_ids,
    path_table,
    up_master,
    down_master,
    up_momentum,
    down_momentum,
    up_first,
    up_second,
    down_first,
    down_second,
):
    anywhere = pl.BlockSpec(memory_space=pl.ANY)
    smem = pl.BlockSpec(memory_space=pltpu.SMEM)
    vmem = pl.BlockSpec(memory_space=pltpu.VMEM)
    dma = pltpu.SemaphoreType.DMA
    up_mean, down_mean = pl.pallas_call(
        kernel,
        out_shape=[jax.ShapeDtypeStruct(array.shape, F32) for array in (up_master, down_master)],
        in_specs=[smem, vmem] + [anywhere] * 8,
        out_specs=[anywhere] * 2,
        scratch_shapes=[
            pltpu.VMEM((C, 16, HALF_F), F32),
            pltpu.VMEM((C, 64, HALF_D), F32),
            pltpu.VMEM((TOK, D), BF16),
            pltpu.VMEM((TOK, D), BF16),
            pltpu.VMEM((C, 16, HALF_F), BF16),
            pltpu.VMEM((C, 16, HALF_F), BF16),
            pltpu.VMEM((C, 64, HALF_D), BF16),
            pltpu.VMEM((2, C, 64, HALF_D), BF16),
            pltpu.VMEM((2 * GROUP, 16, HALF_F), BF16),
            pltpu.VMEM((2 * GROUP, 64, HALF_D), BF16),
            pltpu.VMEM((2 * GROUP, 16, HALF_F), BF16),
            pltpu.VMEM((2, GROUP, 64, HALF_D), BF16),
            pltpu.VMEM((2, GROUP, 16, HALF_F), BF16),
            pltpu.VMEM((2, GROUP, 64, HALF_D), BF16),
            pltpu.VMEM((HALF_F, HALF_D), BF16),
            pltpu.VMEM((HALF_F, HALF_D), BF16),
            pltpu.VMEM((HALF_F, HALF_D), BF16),
            pltpu.VMEM((2 * TOK, D), BF16),
            pltpu.VMEM((D, 2 * TOK), BF16),
            pltpu.VMEM((2 * TOK, D), BF16),
            pltpu.VMEM((2, 8, 128), F32),
            pltpu.SMEM((2 * C,), jnp.int32),
            pltpu.VMEM((2 * TOK, HALF_F), BF16),
            pltpu.VMEM((2, 2 * TOK, 256), F32),
            pltpu.VMEM((2, 2 * TOK, 256), BF16),
            pltpu.VMEM((2, 256, 512), F32),
            pltpu.VMEM((2, 2, 1024, 512), BF16),
            pltpu.VMEM((C, 16, HALF_F), BF16),
            pltpu.VMEM((C, 16, HALF_F), BF16),
            pltpu.VMEM((C, 64, HALF_D), BF16),
            pltpu.VMEM((C, 64, HALF_D), BF16),
            pltpu.VMEM((GROUP * 16, C * 16), F32),
            pltpu.VMEM((C * 16, GROUP * 16), BF16),
            pltpu.VMEM((C * 16, GROUP * 16), BF16),
            dma((4,)),
            dma((2, 2)),
            dma((2,)),
            dma((6,)),
            dma((6,)),
            dma((2,)),
            dma,
            dma((2,)),
            dma,
            dma,
            dma,
            dma((4,)),
            dma((4,)),
            dma,
            dma((2,)),
            dma,
            dma((2,)),
        ],
        compiler_params=pltpu.CompilerParams(
            collective_id=0, has_side_effects=True, vmem_limit_bytes=62 * 1024 * 1024
        ),
        cost_estimate=pl.CostEstimate(flops=12_884_901_888, bytes_accessed=30_000_000, transcendentals=1_572_864),
    )(
        path_table,
        token_ids,
        activations[0],
        cotangent[0],
        up_master,
        down_master,
        up_first[0],
        up_second[0],
        down_first[0],
        down_second[0],
    )
    new_up_momentum = 0.9 * up_momentum + up_mean
    new_down_momentum = 0.9 * down_momentum + down_mean
    new_up_master = up_master - 0.7 * (up_mean + 0.9 * new_up_momentum)
    new_down_master = down_master - 0.7 * (down_mean + 0.9 * new_down_momentum)
    return (new_up_master, new_down_master, new_up_momentum, new_down_momentum)


def solution(mesh):
    placed = (
        P("path", "dp", None),
        P("path", "dp", None),
        P("path", "dp"),
        P(),
        P(None, "path", "dp"),
        P(None, "path", "dp"),
        P(None, "path", "dp"),
        P(None, "path", "dp"),
        P("path", None, "dp"),
        P("path", None, "dp"),
        P("path", None, "dp"),
        P("path", None, "dp"),
    )
    return jax.shard_map(
        shards,
        mesh=mesh,
        in_specs=placed,
        out_specs=(
            P(None, "path", "dp"),
            P(None, "path", "dp"),
            P(None, "path", "dp"),
            P(None, "path", "dp"),
        ),
        check_vma=False,
    )
```

```python
import jax
import jax.numpy as jnp
from jax import lax
from jax.experimental import pallas as pl
from jax.experimental.pallas import tpu as pltpu
from jax.sharding import PartitionSpec as P

D = 1024
F = 4096
C = 8
TOK = 384
HALF_F = F // 2
HALF_D = D // 2
GROUP = 32
MESH = pl.DeviceIdType.MESH
BF16 = jnp.bfloat16
F32 = jnp.float32
NT = (((1,), (1,)), ((), ()))
TN = (((0,), (0,)), ((), ()))
UP_SCALE = D ** (-0.5)
DOWN_SCALE = F ** (-0.5)


def step_direction(gradient, first_moment, second_moment):
    first_new = 0.9 * first_moment.astype(F32) + 0.1 * gradient
    second_new = 0.95 * second_moment.astype(F32) + 0.05 * gradient * gradient
    below = second_new * lax.rsqrt(second_new) + 1e-08
    over = pl.reciprocal(below, approx=True)
    over = over * (2.0 - below * over)
    return (0.1 * first_new * over).astype(BF16)


def kernel(
    table, ids, act_in, cot_in, um_in, dm_in, up_first, up_second, down_first, down_second, um_out, dm_out,
    um, dm, act, cot, upb, upf, dnb, blk, buf_a, buf_b, wup, wdn, rdn, rup,
    gsend, gmine, grecv, nrm, nrm_t, og, count, used, gp, wide_a, act_a, wide_b, mom,
    pdn_send, pdn_recv, pup_send, pup_recv, pick_t, pick_up, pick_dn,
    in_sem, mom_sem, out_sem, y_send, y_recv, dn_send, blk_recv, wu_send, wu_recv, wd_send, wd_recv,
    g_send, g_recv, dd_send, dd_recv, du_send, du_recv,
):
    path = lax.axis_index("path")
    here = lax.axis_index("dp")
    x = lax.div(path, 16)
    yl = lax.rem(lax.div(path, 8), 2)
    zc = lax.rem(path, 8)
    z = lax.div(zc, 2)
    core = lax.rem(zc, 2)
    group = x * 8 + zc
    other_yl = 1 - yl
    there = 1 - here

    def place(x_, yl_, zc_):
        return x_ * 16 + yl_ * 8 + zc_

    def zc_at(k):
        return lax.rem(z + lax.rem(lax.div(k, 2), 4), 4) * 2 + lax.rem(core + k, 2)

    def peer(k):
        return lax.rem(x + lax.div(k, 8), 4), zc_at(k)

    def remote(src, dst, send, recv, to_path, to_dp):
        return pltpu.make_async_remote_copy(
            src_ref=src, dst_ref=dst, send_sem=send, recv_sem=recv,
            device_id=(to_path, to_dp), device_id_type=MESH,
        )

    def settle(ref, sem):
        pltpu.make_async_copy(ref, ref, sem).wait()

    loads = [
        pltpu.make_async_copy(src, dst, in_sem.at[i])
        for i, (src, dst) in enumerate(
            [(um_in, um), (act_in, act), (dm_in, dm), (cot_in, cot)]
        )
    ]
    for load in loads:
        load.start()

    cross = lax.rem(lax.div(x, 2) + here, 2)
    barrier = pltpu.get_barrier_semaphore()

    def greet(k, _):
        x_, zc_ = peer(k)
        pl.semaphore_signal(barrier, inc=1, device_id=(place(x_, yl, zc_), here), device_id_type=MESH)
        return 0

    lax.fori_loop(1, GROUP, greet, 0)
    for to_path, to_dp in (
        (place(x, other_yl, zc), here),
        (path, there),
        (place(3 - x, yl, zc), there),
        (place(3 - x, other_yl, zc), there),
    ):
        pl.semaphore_signal(barrier, inc=1, device_id=(to_path, to_dp), device_id_type=MESH)

    def pick_up_rows(side, source):
        def one(k, _):
            module = table[lax.div(k, 8) * 16 + yl * 8 + lax.rem(k, 8), 0]
            buf_a[side * GROUP + k] = source[module]
            return 0

        lax.fori_loop(0, GROUP, one, 0)

    loads[0].wait()
    upb[...] = um[...].astype(BF16)
    pick_up_rows(yl, upb)
    pl.semaphore_wait(barrier, GROUP + 3)

    up_swap = remote(upb, upf, y_send.at[0], y_recv.at[0], place(x, other_yl, zc), here)
    up_swap.start()

    def send_up_rows(side, half):
        row = place(x, side, zc)
        pltpu.make_async_copy(buf_a.at[side * GROUP + group], wup.at[row], wu_recv).start()

        def one(k, _):
            x_, zc_ = peer(lax.rem(k * 11, GROUP))
            remote(
                buf_a.at[side * GROUP + x_ * 8 + zc_], wup.at[row], wu_send.at[half], wu_recv, place(x_, yl, zc_), here
            ).start()
            return 0

        lax.fori_loop(1, GROUP, one, 0)

    send_up_rows(yl, 0)

    own_rows = pl.ds(pl.multiple_of(here * TOK, TOK), TOK)
    loads[1].wait()
    for part in range(3):
        rows = pl.ds(part * 128, 128)
        wide = act[rows, :].astype(F32)
        mean_square = jnp.mean(wide * wide, axis=-1, keepdims=True)
        to_rows = pl.ds(pl.multiple_of(here * TOK + part * 128, 128), 128)
        nrm[to_rows, :] = (wide * lax.rsqrt(mean_square + 1e-06)).astype(BF16)
    nrm_swap = remote(nrm.at[own_rows], nrm.at[own_rows], y_send.at[1], y_recv.at[1], path, there)
    nrm_swap.start()

    loads[2].wait()
    dnb[...] = dm[...].astype(BF16)
    x_to = x + cross * (3 - 2 * x)
    dp_to = here + cross * (1 - 2 * here)
    dn_far = remote(dnb, blk.at[yl], dn_send.at[0], blk_recv, place(x_to, other_yl, zc), dp_to)
    dn_far.start()
    dn_near = remote(dnb, blk.at[yl], dn_send.at[1], blk_recv, place(3 - x, yl, zc), there)

    @pl.when(cross == 1)
    def _():
        dn_near.start()

    @pl.when(cross == 0)
    def _():
        pltpu.make_async_copy(dnb, blk.at[yl], blk_recv).start()

    loads[3].wait()
    live = jnp.sum((ids[...] != 0).astype(F32))
    for part in range(3):
        rows = pl.ds(part * 128, 128)
        to_rows = pl.ds(pl.multiple_of(here * TOK + part * 128, 128), 128)
        position = (lax.broadcasted_iota(jnp.int32, (128, D), 0) + part * 128).astype(F32)
        og[to_rows, :] = jnp.where(position < live, cot[rows, :].astype(F32), 0.0).astype(BF16)
    count[0] = jnp.broadcast_to(live, (8, 128))
    count_swap = remote(count.at[0], count.at[1], y_send.at[3], y_recv.at[3], path, there)
    count_swap.start()
    og_swap = remote(og.at[own_rows], og.at[own_rows], y_send.at[2], y_recv.at[2], path, there)
    og_swap.start()

    up_swap.wait()
    pick_up_rows(other_yl, upf)
    send_up_rows(other_yl, 1)

    settle(blk, blk_recv)

    def pick_down_rows(k, _):
        module = table[lax.div(k, 8) * 16 + yl * 8 + lax.rem(k, 8), 1]
        buf_b[k] = blk[0, module]
        buf_b[GROUP + k] = blk[1, module]
        return 0

    lax.fori_loop(0, GROUP, pick_down_rows, 0)

    settle(buf_a.at[pl.ds(0, GROUP - 1)], wu_send.at[0])
    from_x = x_to - 2 * here
    for side in range(2):
        row = from_x * 16 + side * 8 + zc
        pltpu.make_async_copy(buf_b.at[side * GROUP + group], wdn.at[dp_to, row], wd_recv).start()

        def one(k, _, side=side, row=row):
            x_, zc_ = peer(lax.rem(k * 11, GROUP))
            remote(
                buf_b.at[side * GROUP + x_ * 8 + zc_], wdn.at[dp_to, row], wd_send, wd_recv,
                place(x_, yl, zc_), here,
            ).start()
            return 0

        lax.fori_loop(1, GROUP, one, 0)

    nrm_swap.wait()

    def turn(i, _):
        cols = pl.ds(pl.multiple_of(i * 256, 256), 256)
        nrm_t[cols, :] = nrm[:, cols].T
        return 0

    lax.fori_loop(0, 4, turn, 0)
    count_swap.wait()
    per_count = 1.0 / (count[0] + count[1])
    per_count = per_count[0:1, 0:1]
    og_swap.wait()

    def scale_rows(i, _):
        rows = pl.ds(pl.multiple_of(i * 64, 64), 64)
        og[rows, :] = (og[rows, :].astype(F32) * per_count).astype(BF16)
        return 0

    lax.fori_loop(0, 12, scale_rows, 0)

    down_x = [here * 2 + lax.rem(x + i, 2) for i in range(2)] + [there * 2 + lax.rem(x + i, 2) for i in range(2)]
    up_x = [lax.rem(x + i, 4) for i in (2, 1, 3, 0)]

    order = (0, 1, 2, 3, 4, 5, 6, 7)

    def fetch(turn_no):
        if turn_no >= 8:
            return
        slot = turn_no % 2
        step = order[turn_no]
        for kind, (down_source, up_source) in enumerate(((down_first, up_first), (down_second, up_second))):
            if step < 4:
                rows = pl.ds(pl.multiple_of(down_x[step] * 1024, 1024), 1024)
                pltpu.make_async_copy(
                    down_source.at[rows], mom.at[slot, kind], mom_sem.at[slot, kind]
                ).start()
            else:
                rows = pl.ds(pl.multiple_of(up_x[step - 4] * 256, 256), 256)
                for b in range(4):
                    pltpu.make_async_copy(
                        up_source.at[rows, pl.ds(b * 512, 512)],
                        mom.at[slot, kind, pl.ds(b * 256, 256)],
                        mom_sem.at[slot, kind],
                    ).start()

    def await_moments(turn_no):
        slot = turn_no % 2
        for kind in range(2):
            settle(mom.at[slot, kind], mom_sem.at[slot, kind])

    fetch(0)
    fetch(1)

    settle(wup, wu_recv)
    mine_cols = pl.ds(pl.multiple_of(here * HALF_D, HALF_D), HALF_D)
    their_cols = pl.ds(pl.multiple_of(there * HALF_D, HALF_D), HALF_D)

    def g_copy(chunk):
        rows = pl.ds(pl.multiple_of(chunk * 512, 512), 512)
        return remote(gsend.at[rows], grecv.at[rows], g_send.at[chunk], g_recv.at[chunk], path, there)

    def pre_act(i, half):
        cols = pl.ds(pl.multiple_of(i * 256, 256), 256)
        weights = wup[:, :, cols].reshape(D, 256)
        wide_a[half] = jnp.dot(nrm[...], weights, preferred_element_type=F32)

    first_tile = 4 * lax.rem(x, 2)
    pre_act(first_tile, 0)

    def hidden(pair, _):
        for half in range(2):
            i = lax.rem(first_tile + pair * 2 + half, 8)
            pre_act(lax.rem(i + 1, 8), 1 - half)
            cols = pl.ds(pl.multiple_of(i * 256, 256), 256)
            for strip in range(24):
                rows = pl.ds(strip * 32, 32)
                pre = wide_a[half, rows, :] * UP_SCALE
                sig = 0.5 * jnp.tanh(0.5 * pre) + 0.5
                out = pre * sig
                act_a[half, rows, :] = out.astype(BF16)
                gp[rows, cols] = (sig + out * (1.0 - sig)).astype(BF16)
            out_t = act_a[half].T
            theirs = jnp.dot(out_t, og[:, their_cols], preferred_element_type=F32)
            gsend[cols, :] = (theirs * DOWN_SCALE).astype(BF16)
            if half == 1:
                g_copy(lax.div(i, 2)).start()
            mine = jnp.dot(out_t, og[:, mine_cols], preferred_element_type=F32)
            gmine[cols, :] = (mine * DOWN_SCALE).astype(BF16)
        return 0

    lax.fori_loop(0, 4, hidden, 0)

    def down_delta(turn_no):
        step = order[turn_no]
        x_ = down_x[step]
        source = gmine if step < 2 else grecv
        first_row = lax.rem(x_, 2) * 1024
        if step >= 2:
            for half in range(2):
                g_copy(lax.rem(x_, 2) * 2 + half).wait_recv()
        await_moments(turn_no)
        slot = turn_no % 2

        def one(q, _):
            for b in range(4):
                rows = pl.ds(pl.multiple_of(q * 64 + b * 16, 16), 16)
                grad = source[pl.ds(pl.multiple_of(first_row + q * 64 + b * 16, 16), 16), :].astype(F32)
                delta = step_direction(grad, mom[slot, 0, rows, :], mom[slot, 1, rows, :])
                buf_a[x_ * 16 + q, :, pl.ds(b * 512, 512)] = delta
            return 0

        lax.fori_loop(0, 16, one, 0)
        fetch(turn_no + 2)

    def send_down_delta(step, side):
        x_ = down_x[step]

        def send(k, _):
            zc_ = zc_at(k)
            row = x_ * 16 + side * 8 + zc_
            away = (x_ * 8 + zc_) != group

            @pl.when(away)
            def _():
                remote(
                    buf_a.at[row], rdn.at[side, group], dd_send, dd_recv.at[side], place(x_, yl, zc_), here
                ).start()

            @pl.when(jnp.logical_not(away))
            def _():
                pltpu.make_async_copy(buf_a.at[row], rdn.at[side, group], dd_recv.at[side]).start()

            return 0

        lax.fori_loop(0, 8, send, 0)

    settle(buf_a.at[pl.ds(0, GROUP - 1)], wu_send.at[1])
    for turn_no in range(2):
        down_delta(turn_no)
        send_down_delta(turn_no, other_yl)
        send_down_delta(turn_no, yl)

    settle(wdn, wd_recv)

    def hidden_grad(i, _):
        cols = pl.ds(pl.multiple_of(i * 256, 256), 256)
        low = wdn[0, pl.ds(i * 4, 4)].reshape(256, HALF_D)
        high = wdn[1, pl.ds(i * 4, 4)].reshape(256, HALF_D)
        grad = lax.dot_general(og[:, pl.ds(0, HALF_D)], low, NT, preferred_element_type=F32)
        grad += lax.dot_general(og[:, pl.ds(HALF_D, HALF_D)], high, NT, preferred_element_type=F32)
        gp[:, cols] = (grad * DOWN_SCALE * gp[:, cols].astype(F32)).astype(BF16)
        return 0

    lax.fori_loop(0, 8, hidden_grad, 0)
    settle(buf_b.at[pl.ds(0, 2 * GROUP - 2)], wd_send)
    for turn_no in range(2, 4):
        down_delta(turn_no)
        send_down_delta(turn_no, other_yl)
        send_down_delta(turn_no, yl)

    def send_up_delta(x_, zc_, side):
        row = x_ * 16 + side * 8 + zc_
        away = (x_ * 8 + zc_) != group

        @pl.when(away)
        def _():
            remote(
                buf_b.at[row], rup.at[side, group], du_send, du_recv.at[side], place(x_, yl, zc_), here
            ).start()

        @pl.when(jnp.logical_not(away))
        def _():
            pltpu.make_async_copy(buf_b.at[row], rup.at[side, group], du_recv.at[side]).start()

    def up_step(turn_no):
        x_ = up_x[order[turn_no] - 4]
        slot = turn_no % 2
        lhs = nrm_t[pl.ds(pl.multiple_of(x_ * 256, 256), 256), :]

        def up_grad(b):
            wide_b[b % 2] = jnp.dot(lhs, gp[:, pl.ds(b * 512, 512)], preferred_element_type=F32)

        up_grad(0)
        await_moments(turn_no)
        for b in range(4):
            if b < 3:
                up_grad(b + 1)
            for i in range(16):
                rows = pl.ds(b * 256 + i * 16, 16)
                grad = wide_b[b % 2, pl.ds(i * 16, 16), :] * UP_SCALE
                delta = step_direction(grad, mom[slot, 0, rows, :], mom[slot, 1, rows, :])
                buf_b[x_ * 16 + i, pl.ds(b * 16, 16), :] = delta
        fetch(turn_no + 2)

        def send(k, _):
            send_up_delta(x_, zc_at(k), other_yl)
            return 0

        lax.fori_loop(0, 8, send, 0)

    for turn_no in range(4, 8):
        up_step(turn_no)

    def send_rest(k, _):
        x_, zc_ = peer(lax.rem(k * 11, GROUP))
        send_up_delta(x_, zc_, yl)
        return 0

    lax.fori_loop(0, GROUP, send_rest, 0)

    lane = lax.broadcasted_iota(jnp.int32, (16, C * 16), 1)
    same_row = (lane & 15) == lax.broadcasted_iota(jnp.int32, (16, C * 16), 0)
    for level, pick in enumerate((pick_up, pick_dn)):

        def fill(k, _, level=level):
            module = table[lax.div(k, 8) * 16 + yl * 8 + lax.rem(k, 8), level]
            rows = pl.ds(pl.multiple_of(k * 16, 16), 16)
            pick_t[rows, :] = jnp.where(same_row & ((lane >> 4) == module), 1.0, 0.0)
            return 0

        lax.fori_loop(0, GROUP, fill, 0)
        pick[...] = pick_t[...].T.astype(BF16)

        def tally(k, counts, level=level):
            module = table[k, level]
            return tuple(n + jnp.where(module == m, 1, 0) for m, n in enumerate(counts))

        counts = lax.fori_loop(0, 64, tally, (jnp.int32(0),) * C)
        for m in range(C):
            used[level * C + m] = counts[m]

    def down_sum(side, b):
        block = rdn[side, :, :, pl.ds(b * 512, 512)].reshape(GROUP * 16, 512)
        return jnp.dot(pick_dn[...], block, preferred_element_type=F32).reshape(C, 16, 512)

    def up_sum(side, b):
        block = rup[side, :, pl.ds(b * 16, 16), :].reshape(GROUP * 16, 512)
        return jnp.dot(pick_up[...], block, preferred_element_type=F32).reshape(C, 16, 512)

    def finish(total, master, level, rows, cols):
        for m in range(C):
            number = jnp.broadcast_to(used[level * C + m].astype(F32), (8, 128))
            per_used = (1.0 / jnp.maximum(number, 1.0))[0:1, 0:1]
            decay = (0.01 * jnp.minimum(number, 1.0))[0:1, 0:1]
            weights = master[m, rows, cols].astype(BF16).astype(F32)
            master[m, rows, cols] = total[m] * per_used + decay * weights

    mate = place(x, other_yl, zc)
    stores = [
        pltpu.make_async_copy(src, dst, out_sem.at[i]) for i, (src, dst) in enumerate([(dm, dm_out), (um, um_out)])
    ]
    settle(rdn.at[other_yl], dd_recv.at[other_yl])
    for b in range(4):
        pdn_send[:, :, pl.ds(b * 512, 512)] = down_sum(other_yl, b).astype(BF16)
    dn_part = remote(pdn_send, pdn_recv, y_send.at[4], y_recv.at[4], mate, here)
    dn_part.start()
    settle(rdn.at[yl], dd_recv.at[yl])
    dn_part.wait()
    for b in range(4):
        cols = pl.ds(b * 512, 512)
        total = down_sum(yl, b) + pdn_recv[:, :, cols].astype(F32)
        finish(total, dm, 1, pl.ds(b * 16, 16), pl.ds(0, 512))
    stores[0].start()

    settle(rup.at[other_yl], du_recv.at[other_yl])
    for b in range(4):
        pup_send[:, pl.ds(b * 16, 16), :] = up_sum(other_yl, b).astype(BF16)
    up_part = remote(pup_send, pup_recv, y_send.at[5], y_recv.at[5], mate, here)
    up_part.start()
    settle(rup.at[yl], du_recv.at[yl])
    up_part.wait()
    for b in range(4):
        rows = pl.ds(b * 16, 16)
        total = up_sum(yl, b) + pup_recv[:, rows, :].astype(F32)
        finish(total, um, 0, pl.ds(0, 16), pl.ds(b * 512, 512))
    stores[1].start()

    dn_far.wait_send()

    @pl.when(cross == 1)
    def _():
        dn_near.wait_send()

    for chunk in range(4):
        g_copy(chunk).wait_send()
    settle(buf_a.at[pl.ds(0, 2 * GROUP - 2)], dd_send)
    settle(buf_b.at[pl.ds(0, 2 * GROUP - 2)], du_send)
    for store in stores:
        store.wait()


def shards(
    activations,
    cotangent,
    token_ids,
    path_table,
    up_master,
    down_master,
    up_momentum,
    down_momentum,
    up_first,
    up_second,
    down_first,
    down_second,
):
    anywhere = pl.BlockSpec(memory_space=pl.ANY)
    smem = pl.BlockSpec(memory_space=pltpu.SMEM)
    vmem = pl.BlockSpec(memory_space=pltpu.VMEM)
    dma = pltpu.SemaphoreType.DMA
    up_mean, down_mean = pl.pallas_call(
        kernel,
        out_shape=[jax.ShapeDtypeStruct(array.shape, F32) for array in (up_master, down_master)],
        in_specs=[smem, vmem] + [anywhere] * 8,
        out_specs=[anywhere] * 2,
        scratch_shapes=[
            pltpu.VMEM((C, 16, HALF_F), F32),
            pltpu.VMEM((C, 64, HALF_D), F32),
            pltpu.VMEM((TOK, D), BF16),
            pltpu.VMEM((TOK, D), BF16),
            pltpu.VMEM((C, 16, HALF_F), BF16),
            pltpu.VMEM((C, 16, HALF_F), BF16),
            pltpu.VMEM((C, 64, HALF_D), BF16),
            pltpu.VMEM((2, C, 64, HALF_D), BF16),
            pltpu.VMEM((2 * GROUP, 16, HALF_F), BF16),
            pltpu.VMEM((2 * GROUP, 64, HALF_D), BF16),
            pltpu.VMEM((2 * GROUP, 16, HALF_F), BF16),
            pltpu.VMEM((2, GROUP, 64, HALF_D), BF16),
            pltpu.VMEM((2, GROUP, 16, HALF_F), BF16),
            pltpu.VMEM((2, GROUP, 64, HALF_D), BF16),
            pltpu.VMEM((HALF_F, HALF_D), BF16),
            pltpu.VMEM((HALF_F, HALF_D), BF16),
            pltpu.VMEM((HALF_F, HALF_D), BF16),
            pltpu.VMEM((2 * TOK, D), BF16),
            pltpu.VMEM((D, 2 * TOK), BF16),
            pltpu.VMEM((2 * TOK, D), BF16),
            pltpu.VMEM((2, 8, 128), F32),
            pltpu.SMEM((2 * C,), jnp.int32),
            pltpu.VMEM((2 * TOK, HALF_F), BF16),
            pltpu.VMEM((2, 2 * TOK, 256), F32),
            pltpu.VMEM((2, 2 * TOK, 256), BF16),
            pltpu.VMEM((2, 256, 512), F32),
            pltpu.VMEM((2, 2, 1024, 512), BF16),
            pltpu.VMEM((C, 16, HALF_F), BF16),
            pltpu.VMEM((C, 16, HALF_F), BF16),
            pltpu.VMEM((C, 64, HALF_D), BF16),
            pltpu.VMEM((C, 64, HALF_D), BF16),
            pltpu.VMEM((GROUP * 16, C * 16), F32),
            pltpu.VMEM((C * 16, GROUP * 16), BF16),
            pltpu.VMEM((C * 16, GROUP * 16), BF16),
            dma((4,)),
            dma((2, 2)),
            dma((2,)),
            dma((6,)),
            dma((6,)),
            dma((2,)),
            dma,
            dma((2,)),
            dma,
            dma,
            dma,
            dma((4,)),
            dma((4,)),
            dma,
            dma((2,)),
            dma,
            dma((2,)),
        ],
        compiler_params=pltpu.CompilerParams(
            collective_id=0, has_side_effects=True, vmem_limit_bytes=62 * 1024 * 1024
        ),
        cost_estimate=pl.CostEstimate(flops=12_884_901_888, bytes_accessed=30_000_000, transcendentals=1_572_864),
    )(
        path_table,
        token_ids,
        activations[0],
        cotangent[0],
        up_master,
        down_master,
        up_first[0],
        up_second[0],
        down_first[0],
        down_second[0],
    )
    flat = (C * 16, HALF_F)
    up_mean = up_mean.reshape(flat)
    new_up_momentum = 0.9 * up_momentum.reshape(flat) + up_mean
    new_up_master = up_master.reshape(flat) - 0.7 * (up_mean + 0.9 * new_up_momentum)
    new_up_momentum = new_up_momentum.reshape(up_momentum.shape)
    new_up_master = new_up_master.reshape(up_master.shape)
    new_down_momentum = 0.9 * down_momentum + down_mean
    new_down_master = down_master - 0.7 * (down_mean + 0.9 * new_down_momentum)
    return (new_up_master, new_down_master, new_up_momentum, new_down_momentum)


def solution(mesh):
    placed = (
        P("path", "dp", None),
        P("path", "dp", None),
        P("path", "dp"),
        P(),
        P(None, "path", "dp"),
        P(None, "path", "dp"),
        P(None, "path", "dp"),
        P(None, "path", "dp"),
        P("path", None, "dp"),
        P("path", None, "dp"),
        P("path", None, "dp"),
        P("path", None, "dp"),
    )
    return jax.shard_map(
        shards,
        mesh=mesh,
        in_specs=placed,
        out_specs=(
            P(None, "path", "dp"),
            P(None, "path", "dp"),
            P(None, "path", "dp"),
            P(None, "path", "dp"),
        ),
        check_vma=False,
    )
```
